32 devices in a mesh: dp: 4 (over z), tensor: 8 (over y, x, core).
Axes of the slice: x: 2, y: 2, z: 4, core: 2. Of those that a mesh axis runs over, the one named last changes fastest.
Arguments:
- activations: bfloat16 [4096, 13312], P('dp', 'tensor'), may hold values from -6 to 6
- plan: int32 [2], replicated, may hold values from 1 to 7, as said below
Outputs:
- covariance_tiles: float32 [2, 1664, 13312], P(None, 'dp', 'tensor')
The draws below stay inside these ranges and needn't reach their ends.
Inputs may be any that keep to these rules, and one draw needn't show every extreme that they name: `plan`: the masks differ from each other and one of them has every bit of the panel index set.
All inputs are finite; a program needn't handle non-finite values.
Results may differ from the reference program's by a relative error of at most 0.0003.
Values may be sent and summed in bfloat16 or wider, within the bound.
No kernel may reach another device: no remote copies, remote signals or barrier semaphores. Data moves between devices by JAX's collectives and lax.ppermute only.
A program may use at most 128 MiB of HBM per device.

```python
import math
import jax
import jax.numpy as jnp
from jax import lax

PANEL = 1664
ROUNDS = 2
FFW = 13312
TOKENS = 4096
N_TENSOR = 8


def draw_plan(key, part):
    key = jax.random.fold_in(key, 7)
    first_key, second_key = jax.random.split(key)
    other = jax.random.randint(first_key, (), 1, N_TENSOR - 1)
    flip = jax.random.randint(second_key, (), 0, 2)
    top = jnp.int32(N_TENSOR - 1)
    masks = jnp.where(flip == 0, jnp.stack([top, other]), jnp.stack([other, top]))
    return masks.astype(jnp.int32)


def block_scale(own_key, shape, cuts, low, high):
    def one(dim, blocks):
        heights = jax.random.uniform(jax.random.fold_in(jax.random.fold_in(own_key, 6), dim), (blocks,), jnp.float32, low / len(cuts), high / len(cuts))
        return jnp.repeat(jnp.exp(heights), shape[dim] // blocks).reshape((-1,) + (1,) * (len(shape) - dim - 1))

    factor_of = one(*cuts[0])
    for cut in cuts[1:]:
        factor_of = factor_of * one(*cut)
    return factor_of


def scatter_about(own_key, shape, deviation, bound, pieces=(), kind=jnp.bfloat16):
    drawn = jax.random.normal(own_key, shape, jnp.float32) * deviation
    if len(pieces) > 0:
        drawn = block_scale(own_key, shape, pieces, -0.22, 0.18) * drawn
    return jnp.clip(drawn, min=-bound, max=bound).astype(kind)


def setup_inputs(seed: int = 0) -> dict:
    seeds = jax.random.split(jax.random.key(seed), 3)
    return {
        "activations": scatter_about(seeds[0], (TOKENS, FFW), 1.0, 6.0, ((0, 4), (1, 8))),
        "plan": draw_plan(jax.random.fold_in(seeds[2], 71), 0),
    }


def reference(activations, plan):
    scale = jnp.float32(1.0 / math.sqrt(TOKENS))
    panels = activations.reshape(TOKENS, N_TENSOR, PANEL).transpose(1, 0, 2)

    def one_panel(index):
        own = panels[index]
        tiles = []
        for r in range(ROUNDS):
            partner = jnp.bitwise_xor(index, plan[r]).astype(jnp.int32)
            other = lax.dynamic_index_in_dim(panels, partner, 0, keepdims=False)
            tile = lax.dot_general(other, own, (((0,), (0,)), ((), ())), preferred_element_type=jnp.float32)
            tiles.append(tile * scale)
        return jnp.stack(tiles)
    result = lax.map(one_panel, jnp.arange(N_TENSOR, dtype=jnp.int32))
    return result.transpose(1, 2, 0, 3).reshape(ROUNDS, PANEL, FFW)
```

```python
import math

import jax
import jax.numpy as jnp
from jax import lax
from jax.sharding import PartitionSpec as P

ROUNDS = 2
LINE = 4


def swapped(x, axis, apart):
    return lax.ppermute(x, axis, [(i, i ^ 1 << apart) for i in range(lax.axis_size(axis))])


def partner_panel(own, mask, width):
    current = own
    for bit in range(width):
        taken = jnp.bitwise_and(jnp.right_shift(mask, bit), 1) == 1
        current = jnp.where(taken, swapped(current, "tensor", bit), current)
    return current


def shards_any(activations, plan):
    width = lax.axis_size("tensor").bit_length() - 1
    scale = jnp.float32(1.0 / math.sqrt(activations.shape[0] * lax.axis_size("dp")))
    tiles = []
    for r in range(ROUNDS):
        other = partner_panel(activations, plan[r], width)
        tiles.append(
            lax.dot_general(other, activations, (((0,), (0,)), ((), ())), preferred_element_type=jnp.float32)
        )
    return lax.psum_scatter(jnp.stack(tiles), "dp", scatter_dimension=1, tiled=True) * scale


def inward(x):
    return lax.ppermute(x, "dp", [(0, 1), (3, 2)])


def across(x):
    return lax.ppermute(x, "dp", [(1, 2), (2, 1)])


def outward(x):
    return lax.ppermute(x, "dp", [(1, 0), (2, 3)])


def partner(x, mask):
    return lax.ppermute(x, "tensor", [(i, i ^ mask) for i in range(lax.axis_size("tensor"))])


def product(rows, columns):
    return lax.dot_general(rows, columns, (((1,), (1,)), ((), ())), preferred_element_type=jnp.float32)


def packed(tile):
    biggest = jnp.max(jnp.abs(tile))
    power = jnp.ceil(jnp.log2(jnp.maximum(biggest, 1e-30)))
    flat = (tile * jnp.exp2(14.0 - power)).reshape(-1, tile.shape[-1])
    return jnp.concatenate([flat, jnp.full((16, flat.shape[1]), power)]).astype(jnp.float16)


def unpacked(flat, shape):
    power = flat[-1, 0].astype(jnp.float32)
    return flat[:-16].reshape(shape).astype(jnp.float32) * jnp.exp2(power - 14.0)


def line_branch(mask, top):
    rest = top ^ mask

    def run(w0, w1, w2, w3, scale):
        w = [w0, w1, w2, w3]
        e, f, g = [None] * 4, [None] * 4, [None] * 4
        e[3] = inward(w[3])
        f[0] = across(w[3])
        wm = [partner(w[0], mask), None]
        e[2] = inward(w[2])
        g[0] = across(e[3])
        w7 = [partner(wm[0], rest), None]
        em = [inward(wm[0]), None]
        f[1] = across(w[2])
        fm = [partner(f[0], mask), None]
        e7 = [inward(w7[0]), None]
        g[1] = across(e[2])
        gm = [partner(g[0], mask), None]
        f7 = [partner(fm[0], rest), None]
        e[1] = inward(w[1])
        f[2] = across(w[1])
        wm[1] = partner(w[1], mask)
        g7 = [partner(gm[0], rest), None]
        e[0] = inward(w[0])
        g[2] = across(e[1])
        w7[1] = partner(wm[1], rest)
        em[1] = inward(wm[1])
        f[3] = across(w[0])
        fm[1] = partner(f[1], mask)
        e7[1] = inward(w7[1])
        g[3] = across(e[0])
        gm[1] = partner(g[1], mask)
        f7[1] = partner(fm[1], rest)
        g7[1] = partner(gm[1], rest)

        rows_m = [jnp.concatenate([wm[q], em[q], fm[q], gm[q]], 1) for q in range(2)]
        rows_7 = [jnp.concatenate([w7[q], e7[q], f7[q], g7[q]], 1) for q in range(2)]
        columns = [jnp.concatenate([w[j], e[j], f[j], g[j]], 1) for j in range(4)]

        pieces = []
        for j in range(4):
            sent = jnp.stack([product(rows_m[0], columns[j]), product(rows_7[0], columns[j])]) * scale
            pieces.append((sent.shape, outward(packed(sent))))
        middle = (lax.axis_index("dp") == 1) | (lax.axis_index("dp") == 2)
        done = []
        for j in range(4):
            own = jnp.stack([product(rows_m[1], columns[j]), product(rows_7[1], columns[j])]) * scale
            shape, flat = pieces[j]
            done.append(jnp.where(middle, own, unpacked(flat, shape)))
        low = lax.axis_index("dp") < 2
        return [jnp.where(low, done[j], done[3 - j]) for j in range(4)]

    return run


def shards_line(activations, plan):
    tokens, units = activations.shape
    top = lax.axis_size("tensor") - 1
    scale = jnp.float32(1.0 / math.sqrt(tokens * LINE))
    blocks = activations.T.reshape(LINE, units // LINE, tokens)
    low = lax.axis_index("dp") < 2
    w = [jnp.where(low, blocks[j], blocks[3 - j]) for j in range(4)]
    first_is_top = plan[0] == top
    other = plan[0] + plan[1] - top
    pieces = lax.switch(other - 1, [line_branch(m, top) for m in range(1, top)], *w, scale)
    out = jnp.concatenate(pieces, 2)
    return jnp.where(first_is_top, out[::-1], out)


def solution(mesh):
    fast = mesh.shape["dp"] == LINE
    return jax.shard_map(
        shards_line if fast else shards_any,
        mesh=mesh,
        in_specs=(P("dp", "tensor"), P()),
        out_specs=P(None, "dp", "tensor"),
        check_vma=False,
    )
```

```python
import functools
import math

import jax
import jax.numpy as jnp
from jax import lax
from jax.experimental import pallas as pl
from jax.experimental.pallas import tpu as pltpu
from jax.sharding import PartitionSpec as P

ROUNDS = 2
LINE = 4
LANES = 128
VMEM_LIMIT = 40 * 2**20


def swapped(x, axis, apart):
    return lax.ppermute(x, axis, [(i, i ^ 1 << apart) for i in range(lax.axis_size(axis))])


def partner_panel(own, mask, width):
    current = own
    for bit in range(width):
        taken = jnp.bitwise_and(jnp.right_shift(mask, bit), 1) == 1
        current = jnp.where(taken, swapped(current, "tensor", bit), current)
    return current


def shards_any(activations, plan):
    width = lax.axis_size("tensor").bit_length() - 1
    scale = jnp.float32(1.0 / math.sqrt(activations.shape[0] * lax.axis_size("dp")))
    tiles = []
    for r in range(ROUNDS):
        other = partner_panel(activations, plan[r], width)
        tiles.append(
            lax.dot_general(other, activations, (((0,), (0,)), ((), ())), preferred_element_type=jnp.float32)
        )
    return lax.psum_scatter(jnp.stack(tiles), "dp", scatter_dimension=1, tiled=True) * scale


def inward(x):
    return lax.ppermute(x, "dp", [(0, 1), (3, 2)])


def across(x):
    return lax.ppermute(x, "dp", [(1, 2), (2, 1)])


def skipping(x):
    return lax.ppermute(x, "dp", [(0, 2), (3, 1)])


def outward(x):
    return lax.ppermute(x, "dp", [(1, 0), (2, 3)])


def partner(x, mask):
    return lax.ppermute(x, "tensor", [(i, i ^ mask) for i in range(lax.axis_size("tensor"))])


def after(x, *others):
    return lax.optimization_barrier((x, *others))[0]


def times(rows, columns):
    return lax.dot_general(rows, columns, (((1,), (1,)), ((), ())), preferred_element_type=jnp.float32)


def pieces_of(units):
    block = units // LINE
    widths = [block // LANES * LANES] * (LINE - 1)
    widths.append(units - sum(widths))
    return [(w, (block - widths[0]) * p) for p, w in enumerate(widths)]


def edge_kernel(width, before, scale, low_ref, *refs):
    rows, news, olds = refs[:8], refs[8:12], refs[12:16] if before else ()
    out_ref, row_buf, col_buf, acc, row_sems, col_sems = refs[-6:]
    block = rows[0].shape[0]
    low = low_ref[0] == 1
    new = width - before
    copies = []
    for v in range(4):
        source = pl.multiple_of(jnp.where(low, 0, block - new), 16)
        target = pl.multiple_of(jnp.where(low, before, 0), 16)
        copies.append(
            pltpu.make_async_copy(
                news[v].at[pl.ds(source, new)], col_buf.at[v, pl.ds(target, new)], col_sems.at[v]
            )
        )
        if before:
            source = pl.multiple_of(jnp.where(low, block - before, 0), 16)
            target = pl.multiple_of(jnp.where(low, 0, new), 16)
            copies.append(
                pltpu.make_async_copy(
                    olds[v].at[pl.ds(source, before)], col_buf.at[v, pl.ds(target, before)], col_sems.at[4 + v]
                )
            )
    row_copies = [pltpu.make_async_copy(rows[i], row_buf.at[i], row_sems.at[i]) for i in range(8)]
    for v in range(4):
        row_copies[v].start()
        for copy in copies[v * len(copies) // 4 : (v + 1) * len(copies) // 4]:
            copy.start()
    for v in range(4, 8):
        row_copies[v].start()
    for copy in copies:
        copy.wait()

    acc[...] = jnp.zeros_like(acc)

    def step(i, _):
        pltpu.make_async_copy(row_buf.at[i], row_buf.at[i], row_sems.at[i]).wait()
        acc[i // 4] += times(row_buf[i], col_buf[i % 4])
        return 0

    lax.fori_loop(0, 8, step, 0)
    biggest = jnp.max(jnp.abs(acc[...]), axis=(0, 1, 2), keepdims=True)
    power = jnp.ceil(jnp.log2(jnp.maximum(biggest * scale, 1e-30)))
    factor = scale * jnp.exp2(14.0 - power)
    for k in range(2):
        value = acc[k] * factor[0]
        spread = value * 8193.0
        out_ref[k * block : (k + 1) * block] = spread - (spread - value)
    out_ref[2 * block :] = jnp.broadcast_to(power[0], (16, width))


def edge_tiles(low, rows, news, olds, width, before, scale):
    block, tokens = rows[0].shape
    operands = [*rows, *news, *(olds if before else ())]
    return pl.pallas_call(
        functools.partial(edge_kernel, width, before, scale),
        out_shape=jax.ShapeDtypeStruct((2 * block + 16, width), jnp.float32),
        in_specs=[pl.BlockSpec(memory_space=pltpu.SMEM)] + [pl.BlockSpec(memory_space=pl.ANY)] * len(operands),
        out_specs=pl.BlockSpec(memory_space=pltpu.VMEM),
        scratch_shapes=[
            pltpu.VMEM((8, block, tokens), jnp.bfloat16),
            pltpu.VMEM((4, width, tokens), jnp.bfloat16),
            pltpu.VMEM((2, block, width), jnp.float32),
            pltpu.SemaphoreType.DMA((8,)),
            pltpu.SemaphoreType.DMA((8,)),
        ],
        compiler_params=pltpu.CompilerParams(vmem_limit_bytes=VMEM_LIMIT),
        cost_estimate=pl.CostEstimate(
            flops=2 * 8 * block * tokens * width, bytes_accessed=2 * (8 * block + 4 * width) * tokens, transcendentals=0
        ),
        name="edge_tiles",
    )(low, *operands)


def unpack(flat, row, scale_row, block):
    return flat[row : row + block] * jnp.exp2(flat[scale_row : scale_row + 1, :1] - 14.0)


def middle_kernel(pieces, scale, flags_ref, *refs):
    rows, columns, packed = refs[:8], refs[8:24], refs[24:27]
    out_ref, row_buf, col_buf, row_sems, col_sems = refs[-5:]
    block = rows[0].shape[0]
    units = 4 * block
    low = flags_ref[0] == 1
    middle = flags_ref[1] == 1
    first = flags_ref[2]

    @pl.when(middle)
    def _():
        copies = []
        for v in range(4):
            for j in range(4):
                target = pl.multiple_of(jnp.where(low, j * block, (3 - j) * block), 16)
                copies.append(
                    pltpu.make_async_copy(columns[4 * v + j], col_buf.at[v, pl.ds(target, block)], col_sems.at[4 * v + j])
                )
        row_copies = [pltpu.make_async_copy(rows[i], row_buf.at[i], row_sems.at[i]) for i in range(8)]
        for copy in row_copies + copies:
            copy.start()
        for copy in row_copies + copies:
            copy.wait()

        def tile(k, start, width):
            total = times(row_buf[4 * k], col_buf[0, pl.ds(start, width)])
            for v in range(1, 4):
                total += times(row_buf[4 * k + v], col_buf[v, pl.ds(start, width)])
            out_ref[lax.bitwise_xor(first, k), :, pl.ds(start, width)] = total * scale

        wide = 2 * LANES
        full = units // wide

        def step(i, _):
            tile(i // full, pl.multiple_of(i % full * wide, wide), wide)
            return 0

        lax.fori_loop(0, 2 * full, step, 0)
        if units % wide:

            def last(k, _):
                tile(k, full * wide, units % wide)
                return 0

            lax.fori_loop(0, 2, last, 0)

    @pl.when(jnp.logical_not(middle))
    def _():
        done = 0
        for p, (width, _) in enumerate(pieces[:3]):
            start = pl.multiple_of(jnp.where(low, done, units - done - width), LANES)
            for k in range(2):
                out_ref[lax.bitwise_xor(first, k), :, pl.ds(start, width)] = unpack(packed[p], k * block, 2 * block, block)
            done += width


def middle_tiles(flags, rows, columns, packed, scale):
    block, tokens = rows[0].shape
    units = 4 * block
    operands = [*rows, *columns]
    return pl.pallas_call(
        functools.partial(middle_kernel, pieces_of(units), scale),
        out_shape=jax.ShapeDtypeStruct((2, block, units), jnp.float32),
        in_specs=[pl.BlockSpec(memory_space=pltpu.SMEM)]
        + [pl.BlockSpec(memory_space=pl.ANY)] * len(operands)
        + [pl.BlockSpec(memory_space=pltpu.VMEM)] * len(packed),
        out_specs=pl.BlockSpec(memory_space=pltpu.VMEM),
        scratch_shapes=[
            pltpu.VMEM((8, block, tokens), jnp.bfloat16),
            pltpu.VMEM((4, units, tokens), jnp.bfloat16),
            pltpu.SemaphoreType.DMA((8,)),
            pltpu.SemaphoreType.DMA((16,)),
        ],
        compiler_params=pltpu.CompilerParams(vmem_limit_bytes=VMEM_LIMIT),
        cost_estimate=pl.CostEstimate(
            flops=2 * 8 * block * tokens * units, bytes_accessed=2 * (8 * block + 4 * units) * tokens, transcendentals=0
        ),
        name="middle_tiles",
    )(flags, *operands, *packed)


def last_kernel(width, flags_ref, out_in, flat_ref, out_ref, buf, sem):
    block, units = out_in.shape[1:]
    low = flags_ref[0] == 1
    first = flags_ref[2]

    @pl.when(flags_ref[1] == 0)
    def _():
        start = pl.multiple_of(jnp.where(low, units - width, 0), LANES)
        for k in range(2):
            buf[lax.bitwise_xor(first, k)] = unpack(flat_ref, k * block, 2 * block, block)
        copy = pltpu.make_async_copy(buf, out_ref.at[:, :, pl.ds(start, width)], sem)
        copy.start()
        copy.wait()


def last_tiles(flags, out, flat):
    width = flat.shape[1]
    return pl.pallas_call(
        functools.partial(last_kernel, width),
        out_shape=jax.ShapeDtypeStruct(out.shape, out.dtype),
        in_specs=[
            pl.BlockSpec(memory_space=pltpu.SMEM),
            pl.BlockSpec(memory_space=pl.ANY),
            pl.BlockSpec(memory_space=pltpu.VMEM),
        ],
        out_specs=pl.BlockSpec(memory_space=pl.ANY),
        scratch_shapes=[pltpu.VMEM((2, out.shape[1], width), jnp.float32), pltpu.SemaphoreType.DMA],
        input_output_aliases={1: 0},
        compiler_params=pltpu.CompilerParams(vmem_limit_bytes=VMEM_LIMIT),
        cost_estimate=pl.CostEstimate(flops=0, bytes_accessed=6 * flat.size, transcendentals=0),
        name="last_tiles",
    )(flags, out, flat)


def line_branch(mask, top, scale):
    rest = top ^ mask

    def run(flags, *w):
        low = flags[:1]
        e, f, g = [None] * 4, [None] * 4, [None] * 4
        g[0] = skipping(w[3])
        f[0] = across(w[3])
        wm = [partner(w[0], mask), None]
        e[0] = inward(w[0])
        w7 = [partner(wm[0], rest), None]
        g[1] = skipping(w[2])
        f[1] = across(w[2])
        em = [partner(e[0], mask), None]
        fm = [partner(f[0], mask), None]
        e[1] = inward(w[1])
        e7 = [partner(em[0], rest), None]
        gm = [partner(g[0], mask), None]
        f7 = [partner(fm[0], rest), None]
        f[2] = across(w[1])
        wm[1] = partner(w[1], mask)
        g7 = [partner(gm[0], rest), None]
        w7[1] = partner(wm[1], rest)
        g[2] = across(e[1])
        fm[1] = partner(f[1], mask)
        em[1] = inward(wm[1])
        e7[1] = inward(w7[1])
        f7[1] = partner(fm[1], rest)
        f[3] = across(w[0])
        gm[1] = partner(g[1], mask)
        e[2] = inward(w[2])
        g[3] = across(e[0])
        g7[1] = partner(gm[1], rest)
        e[3] = inward(w[3])

        pieces = pieces_of(4 * w[0].shape[0])
        columns = [[w[j], e[j], f[j], g[j]] for j in range(4)]
        near, own = [[wm[q], em[q], fm[q], gm[q], w7[q], e7[q], f7[q], g7[q]] for q in range(2)]
        sent = []
        for p, (width, before) in enumerate(pieces):
            flat = edge_tiles(low, near, columns[p], columns[max(p - 1, 0)], width, before, scale)
            sent.append(outward(flat.astype(jnp.float16)).astype(jnp.float32))
        out = middle_tiles(flags, own, [columns[j][v] for v in range(4) for j in range(4)], sent[:3], scale)
        return last_tiles(flags, out, sent[3])

    return run


def shards_line(activations, plan):
    tokens, units = activations.shape
    top = lax.axis_size("tensor") - 1
    scale = 1.0 / math.sqrt(tokens * LINE)
    place = lax.axis_index("dp")
    low = place < 2
    first = plan[0] == top
    flags = jnp.stack([low, (place == 1) | (place == 2), first]).astype(jnp.int32)
    blocks = activations.T.reshape(LINE, units // LINE, tokens)
    w = [jnp.where(low, blocks[j], blocks[3 - j]) for j in range(LINE)]
    other = plan[0] + plan[1] - top
    return lax.switch(other - 1, [line_branch(m, top, scale) for m in range(1, top)], flags, *w)


def solution(mesh):
    fast = mesh.shape["dp"] == LINE
    return jax.shard_map(
        shards_line if fast else shards_any,
        mesh=mesh,
        in_specs=(P("dp", "tensor"), P()),
        out_specs=P(None, "dp", "tensor"),
        check_vma=False,
    )
```

```python
import functools
import math

import jax
import jax.numpy as jnp
from jax import lax
from jax.experimental import pallas as pl
from jax.experimental.pallas import tpu as pltpu
from jax.sharding import PartitionSpec as P

ROUNDS = 2
LINE = 4
LANES = 128
EDGE_VMEM = 20 * 2**20
MIDDLE_VMEM = 36 * 2**20


def swapped(x, axis, apart):
    return lax.ppermute(x, axis, [(i, i ^ 1 << apart) for i in range(lax.axis_size(axis))])


def partner_panel(own, mask, width):
    current = own
    for bit in range(width):
        taken = jnp.bitwise_and(jnp.right_shift(mask, bit), 1) == 1
        current = jnp.where(taken, swapped(current, "tensor", bit), current)
    return current


def shards_any(activations, plan):
    width = lax.axis_size("tensor").bit_length() - 1
    scale = jnp.float32(1.0 / math.sqrt(activations.shape[0] * lax.axis_size("dp")))
    tiles = []
    for r in range(ROUNDS):
        other = partner_panel(activations, plan[r], width)
        tiles.append(
            lax.dot_general(other, activations, (((0,), (0,)), ((), ())), preferred_element_type=jnp.float32)
        )
    return lax.psum_scatter(jnp.stack(tiles), "dp", scatter_dimension=1, tiled=True) * scale


def inward(x):
    return lax.ppermute(x, "dp", [(0, 1), (3, 2)])


def across(x):
    return lax.ppermute(x, "dp", [(1, 2), (2, 1)])


def outward(x):
    return lax.ppermute(x, "dp", [(1, 0), (2, 3)])


def partner(x, mask):
    return lax.ppermute(x, "tensor", [(i, i ^ mask) for i in range(lax.axis_size("tensor"))])


def gated(values, *others):
    return lax.optimization_barrier((*values, *others))[: len(values)]


def times(rows, columns):
    return lax.dot_general(rows, columns, (((1,), (1,)), ((), ())), preferred_element_type=jnp.float32)


def pieces_of(units):
    block = units // LINE
    widths = [block // LANES * LANES] * (LINE - 1)
    widths.append(units - sum(widths))
    return [(w, (block - widths[0]) * p) for p, w in enumerate(widths)]


def edge_kernel(width, before, scale, low_ref, *refs):
    rows, news, olds = refs[:8], refs[8:12], refs[12:16] if before else ()
    out_ref, row_buf, col_buf, acc, row_sems, col_sems = refs[-6:]
    block = rows[0].shape[0]
    low = low_ref[0] == 1
    new = width - before
    for v in range(4):
        for k in range(2):
            pltpu.make_async_copy(
                rows[4 * k + v], row_buf.at[v, pl.ds(k * block, block)], row_sems.at[v]
            ).start()
        source = pl.multiple_of(jnp.where(low, 0, block - new), 16)
        target = pl.multiple_of(jnp.where(low, before, 0), 16)
        pltpu.make_async_copy(
            news[v].at[pl.ds(source, new)], col_buf.at[v, pl.ds(target, new)], col_sems.at[v]
        ).start()
        if before:
            source = pl.multiple_of(jnp.where(low, block - before, 0), 16)
            target = pl.multiple_of(jnp.where(low, 0, new), 16)
            pltpu.make_async_copy(
                olds[v].at[pl.ds(source, before)], col_buf.at[v, pl.ds(target, before)], col_sems.at[v]
            ).start()

    acc[...] = jnp.zeros_like(acc)

    def step(v, _):
        pltpu.make_async_copy(row_buf.at[v], row_buf.at[v], row_sems.at[v]).wait()
        pltpu.make_async_copy(col_buf.at[v], col_buf.at[v], col_sems.at[v]).wait()
        acc[...] += times(row_buf[v], col_buf[v])
        return 0

    lax.fori_loop(0, 4, step, 0)
    biggest = jnp.max(jnp.abs(acc[...]), axis=(0, 1), keepdims=True)
    power = jnp.ceil(jnp.log2(jnp.maximum(biggest * scale, 1e-30)))
    factor = scale * jnp.exp2(14.0 - power)
    out_ref[: 2 * block] = acc[...] * factor
    out_ref[2 * block :] = jnp.broadcast_to(power, (16, width))


def edge_tiles(low, rows, news, olds, width, before, scale):
    block, tokens = rows[0].shape
    operands = [*rows, *news, *(olds if before else ())]
    return pl.pallas_call(
        functools.partial(edge_kernel, width, before, scale),
        out_shape=jax.ShapeDtypeStruct((2 * block + 16, width), jnp.float32),
        in_specs=[pl.BlockSpec(memory_space=pltpu.SMEM)] + [pl.BlockSpec(memory_space=pl.ANY)] * len(operands),
        out_specs=pl.BlockSpec(memory_space=pltpu.VMEM),
        scratch_shapes=[
            pltpu.VMEM((4, 2 * block, tokens), jnp.bfloat16),
            pltpu.VMEM((4, width, tokens), jnp.bfloat16),
            pltpu.VMEM((2 * block, width), jnp.float32),
            pltpu.SemaphoreType.DMA((4,)),
            pltpu.SemaphoreType.DMA((4,)),
        ],
        compiler_params=pltpu.CompilerParams(vmem_limit_bytes=EDGE_VMEM),
        cost_estimate=pl.CostEstimate(
            flops=2 * 8 * block * tokens * width, bytes_accessed=2 * (8 * block + 4 * width) * tokens, transcendentals=0
        ),
        name="edge_tiles",
    )(low, *operands)


def unpack(flat, row, scale_row, block):
    return flat[row : row + block] * jnp.exp2(flat[scale_row : scale_row + 1, :1] - 14.0)


def middle_kernel(pieces, scale, flags_ref, *refs):
    rows, columns, packed = refs[:8], refs[8:24], refs[24:27]
    out_ref, row_buf, col_buf, row_sems, col_sems = refs[-5:]
    block = rows[0].shape[0]
    units = 4 * block
    low = flags_ref[0] == 1
    middle = flags_ref[1] == 1
    first = flags_ref[2]

    @pl.when(middle)
    def _():
        for v in range(4):
            for k in range(2):
                pltpu.make_async_copy(
                    rows[4 * k + v], row_buf.at[v, pl.ds(k * block, block)], row_sems.at[v]
                ).start()
            for j in range(4):
                target = pl.multiple_of(jnp.where(low, j * block, (3 - j) * block), 16)
                pltpu.make_async_copy(
                    columns[4 * v + j], col_buf.at[v, pl.ds(target, block)], col_sems.at[v]
                ).start()

        def add(v, start, width):
            tile = times(row_buf[v], col_buf[v, pl.ds(start, width)]) * scale
            for k in range(2):
                part = tile[k * block : (k + 1) * block]
                place = (lax.bitwise_xor(first, k), slice(None), pl.ds(start, width))
                out_ref[place] = jnp.where(v == 0, part, out_ref[place] + part)

        wide = 4 * LANES
        full = units // wide

        def group(v, _):
            pltpu.make_async_copy(row_buf.at[v], row_buf.at[v], row_sems.at[v]).wait()
            pltpu.make_async_copy(col_buf.at[v], col_buf.at[v], col_sems.at[v]).wait()

            def step(i, _):
                add(v, pl.multiple_of(i * wide, wide), wide)
                return 0

            lax.fori_loop(0, full, step, 0)
            if units % wide:
                add(v, full * wide, units % wide)
            return 0

        lax.fori_loop(0, 4, group, 0)

    @pl.when(jnp.logical_not(middle))
    def _():
        done = 0
        for p, (width, _) in enumerate(pieces[:3]):
            start = pl.multiple_of(jnp.where(low, done, units - done - width), LANES)
            for k in range(2):
                out_ref[lax.bitwise_xor(first, k), :, pl.ds(start, width)] = unpack(packed[p], k * block, 2 * block, block)
            done += width


def middle_tiles(flags, rows, columns, packed, scale):
    block, tokens = rows[0].shape
    units = 4 * block
    operands = [*rows, *columns]
    return pl.pallas_call(
        functools.partial(middle_kernel, pieces_of(units), scale),
        out_shape=jax.ShapeDtypeStruct((2, block, units), jnp.float32),
        in_specs=[pl.BlockSpec(memory_space=pltpu.SMEM)]
        + [pl.BlockSpec(memory_space=pl.ANY)] * len(operands)
        + [pl.BlockSpec(memory_space=pltpu.VMEM)] * len(packed),
        out_specs=pl.BlockSpec(memory_space=pltpu.VMEM),
        scratch_shapes=[
            pltpu.VMEM((4, 2 * block, tokens), jnp.bfloat16),
            pltpu.VMEM((4, units, tokens), jnp.bfloat16),
            pltpu.SemaphoreType.DMA((4,)),
            pltpu.SemaphoreType.DMA((4,)),
        ],
        compiler_params=pltpu.CompilerParams(vmem_limit_bytes=MIDDLE_VMEM),
        cost_estimate=pl.CostEstimate(
            flops=2 * 8 * block * tokens * units, bytes_accessed=2 * (8 * block + 4 * units) * tokens, transcendentals=0
        ),
        name="middle_tiles",
    )(flags, *operands, *packed)


def last_kernel(width, flags_ref, out_in, flat_ref, out_ref, buf, sem):
    block, units = out_in.shape[1:]
    low = flags_ref[0] == 1
    first = flags_ref[2]

    @pl.when(flags_ref[1] == 0)
    def _():
        start = pl.multiple_of(jnp.where(low, units - width, 0), LANES)
        for k in range(2):
            buf[lax.bitwise_xor(first, k)] = unpack(flat_ref, k * block, 2 * block, block)
        copy = pltpu.make_async_copy(buf, out_ref.at[:, :, pl.ds(start, width)], sem)
        copy.start()
        copy.wait()


def last_tiles(flags, out, flat):
    width = flat.shape[1]
    return pl.pallas_call(
        functools.partial(last_kernel, width),
        out_shape=jax.ShapeDtypeStruct(out.shape, out.dtype),
        in_specs=[
            pl.BlockSpec(memory_space=pltpu.SMEM),
            pl.BlockSpec(memory_space=pl.ANY),
            pl.BlockSpec(memory_space=pltpu.VMEM),
        ],
        out_specs=pl.BlockSpec(memory_space=pl.ANY),
        scratch_shapes=[pltpu.VMEM((2, out.shape[1], width), jnp.float32), pltpu.SemaphoreType.DMA],
        input_output_aliases={1: 0},
        compiler_params=pltpu.CompilerParams(vmem_limit_bytes=MIDDLE_VMEM),
        cost_estimate=pl.CostEstimate(flops=0, bytes_accessed=6 * flat.size, transcendentals=0),
        name="last_tiles",
    )(flags, out, flat)


def line_branch(mask, top, scale):
    rest = top ^ mask

    def run(flags, *w):
        low = flags[:1]
        e, f, g = [None] * 4, [None] * 4, [None] * 4
        pieces = pieces_of(4 * w[0].shape[0])

        def near(p):
            rows = [wm0, em0, fm0, gm0, w70, e70, f70, g70]
            columns = [[x[j] for x in (w, e, f, g)] for j in (p, max(p - 1, 0))]
            return edge_tiles(low, rows, *columns, *pieces[p], scale).astype(jnp.float16)

        f[0], e[3], wm0, f[1] = across(w[3]), inward(w[3]), partner(w[0], mask), across(w[2])

        x, w2, y, w70 = gated((e[3], w[2], f[0], wm0), wm0)
        g[0], e[2], fm0, w70 = across(x), inward(w2), partner(y, mask), partner(w70, rest)

        x, w0, w1, y = gated((e[2], w[0], w[1], fm0), f[1], e[2], fm0, w70)
        g[1], e[0], wm1, f70 = across(x), inward(w0), partner(w1, mask), partner(y, rest)

        w1, x, y, z = gated((w[1], wm0, g[0], wm1), e[0], f70)
        f[2], em0, gm0, w71 = across(w1), inward(x), partner(y, mask), partner(z, rest)

        w0, x, y, z = gated((w[0], w70, f[1], gm0), g[1], em0, gm0, w71)
        f[3], e70, fm1, g70 = across(w0), inward(x), partner(y, mask), partner(z, rest)

        w1, y, z = gated((w[1], g[1], fm1), f[2], e70, fm1, g70)
        e[1], gm1, f71 = inward(w1), partner(y, mask), partner(z, rest)
        flat = near(0)
        sent = [outward(flat)]

        x, y, w1, z = gated((e[1], e[0], wm1, gm1), f[3], f71, flat)
        g[2], g[3], em1, g71 = across(x), across(y), inward(w1), partner(z, rest)
        flat = near(1)
        sent.append(outward(flat))

        w1, _ = gated((w71, flat), g[2], em1, g71, sent[0])
        e71 = inward(w1)
        flat = near(2)
        sent.append(outward(flat))

        g[3], _ = gated((g[3], flat), e71, sent[1])
        sent.append(outward(near(3)))
        sent = [x.astype(jnp.float32) for x in sent]
        own = [wm1, em1, fm1, gm1, w71, e71, f71, g71]
        columns = [x[j] for x in (w, e, f, g) for j in range(4)]
        out = middle_tiles(flags, own, columns, sent[:3], scale)
        return last_tiles(flags, out, sent[3])

    return run


def shards_line(activations, plan):
    tokens, units = activations.shape
    top = lax.axis_size("tensor") - 1
    scale = 1.0 / math.sqrt(tokens * LINE)
    place = lax.axis_index("dp")
    low = place < 2
    first = plan[0] == top
    flags = jnp.stack([low, (place == 1) | (place == 2), first]).astype(jnp.int32)
    blocks = activations.T.reshape(LINE, units // LINE, tokens)
    w = [jnp.where(low, blocks[j], blocks[3 - j]) for j in range(LINE)]
    other = plan[0] + plan[1] - top
    return lax.switch(other - 1, [line_branch(m, top, scale) for m in range(1, top)], flags, *w)


def solution(mesh):
    fast = mesh.shape["dp"] == LINE
    return jax.shard_map(
        shards_line if fast else shards_any,
        mesh=mesh,
        in_specs=(P("dp", "tensor"), P()),
        out_specs=P(None, "dp", "tensor"),
        check_vma=False,
    )
```

```python
import functools
import math

import jax
import jax.numpy as jnp
from jax import lax
from jax.experimental import pallas as pl
from jax.experimental.pallas import tpu as pltpu
from jax.sharding import PartitionSpec as P

ROUNDS = 2
LINE = 4
LANES = 128
STRIP = 16
EDGE_VMEM = 20 * 2**20
MIDDLE_VMEM = 36 * 2**20


def swapped(x, axis, apart):
    return lax.ppermute(x, axis, [(i, i ^ 1 << apart) for i in range(lax.axis_size(axis))])


def partner_panel(own, mask, width):
    current = own
    for bit in range(width):
        taken = jnp.bitwise_and(jnp.right_shift(mask, bit), 1) == 1
        current = jnp.where(taken, swapped(current, "tensor", bit), current)
    return current


def shards_any(activations, plan):
    width = lax.axis_size("tensor").bit_length() - 1
    scale = jnp.float32(1.0 / math.sqrt(activations.shape[0] * lax.axis_size("dp")))
    tiles = []
    for r in range(ROUNDS):
        other = partner_panel(activations, plan[r], width)
        tiles.append(
            lax.dot_general(other, activations, (((0,), (0,)), ((), ())), preferred_element_type=jnp.float32)
        )
    return lax.psum_scatter(jnp.stack(tiles), "dp", scatter_dimension=1, tiled=True) * scale


def inward(x):
    return lax.ppermute(x, "dp", [(0, 1), (3, 2)])


def across(x):
    return lax.ppermute(x, "dp", [(1, 2), (2, 1)])


def outward(x):
    return lax.ppermute(x, "dp", [(1, 0), (2, 3)])


def partner(x, mask):
    return lax.ppermute(x, "tensor", [(i, i ^ mask) for i in range(lax.axis_size("tensor"))])


def gated(values, *others):
    return lax.optimization_barrier((*values, *others))[: len(values)]


def strip(i):
    return pl.ds(pl.multiple_of(i * STRIP, STRIP), STRIP)


def times(rows, columns):
    return lax.dot_general(rows, columns, (((1,), (1,)), ((), ())), preferred_element_type=jnp.float32)


def end_start(low, quarter):
    return pl.multiple_of(jnp.where(low, 0, quarter), STRIP)


def own_start(low, quarter):
    return pl.multiple_of(jnp.where(low, quarter, 0), STRIP)


def pieces_of(units):
    near = units // 2 // LANES * LANES
    last = (units - near) // 2 // LANES * LANES
    return near, units - near - last, last


def load_rows(rows, starts, row_buf, sems, quarter):
    for k, blocks in enumerate(rows):
        for v, block in enumerate(blocks):
            start = starts if block.shape[0] > quarter else 0
            pltpu.make_async_copy(
                block.at[pl.ds(start, quarter)], row_buf.at[v, pl.ds(k * quarter, quarter)], sems.at[v]
            ).start()


def wait_all(buf, sem):
    pltpu.make_async_copy(buf, buf, sem).wait()


def edge_kernel(masks, piece, width, tile, scale, low_ref, *refs):
    rows = [refs[4 * k : 4 * k + 4] for k in range(masks)]
    nears, fars = refs[4 * masks : 4 * masks + 4], refs[4 * masks + 4 : -6]
    out_ref, row_buf, col_buf, acc, row_sems, col_sems = refs[-6:]
    quarter = row_buf.shape[1] // masks
    half = 2 * quarter
    near_width, middle_width, _ = pieces_of(4 * quarter)
    low = low_ref[0] == 1

    load_rows(rows, end_start(low, quarter), row_buf, row_sems, quarter)
    for v in range(4):

        def load(block, source, target, size):
            pltpu.make_async_copy(
                block.at[pl.ds(pl.multiple_of(source, STRIP), size)],
                col_buf.at[v, pl.ds(pl.multiple_of(target, STRIP), size)],
                col_sems.at[v],
            ).start()

        if piece == 0:
            load(nears[v], jnp.where(low, 0, half - width), 0, width)
        elif piece == 1:
            before = half - near_width
            new = width - before
            load(nears[v], jnp.where(low, near_width, 0), jnp.where(low, 0, new), before)
            source = jnp.where(low, 0, half - new) if fars[v].shape[0] == half else 0
            load(fars[v], source, jnp.where(low, before, 0), new)
        else:
            source = jnp.where(low, half - width, 0) if fars[v].shape[0] == half else 0
            load(fars[v], source, 0, width)

    @pl.loop(0, 4)
    def _(v):
        wait_all(row_buf.at[v], row_sems.at[v])
        wait_all(col_buf.at[v], col_sems.at[v])

        @pl.loop(0, masks)
        def _(k):
            part = pl.ds(pl.multiple_of(k * quarter, STRIP), quarter)

            @pl.loop(0, width // tile)
            def _(n):
                columns = pl.ds(pl.multiple_of(n * tile, LANES), tile)
                total = times(row_buf[v, part], col_buf[v, columns])

                @pl.when(v == 0)
                def _():
                    acc[part, columns] = total

                @pl.when(v > 0)
                def _():
                    acc[part, columns] += total

    def larger(i, most):
        return jnp.maximum(most, jnp.abs(acc[strip(i)]))

    strips = masks * quarter // STRIP
    most = lax.fori_loop(0, strips, larger, jnp.zeros((STRIP, width), jnp.float32))
    biggest = jnp.max(most, axis=(0, 1), keepdims=True)
    power = jnp.ceil(jnp.log2(jnp.maximum(biggest * scale, 1e-30)))
    factor = scale * jnp.exp2(14.0 - power)

    @pl.loop(0, strips)
    def _(i):
        out_ref[strip(i)] = acc[strip(i)] * factor

    out_ref[masks * quarter :] = jnp.broadcast_to(power, (STRIP, width))


def edge_tiles(low, rows, nears, fars, piece, quarter, scale):
    masks, tokens = len(rows), rows[0][0].shape[1]
    width = pieces_of(4 * quarter)[piece]
    tile = next(t for t in (512, 384, 256, 128) if width % t == 0)
    operands = [*sum(rows, []), *nears, *fars]
    flat = pl.pallas_call(
        functools.partial(edge_kernel, masks, piece, width, tile, scale),
        out_shape=jax.ShapeDtypeStruct((masks * quarter + STRIP, width), jnp.float32),
        in_specs=[pl.BlockSpec(memory_space=pltpu.SMEM)] + [pl.BlockSpec(memory_space=pl.ANY)] * len(operands),
        out_specs=pl.BlockSpec(memory_space=pltpu.VMEM),
        scratch_shapes=[
            pltpu.VMEM((4, masks * quarter, tokens), jnp.bfloat16),
            pltpu.VMEM((4, width, tokens), jnp.bfloat16),
            pltpu.VMEM((masks * quarter, width), jnp.float32),
            pltpu.SemaphoreType.DMA((4,)),
            pltpu.SemaphoreType.DMA((4,)),
        ],
        compiler_params=pltpu.CompilerParams(vmem_limit_bytes=EDGE_VMEM),
        cost_estimate=pl.CostEstimate(
            flops=8 * masks * quarter * tokens * width,
            bytes_accessed=8 * (masks * quarter + width) * tokens,
            transcendentals=0,
        ),
        name="edge_tiles",
    )(low, *operands)
    return flat.astype(jnp.float16)


def unpack(flat, target, round_of, columns, quarter):
    rows = flat.shape[0] - STRIP
    factor = jnp.exp2(flat[rows : rows + 1, :1] - 14.0)
    strips = quarter // STRIP

    @pl.loop(0, rows // STRIP)
    def _(i):
        k = i // strips
        target[round_of(k), strip(i - k * strips), columns] = flat[strip(i)] * factor


def middle_kernel(scale, flags_ref, *refs):
    rows, nears, fars, packed = [refs[:4], refs[4:8]], refs[8:12], refs[12:17], refs[17:20]
    out_ref, row_buf, col_buf, row_sems, col_sems = refs[-5:]
    quarter = row_buf.shape[1] // 2
    half, units = 2 * quarter, 4 * quarter
    near_width, middle_width, last_width = pieces_of(units)
    low = flags_ref[0] == 1
    middle = flags_ref[1] == 1
    first = flags_ref[2]

    @pl.when(middle)
    def _():
        load_rows(rows, own_start(low, quarter), row_buf, row_sems, quarter)
        for v in range(4):

            def load(block, target):
                size = block.shape[0]
                pltpu.make_async_copy(
                    block, col_buf.at[v, pl.ds(pl.multiple_of(target, STRIP), size)], col_sems.at[v]
                ).start()

            load(nears[v], jnp.where(low, 0, half))
            if v < 3:
                load(fars[v], jnp.where(low, half, 0))
            else:
                load(fars[3], jnp.where(low, half, last_width))
                load(fars[4], jnp.where(low, units - last_width, 0))

        wide = 4 * LANES
        full = units // wide

        def add(v, k, start, width):
            columns = pl.ds(start, width)
            part = pl.ds(pl.multiple_of(k * quarter, STRIP), quarter)
            total = times(row_buf[v, part], col_buf[v, columns]) * scale
            place = (lax.bitwise_xor(first, k), slice(None), columns)

            @pl.when(v == 0)
            def _():
                out_ref[place] = total

            @pl.when(v > 0)
            def _():
                out_ref[place] += total

        @pl.loop(0, 4)
        def _(v):
            wait_all(row_buf.at[v], row_sems.at[v])
            wait_all(col_buf.at[v], col_sems.at[v])

            @pl.loop(0, 2 * full)
            def _(i):
                k = i // full
                add(v, k, pl.multiple_of((i - k * full) * wide, wide), wide)

            if units % wide:

                @pl.loop(0, 2)
                def _(k):
                    add(v, k, full * wide, units % wide)

    @pl.when(jnp.logical_not(middle))
    def _():
        near = pl.ds(pl.multiple_of(jnp.where(low, 0, units - near_width), LANES), near_width)
        inner = pl.ds(pl.multiple_of(jnp.where(low, near_width, last_width), LANES), middle_width)
        unpack(packed[0], out_ref, lambda k: first, near, quarter)
        unpack(packed[1], out_ref, lambda k: 1 - first, near, quarter)
        unpack(packed[2], out_ref, lambda k: lax.bitwise_xor(first, k), inner, quarter)


def middle_tiles(flags, rows, nears, fars, packed, quarter, scale):
    tokens, units = rows[0][0].shape[1], 4 * quarter
    operands = [*sum(rows, []), *nears, *fars]
    return pl.pallas_call(
        functools.partial(middle_kernel, scale),
        out_shape=jax.ShapeDtypeStruct((2, quarter, units), jnp.float32),
        in_specs=[pl.BlockSpec(memory_space=pltpu.SMEM)]
        + [pl.BlockSpec(memory_space=pl.ANY)] * len(operands)
        + [pl.BlockSpec(memory_space=pltpu.VMEM)] * len(packed),
        out_specs=pl.BlockSpec(memory_space=pltpu.VMEM),
        scratch_shapes=[
            pltpu.VMEM((4, 2 * quarter, tokens), jnp.bfloat16),
            pltpu.VMEM((4, units, tokens), jnp.bfloat16),
            pltpu.SemaphoreType.DMA((4,)),
            pltpu.SemaphoreType.DMA((4,)),
        ],
        compiler_params=pltpu.CompilerParams(vmem_limit_bytes=MIDDLE_VMEM),
        cost_estimate=pl.CostEstimate(
            flops=16 * quarter * tokens * units, bytes_accessed=8 * (2 * quarter + units) * tokens, transcendentals=0
        ),
        name="middle_tiles",
    )(flags, *operands, *packed)


def last_kernel(flags_ref, out_in, flat_ref, out_ref, buf, sem):
    quarter, units = out_in.shape[1:]
    width = flat_ref.shape[1]
    first = flags_ref[2]

    @pl.when(flags_ref[1] == 0)
    def _():
        start = pl.multiple_of(jnp.where(flags_ref[0] == 1, units - width, 0), LANES)
        unpack(flat_ref, buf, lambda k: lax.bitwise_xor(first, k), slice(None), quarter)
        copy = pltpu.make_async_copy(buf, out_ref.at[:, :, pl.ds(start, width)], sem)
        copy.start()
        copy.wait()


def last_tiles(flags, out, flat):
    return pl.pallas_call(
        last_kernel,
        out_shape=jax.ShapeDtypeStruct(out.shape, out.dtype),
        in_specs=[
            pl.BlockSpec(memory_space=pltpu.SMEM),
            pl.BlockSpec(memory_space=pl.ANY),
            pl.BlockSpec(memory_space=pltpu.VMEM),
        ],
        out_specs=pl.BlockSpec(memory_space=pl.ANY),
        scratch_shapes=[pltpu.VMEM((2, out.shape[1], flat.shape[1]), jnp.float32), pltpu.SemaphoreType.DMA],
        input_output_aliases={1: 0},
        compiler_params=pltpu.CompilerParams(vmem_limit_bytes=EDGE_VMEM),
        cost_estimate=pl.CostEstimate(flops=0, bytes_accessed=6 * flat.size, transcendentals=0),
        name="last_tiles",
    )(flags, out, flat)


def line_branch(mask, top, scale):
    rest = top ^ mask

    def run(flags, w_near, w_far):
        quarter = w_near.shape[0] // 2
        units = 4 * quarter
        low = flags[0] == 1
        near_width, middle_width, last_width = pieces_of(units)

        def rows_of(x, start, size):
            return lax.dynamic_slice_in_dim(x, start, size, 0)

        def end_part(x):
            return rows_of(x, jnp.where(low, 0, quarter), quarter)

        def own_part(x):
            return rows_of(x, jnp.where(low, quarter, 0), quarter)

        f_near, e_far, wm, e_near = across(w_far), inward(w_far), partner(w_near, mask), inward(w_near)

        e_far, f_near, wm = gated((e_far, f_near, wm), e_far)
        g_near, f_far, fm, wt = across(e_far), across(w_near), partner(f_near, mask), partner(wm, rest)

        g_near, e_near, fm, wt = gated((g_near, e_near, fm, wt), wm)
        gm_end, ft_end, em_end = partner(end_part(g_near), mask), partner(end_part(fm), rest), inward(end_part(wm))
        gm_own = partner(own_part(g_near), mask)

        gm_end, ft_end, em_end, wt_end = gated((gm_end, ft_end, em_end, end_part(wt)))
        gt_end, et_end = partner(gm_end, rest), inward(wt_end)
        inner = 2 * quarter - last_width
        g_mid = across(rows_of(e_near, jnp.where(low, last_width, 0), inner))
        nears = [w_near, e_near, f_near, g_near]
        ends_m = [wm, em_end, fm, gm_end]
        flat_m = edge_tiles(flags[:1], [ends_m], nears, [], 0, quarter, scale)
        sent = [outward(flat_m)]

        gt_end, et_end, gm_own, f_far = gated((gt_end, et_end, gm_own, f_far), flat_m)
        ft_own, em_own = partner(own_part(fm), rest), inward(own_part(wm))
        g_last = across(rows_of(e_near, jnp.where(low, 0, inner), last_width))
        ends_t = [wt, et_end, ft_end, gt_end]
        flat_t = edge_tiles(flags[:1], [ends_t], nears, [], 0, quarter, scale)
        sent.append(outward(flat_t))

        ft_own, em_own, g_mid, gm_own, wt_own = gated((ft_own, em_own, g_mid, gm_own, own_part(wt)), flat_t, sent[0])
        gt_own, et_own = partner(gm_own, rest), inward(wt_own)
        fars = [w_far, e_far, f_far, g_mid]
        flat = edge_tiles(flags[:1], [ends_m, ends_t], nears, fars, 1, quarter, scale)
        sent.append(outward(flat))

        g_last, gt_own, et_own = gated((g_last, gt_own, et_own), flat, sent[1])
        fars = [w_far, e_far, f_far, g_last]
        flat = edge_tiles(flags[:1], [ends_m, ends_t], nears, fars, 2, quarter, scale)
        last = outward(flat).astype(jnp.float32)

        sent = [x.astype(jnp.float32) for x in sent]
        own = [[wm, em_own, fm, gm_own], [wt, et_own, ft_own, gt_own]]
        fars = [w_far, e_far, f_far, g_mid, g_last]
        out = middle_tiles(flags, own, nears, fars, sent, quarter, scale)
        return last_tiles(flags, out, last)

    return run


def shards_line(activations, plan):
    tokens, units = activations.shape
    top = lax.axis_size("tensor") - 1
    scale = 1.0 / math.sqrt(tokens * LINE)
    place = lax.axis_index("dp")
    low = place < 2
    first = plan[0] == top
    flags = jnp.stack([low, (place == 1) | (place == 2), first]).astype(jnp.int32)
    top_half, bottom_half = jnp.split(activations.T, 2)
    halves = [jnp.where(low, top_half, bottom_half), jnp.where(low, bottom_half, top_half)]
    other = plan[0] + plan[1] - top
    return lax.switch(other - 1, [line_branch(m, top, scale) for m in range(1, top)], flags, *halves)


def solution(mesh):
    fast = mesh.shape["dp"] == LINE
    return jax.shard_map(
        shards_line if fast else shards_any,
        mesh=mesh,
        in_specs=(P("dp", "tensor"), P()),
        out_specs=P(None, "dp", "tensor"),
        check_vma=False,
    )
```

```python
import functools
import math

import jax
import jax.numpy as jnp
from jax import lax
from jax.experimental import pallas as pl
from jax.experimental.pallas import tpu as pltpu
from jax.sharding import PartitionSpec as P

ROUNDS = 2
LINE = 4
LANES = 128
STRIP = 104
TAIL = 16
EDGE_VMEM = 16 * 2**20
MIDDLE_VMEM = 24 * 2**20


def swapped(x, axis, apart):
    return lax.ppermute(x, axis, [(i, i ^ 1 << apart) for i in range(lax.axis_size(axis))])


def partner_panel(own, mask, width):
    current = own
    for bit in range(width):
        taken = jnp.bitwise_and(jnp.right_shift(mask, bit), 1) == 1
        current = jnp.where(taken, swapped(current, "tensor", bit), current)
    return current


def shards_any(activations, plan):
    width = lax.axis_size("tensor").bit_length() - 1
    scale = jnp.float32(1.0 / math.sqrt(activations.shape[0] * lax.axis_size("dp")))
    tiles = []
    for r in range(ROUNDS):
        other = partner_panel(activations, plan[r], width)
        tiles.append(
            lax.dot_general(other, activations, (((0,), (0,)), ((), ())), preferred_element_type=jnp.float32)
        )
    return lax.psum_scatter(jnp.stack(tiles), "dp", scatter_dimension=1, tiled=True) * scale


def inward(x):
    return lax.ppermute(x, "dp", [(0, 1), (3, 2)])


def across(x):
    return lax.ppermute(x, "dp", [(1, 2), (2, 1)])


def outward(x):
    return lax.ppermute(x, "dp", [(1, 0), (2, 3)])


def partner(x, mask):
    return lax.ppermute(x, "tensor", [(i, i ^ mask) for i in range(lax.axis_size("tensor"))])


def gated(values, *others):
    return lax.optimization_barrier((*values, *others))[: len(values)]


def strip(i):
    return pl.ds(pl.multiple_of(i * STRIP, 8), STRIP)


def times(rows, columns):
    return lax.dot_general(rows, columns, (((1,), (1,)), ((), ())), preferred_element_type=jnp.float32)


def end_start(low, quarter):
    return jnp.where(low, 0, quarter)


def own_start(low, quarter):
    return jnp.where(low, quarter, 0)


def pieces_of(units):
    near = units // 2 // LANES * LANES
    last = (units - near) // 2 // LANES * LANES
    return near, units - near - last, last


def cut(ref, start, size):
    return ref[pl.ds(pl.multiple_of(start, 16), size)]


class Columns:
    def __init__(self, low, quarter):
        self.low, self.half = low, 2 * quarter
        self.near_width, middle, self.last = pieces_of(4 * quarter)
        self.spill = self.half - self.near_width
        self.inner = middle - 2 * self.spill

    def near(self, block, n, tile):
        return cut(block, jnp.where(self.low, 0, self.spill) + n * tile, tile)

    def seam(self, near, far):
        top = far.shape[0] - self.spill if far.shape[0] < self.half else self.half - self.spill
        inward = jnp.where(self.low, cut(near, self.near_width, self.spill), cut(far, top, self.spill))
        outward = jnp.where(self.low, cut(far, 0, self.spill), cut(near, 0, self.spill))
        return jnp.concatenate([inward, outward])

    def middle(self, far):
        past = self.last if far.shape[0] == self.half else 0
        return cut(far, jnp.where(self.low, self.spill, past), self.inner)

    def outer(self, far):
        past = self.half - self.last if far.shape[0] == self.half else 0
        return cut(far, jnp.where(self.low, past, 0), self.last)


def both(rows, start, quarter):
    parts = [cut(ref, start, quarter) if ref.shape[0] > quarter else ref[...] for ref in rows]
    return jnp.concatenate(parts) if len(parts) > 1 else parts[0]


def summed(rows, start, quarter, columns):
    total = None
    for v in range(4):
        term = times(both([r[v] for r in rows], start, quarter), columns(v))
        total = term if total is None else total + term
    return total


def edge_kernel(masks, piece, scale, flags_ref, *refs):
    rows = [refs[4 * k : 4 * k + 4] for k in range(masks)]
    nears, fars = refs[4 * masks : -2][:4], refs[4 * masks : -2][-4:]
    out_ref, most = refs[-2:]
    height = out_ref.shape[0] - TAIL
    quarter = height // masks
    low = flags_ref[0] == 1

    @pl.when(flags_ref[1] == 1)
    def _():
        cols = Columns(low, quarter)
        start = end_start(low, quarter)
        most[...] = jnp.zeros_like(most)

        def put(place, columns):
            total = summed(rows, start, quarter, columns)
            out_ref[:height, place] = total
            high = jnp.max(jnp.abs(total).reshape(height // 8, 8, total.shape[1]), axis=0)
            for i in range(total.shape[1] // LANES):
                most[...] = jnp.maximum(most[...], high[:, i * LANES : (i + 1) * LANES])

        if piece == 0:
            tile = 3 * LANES

            @pl.loop(0, cols.near_width // tile)
            def _(n):
                put(pl.ds(pl.multiple_of(n * tile, LANES), tile), lambda v: cols.near(nears[v], n, tile))

        elif piece == 1:
            seam = 2 * cols.spill
            put(
                pl.ds(pl.multiple_of(jnp.where(low, 0, cols.inner), LANES), seam),
                lambda v: cols.seam(nears[v], fars[v]),
            )
            put(
                pl.ds(pl.multiple_of(jnp.where(low, seam, 0), LANES), cols.inner),
                lambda v: cols.middle(fars[v]),
            )
        else:
            put(slice(None), lambda v: cols.outer(fars[v]))

        biggest = jnp.max(most[...], axis=(0, 1), keepdims=True)
        power = jnp.ceil(jnp.log2(jnp.maximum(biggest * scale, 1e-30)))
        factor = scale * jnp.exp2(14.0 - power)

        @pl.loop(0, height // STRIP)
        def _(i):
            out_ref[strip(i)] = out_ref[strip(i)] * factor

        out_ref[height:] = jnp.broadcast_to(power, (TAIL, out_ref.shape[1]))


def edge_tiles(flags, rows, nears, fars, piece, quarter, scale):
    masks, tokens = len(rows), rows[0][0].shape[1]
    width = pieces_of(4 * quarter)[piece]
    operands = [*sum(rows, []), *nears, *fars]
    flat = pl.pallas_call(
        functools.partial(edge_kernel, masks, piece, scale),
        out_shape=jax.ShapeDtypeStruct((masks * quarter + TAIL, width), jnp.float32),
        in_specs=[pl.BlockSpec(memory_space=pltpu.SMEM)] + [pl.BlockSpec(memory_space=pltpu.VMEM)] * len(operands),
        out_specs=pl.BlockSpec(memory_space=pltpu.VMEM),
        scratch_shapes=[pltpu.VMEM((8, LANES), jnp.float32)],
        compiler_params=pltpu.CompilerParams(vmem_limit_bytes=EDGE_VMEM),
        cost_estimate=pl.CostEstimate(
            flops=8 * masks * quarter * tokens * width,
            bytes_accessed=8 * (masks * quarter + width) * tokens,
            transcendentals=0,
        ),
        name="edge_tiles",
    )(flags, *operands)
    return flat.astype(jnp.float16)


def unpack(flat, target, rounds, columns, quarter):
    rows = flat.shape[0] - TAIL
    factor = jnp.exp2(flat[rows : rows + 1, :1] - 14.0)
    for k, place in enumerate(rounds):

        @pl.loop(0, quarter // STRIP)
        def _(i):
            target[place, strip(i), columns] = flat[strip(i + k * (quarter // STRIP))] * factor


def middle_kernel(scale, flags_ref, *refs):
    rows, nears, fars, packed = [refs[:4], refs[4:8]], refs[8:12], refs[12:17], refs[17:20]
    out_ref = refs[-1]
    quarter, units = out_ref.shape[1:]
    near_width, middle_width, last_width = pieces_of(units)
    low = flags_ref[0] == 1
    middle = flags_ref[1] == 1
    first = flags_ref[2]

    @pl.when(middle)
    def _():
        cols = Columns(low, quarter)
        start = own_start(low, quarter)

        def put(at, size, columns):
            total = summed(rows, start, quarter, columns) * scale
            for k in range(2):
                place = (lax.bitwise_xor(first, k), slice(None), pl.ds(pl.multiple_of(at, LANES), size))
                out_ref[place] = total[k * quarter : (k + 1) * quarter]

        tile = 3 * LANES

        @pl.loop(0, near_width // tile)
        def _(n):
            put(jnp.where(low, 0, units - near_width) + n * tile, tile, lambda v: cols.near(nears[v], n, tile))

        seam = 2 * cols.spill
        put(near_width, seam, lambda v: cols.seam(nears[v], fars[v]))
        put(jnp.where(low, near_width + seam, last_width), cols.inner, lambda v: cols.middle(fars[v]))
        put(jnp.where(low, units - last_width, 0), last_width, lambda v: cols.outer(fars[v + v // 3]))

    @pl.when(jnp.logical_not(middle))
    def _():
        near = pl.ds(pl.multiple_of(jnp.where(low, 0, units - near_width), LANES), near_width)
        inner = pl.ds(pl.multiple_of(jnp.where(low, near_width, last_width), LANES), middle_width)
        unpack(packed[0], out_ref, [first], near, quarter)
        unpack(packed[1], out_ref, [1 - first], near, quarter)
        unpack(packed[2], out_ref, [first, 1 - first], inner, quarter)


def middle_tiles(flags, rows, nears, fars, packed, quarter, scale):
    tokens, units = rows[0][0].shape[1], 4 * quarter
    operands = [*sum(rows, []), *nears, *fars, *packed]
    return pl.pallas_call(
        functools.partial(middle_kernel, scale),
        out_shape=jax.ShapeDtypeStruct((2, quarter, units), jnp.float32),
        in_specs=[pl.BlockSpec(memory_space=pltpu.SMEM)] + [pl.BlockSpec(memory_space=pltpu.VMEM)] * len(operands),
        out_specs=pl.BlockSpec(memory_space=pltpu.VMEM),
        compiler_params=pltpu.CompilerParams(vmem_limit_bytes=MIDDLE_VMEM),
        cost_estimate=pl.CostEstimate(
            flops=16 * quarter * tokens * units, bytes_accessed=8 * (2 * quarter + units) * tokens, transcendentals=0
        ),
        name="middle_tiles",
    )(flags, *operands)


def last_kernel(flags_ref, out_in, flat_ref, out_ref, buf, sem):
    quarter, units = out_in.shape[1:]
    width = flat_ref.shape[1]
    first = flags_ref[2]

    @pl.when(flags_ref[1] == 0)
    def _():
        start = pl.multiple_of(jnp.where(flags_ref[0] == 1, units - width, 0), LANES)
        unpack(flat_ref, buf, [first, 1 - first], slice(None), quarter)
        copy = pltpu.make_async_copy(buf, out_ref.at[:, :, pl.ds(start, width)], sem)
        copy.start()
        copy.wait()


def last_tiles(flags, out, flat):
    return pl.pallas_call(
        last_kernel,
        out_shape=jax.ShapeDtypeStruct(out.shape, out.dtype),
        in_specs=[
            pl.BlockSpec(memory_space=pltpu.SMEM),
            pl.BlockSpec(memory_space=pl.ANY),
            pl.BlockSpec(memory_space=pltpu.VMEM),
        ],
        out_specs=pl.BlockSpec(memory_space=pl.ANY),
        scratch_shapes=[pltpu.VMEM((2, out.shape[1], flat.shape[1]), jnp.float32), pltpu.SemaphoreType.DMA],
        input_output_aliases={1: 0},
        compiler_params=pltpu.CompilerParams(vmem_limit_bytes=EDGE_VMEM),
        cost_estimate=pl.CostEstimate(flops=0, bytes_accessed=6 * flat.size, transcendentals=0),
        name="last_tiles",
    )(flags, out, flat)


def line_branch(mask, top, scale):
    rest = top ^ mask

    def run(flags, w_near, w_far):
        quarter = w_near.shape[0] // 2
        units = 4 * quarter
        low = flags[0] == 1
        near_width, middle_width, last_width = pieces_of(units)

        def rows_of(x, start, size):
            return lax.dynamic_slice_in_dim(x, start, size, 0)

        def end_part(x):
            return rows_of(x, jnp.where(low, 0, quarter), quarter)

        def own_part(x):
            return rows_of(x, jnp.where(low, quarter, 0), quarter)

        f_near, e_far, wm, e_near = across(w_far), inward(w_far), partner(w_near, mask), inward(w_near)

        e_far, f_near, wm = gated((e_far, f_near, wm), e_far)
        g_near, f_far, fm, wt = across(e_far), across(w_near), partner(f_near, mask), partner(wm, rest)

        g_near, e_near, fm, wt = gated((g_near, e_near, fm, wt), wm)
        gm_end, ft_end, em_end = partner(end_part(g_near), mask), partner(end_part(fm), rest), inward(end_part(wm))
        gm_own = partner(own_part(g_near), mask)

        nears = [w_near, e_near, f_near, g_near]
        ends_m = [wm, em_end, fm, gm_end]
        flat_m = edge_tiles(flags, [ends_m], nears, [], 0, quarter, scale)
        sent = [outward(flat_m)]

        gm_end, ft_end, wt_end = gated((gm_end, ft_end, end_part(wt)), em_end)
        gt_end, et_end = partner(gm_end, rest), inward(wt_end)
        inner = 2 * quarter - last_width
        g_mid = across(rows_of(e_near, jnp.where(low, last_width, 0), inner))

        gt_end, et_end, f_far, fm, wm, e_near = gated((gt_end, et_end, f_far, fm, wm, e_near), gm_own, flat_m)
        ft_own, em_own = partner(own_part(fm), rest), inward(own_part(wm))
        g_last = across(rows_of(e_near, jnp.where(low, 0, inner), last_width))
        ends_t = [wt, et_end, ft_end, gt_end]
        flat_t = edge_tiles(flags, [ends_t], nears, [], 0, quarter, scale)
        sent.append(outward(flat_t))

        ft_own, em_own, g_mid, gm_own, wt_own = gated((ft_own, em_own, g_mid, gm_own, own_part(wt)), flat_t, sent[0])
        gt_own, et_own = partner(gm_own, rest), inward(wt_own)
        fars = [w_far, e_far, f_far, g_mid]
        flat = edge_tiles(flags, [ends_m, ends_t], nears, fars, 1, quarter, scale)
        sent.append(outward(flat))

        g_last, gt_own, et_own = gated((g_last, gt_own, et_own), flat, sent[1])
        fars = [w_far, e_far, f_far, g_last]
        flat = edge_tiles(flags, [ends_m, ends_t], [], fars, 2, quarter, scale)
        last = outward(flat).astype(jnp.float32)

        sent = [x.astype(jnp.float32) for x in sent]
        own = [[wm, em_own, fm, gm_own], [wt, et_own, ft_own, gt_own]]
        fars = [w_far, e_far, f_far, g_mid, g_last]
        out = middle_tiles(flags, own, nears, fars, sent, quarter, scale)
        return last_tiles(flags, out, last)

    return run


def shards_line(activations, plan):
    tokens, units = activations.shape
    top = lax.axis_size("tensor") - 1
    scale = 1.0 / math.sqrt(tokens * LINE)
    place = lax.axis_index("dp")
    low = place < 2
    first = plan[0] == top
    flags = jnp.stack([low, (place == 1) | (place == 2), first]).astype(jnp.int32)
    top_half, bottom_half = jnp.split(activations.T, 2)
    halves = [jnp.where(low, top_half, bottom_half), jnp.where(low, bottom_half, top_half)]
    other = plan[0] + plan[1] - top
    return lax.switch(other - 1, [line_branch(m, top, scale) for m in range(1, top)], flags, *halves)


def solution(mesh):
    fast = mesh.shape["dp"] == LINE
    return jax.shard_map(
        shards_line if fast else shards_any,
        mesh=mesh,
        in_specs=(P("dp", "tensor"), P()),
        out_specs=P(None, "dp", "tensor"),
        check_vma=False,
    )
```

```python
import functools
import math

import jax
import jax.numpy as jnp
from jax import lax
from jax.experimental import pallas as pl
from jax.experimental.pallas import tpu as pltpu
from jax.sharding import PartitionSpec as P

ROUNDS = 2
LINE = 4
LANES = 128
STRIP = 104
TAIL = 16
SHORT = pl.CostEstimate(flops=0, bytes_accessed=1024, transcendentals=0)
EDGE_VMEM = 16 * 2**20
MIDDLE_VMEM = 24 * 2**20


def swapped(x, axis, apart):
    return lax.ppermute(x, axis, [(i, i ^ 1 << apart) for i in range(lax.axis_size(axis))])


def partner_panel(own, mask, width):
    current = own
    for bit in range(width):
        taken = jnp.bitwise_and(jnp.right_shift(mask, bit), 1) == 1
        current = jnp.where(taken, swapped(current, "tensor", bit), current)
    return current


def shards_any(activations, plan):
    width = lax.axis_size("tensor").bit_length() - 1
    scale = jnp.float32(1.0 / math.sqrt(activations.shape[0] * lax.axis_size("dp")))
    tiles = []
    for r in range(ROUNDS):
        other = partner_panel(activations, plan[r], width)
        tiles.append(
            lax.dot_general(other, activations, (((0,), (0,)), ((), ())), preferred_element_type=jnp.float32)
        )
    return lax.psum_scatter(jnp.stack(tiles), "dp", scatter_dimension=1, tiled=True) * scale


def inward(x):
    return lax.ppermute(x, "dp", [(0, 1), (3, 2)])


def across(x):
    return lax.ppermute(x, "dp", [(1, 2), (2, 1)])


def outward(x):
    return lax.ppermute(x, "dp", [(1, 0), (2, 3)])


def partner(x, mask):
    return lax.ppermute(x, "tensor", [(i, i ^ mask) for i in range(lax.axis_size("tensor"))])


def gated(values, *others):
    return lax.optimization_barrier((*values, *others))[: len(values)]


def strip(i):
    return pl.ds(pl.multiple_of(i * STRIP, 8), STRIP)


def times(rows, columns):
    return lax.dot_general(rows, columns, (((1,), (1,)), ((), ())), preferred_element_type=jnp.float32)


def end_start(low, quarter):
    return jnp.where(low, 0, quarter)


def own_start(low, quarter):
    return jnp.where(low, quarter, 0)


def pieces_of(units):
    near = units // 2 // LANES * LANES
    last = (units - near) // 2 // LANES * LANES
    return near, units - near - last, last


def cut(ref, start, size):
    return ref[pl.ds(pl.multiple_of(start, 16), size)]


class Columns:
    def __init__(self, low, quarter):
        self.low, self.half = low, 2 * quarter
        self.near_width, middle, self.last = pieces_of(4 * quarter)
        self.spill = self.half - self.near_width
        self.inner = middle - 2 * self.spill

    def near(self, block, n, tile):
        return cut(block, jnp.where(self.low, 0, self.spill) + n * tile, tile)

    def seam(self, near, far):
        top = self.half - self.spill
        inward = jnp.where(self.low, cut(near, self.near_width, self.spill), cut(far, top, self.spill))
        outward = jnp.where(self.low, cut(far, 0, self.spill), cut(near, 0, self.spill))
        return jnp.concatenate([inward, outward])

    def middle(self, far):
        return cut(far, jnp.where(self.low, self.spill, self.last), self.inner)

    def outer(self, far):
        return cut(far, jnp.where(self.low, self.half - self.last, 0), self.last)


def both(rows, start, quarter):
    parts = [cut(ref, start, quarter) if ref.shape[0] > quarter else ref[...] for ref in rows]
    return jnp.concatenate(parts) if len(parts) > 1 else parts[0]


def summed(rows, start, quarter, columns):
    total = None
    for v in range(4):
        term = times(both([r[v] for r in rows], start, quarter), columns(v))
        total = term if total is None else total + term
    return total


def edge_kernel(masks, piece, scale, flags_ref, *refs):
    rows = [refs[4 * k : 4 * k + 4] for k in range(masks)]
    nears, fars = refs[4 * masks : -2][:4], refs[4 * masks : -2][-4:]
    out_ref, most = refs[-2:]
    height = out_ref.shape[0] - TAIL
    quarter = height // masks
    low = flags_ref[0] == 1

    @pl.when(flags_ref[1] == 1)
    def _():
        cols = Columns(low, quarter)
        start = end_start(low, quarter)
        most[...] = jnp.zeros_like(most)

        def put(place, columns):
            total = summed(rows, start, quarter, columns)
            out_ref[:height, place] = total
            high = jnp.max(jnp.abs(total).reshape(height // 8, 8, total.shape[1]), axis=0)
            for i in range(total.shape[1] // LANES):
                most[...] = jnp.maximum(most[...], high[:, i * LANES : (i + 1) * LANES])

        if piece == 0:
            tile = 3 * LANES

            @pl.loop(0, cols.near_width // tile)
            def _(n):
                put(pl.ds(pl.multiple_of(n * tile, LANES), tile), lambda v: cols.near(nears[v], n, tile))

        elif piece == 1:
            seam = 2 * cols.spill
            put(
                pl.ds(pl.multiple_of(jnp.where(low, 0, cols.inner), LANES), seam),
                lambda v: cols.seam(nears[v], fars[v]),
            )
            put(
                pl.ds(pl.multiple_of(jnp.where(low, seam, 0), LANES), cols.inner),
                lambda v: cols.middle(fars[v]),
            )
        else:
            put(slice(None), lambda v: cols.outer(fars[v]))

        biggest = jnp.max(most[...], axis=(0, 1), keepdims=True)
        power = jnp.ceil(jnp.log2(jnp.maximum(biggest * scale, 1e-30)))
        factor = scale * jnp.exp2(14.0 - power)

        @pl.loop(0, height // STRIP)
        def _(i):
            out_ref[strip(i)] = out_ref[strip(i)] * factor

        out_ref[height:] = jnp.broadcast_to(power, (TAIL, out_ref.shape[1]))


def edge_tiles(flags, rows, nears, fars, piece, quarter, scale):
    masks, width = len(rows), pieces_of(4 * quarter)[piece]
    operands = [*sum(rows, []), *nears, *fars]
    flat = pl.pallas_call(
        functools.partial(edge_kernel, masks, piece, scale),
        out_shape=jax.ShapeDtypeStruct((masks * quarter + TAIL, width), jnp.float32),
        in_specs=[pl.BlockSpec(memory_space=pltpu.SMEM)] + [pl.BlockSpec(memory_space=pltpu.VMEM)] * len(operands),
        out_specs=pl.BlockSpec(memory_space=pltpu.VMEM),
        scratch_shapes=[pltpu.VMEM((8, LANES), jnp.float32)],
        compiler_params=pltpu.CompilerParams(vmem_limit_bytes=EDGE_VMEM),
        cost_estimate=SHORT,
        name="edge_tiles",
    )(flags, *operands)
    return flat.astype(jnp.float16)


def unpack(flat, target, rounds, columns, quarter):
    rows = flat.shape[0] - TAIL
    factor = jnp.exp2(flat[rows : rows + 1, :1] - 14.0)
    for k, place in enumerate(rounds):

        @pl.loop(0, quarter // STRIP)
        def _(i):
            target[place, strip(i), columns] = flat[strip(i + k * (quarter // STRIP))] * factor


def middle_kernel(scale, flags_ref, *refs):
    rows, nears, fars, packed = [refs[:4], refs[4:8]], refs[8:12], refs[12:16], refs[16:18]
    out_ref = refs[-1]
    quarter, units = out_ref.shape[1:]
    near_width, middle_width, last_width = pieces_of(units)
    low = flags_ref[0] == 1
    middle = flags_ref[1] == 1
    first = flags_ref[2]

    @pl.when(middle)
    def _():
        cols = Columns(low, quarter)
        start = own_start(low, quarter)

        def put(at, size, columns):
            total = summed(rows, start, quarter, columns) * scale
            for k in range(2):
                place = (lax.bitwise_xor(first, k), slice(None), pl.ds(pl.multiple_of(at, LANES), size))
                out_ref[place] = total[k * quarter : (k + 1) * quarter]

        tile = 3 * LANES

        @pl.loop(0, near_width // tile)
        def _(n):
            put(jnp.where(low, 0, units - near_width) + n * tile, tile, lambda v: cols.near(nears[v], n, tile))

        seam = 2 * cols.spill
        put(near_width, seam, lambda v: cols.seam(nears[v], fars[v]))
        put(jnp.where(low, near_width + seam, last_width), cols.inner, lambda v: cols.middle(fars[v]))
        put(jnp.where(low, units - last_width, 0), last_width, lambda v: cols.outer(fars[v]))

    @pl.when(jnp.logical_not(middle))
    def _():
        near = pl.ds(pl.multiple_of(jnp.where(low, 0, units - near_width), LANES), near_width)
        unpack(packed[0], out_ref, [first], near, quarter)
        unpack(packed[1], out_ref, [1 - first], near, quarter)


def middle_tiles(flags, rows, nears, fars, packed, quarter, scale):
    tokens, units = rows[0][0].shape[1], 4 * quarter
    operands = [*sum(rows, []), *nears, *fars, *packed]
    return pl.pallas_call(
        functools.partial(middle_kernel, scale),
        out_shape=jax.ShapeDtypeStruct((2, quarter, units), jnp.float32),
        in_specs=[pl.BlockSpec(memory_space=pltpu.SMEM)] + [pl.BlockSpec(memory_space=pltpu.VMEM)] * len(operands),
        out_specs=pl.BlockSpec(memory_space=pltpu.VMEM),
        compiler_params=pltpu.CompilerParams(vmem_limit_bytes=MIDDLE_VMEM),
        cost_estimate=pl.CostEstimate(
            flops=16 * quarter * tokens * units, bytes_accessed=8 * (2 * quarter + units) * tokens, transcendentals=0
        ),
        name="middle_tiles",
    )(flags, *operands)


def last_kernel(flags_ref, out_in, inner_ref, outer_ref, out_ref, buf, sem):
    quarter, units = out_in.shape[1:]
    inner, outer = inner_ref.shape[1], outer_ref.shape[1]
    low = flags_ref[0] == 1
    first = flags_ref[2]

    @pl.when(flags_ref[1] == 0)
    def _():
        at = pl.ds(pl.multiple_of(jnp.where(low, 0, outer), LANES), inner)
        unpack(inner_ref, buf, [first, 1 - first], at, quarter)
        at = pl.ds(pl.multiple_of(jnp.where(low, inner, 0), LANES), outer)
        unpack(outer_ref, buf, [first, 1 - first], at, quarter)
        start = pl.multiple_of(jnp.where(low, units - inner - outer, 0), LANES)
        copy = pltpu.make_async_copy(buf, out_ref.at[:, :, pl.ds(start, inner + outer)], sem)
        copy.start()
        copy.wait()


def last_tiles(flags, out, inner, outer):
    return pl.pallas_call(
        last_kernel,
        out_shape=jax.ShapeDtypeStruct(out.shape, out.dtype),
        in_specs=[
            pl.BlockSpec(memory_space=pltpu.SMEM),
            pl.BlockSpec(memory_space=pl.ANY),
            pl.BlockSpec(memory_space=pltpu.VMEM),
            pl.BlockSpec(memory_space=pltpu.VMEM),
        ],
        out_specs=pl.BlockSpec(memory_space=pl.ANY),
        scratch_shapes=[
            pltpu.VMEM((2, out.shape[1], inner.shape[1] + outer.shape[1]), jnp.float32),
            pltpu.SemaphoreType.DMA,
        ],
        input_output_aliases={1: 0},
        compiler_params=pltpu.CompilerParams(vmem_limit_bytes=EDGE_VMEM),
        cost_estimate=SHORT,
        name="last_tiles",
    )(flags, out, inner, outer)


def line_branch(mask, top, scale):
    rest = top ^ mask

    def run(flags, w_near, w_far):
        quarter = w_near.shape[0] // 2
        low = flags[0] == 1

        def rows_of(x, start, size):
            return lax.dynamic_slice_in_dim(x, start, size, 0)

        def end_part(x):
            return rows_of(x, jnp.where(low, 0, quarter), quarter)

        def own_part(x):
            return rows_of(x, jnp.where(low, quarter, 0), quarter)

        f_near, e_far, wm, e_near = across(w_far), inward(w_far), partner(w_near, mask), inward(w_near)

        e_far, f_near, wm = gated((e_far, f_near, wm))
        g_near, fm, wt = across(e_far), partner(f_near, mask), partner(wm, rest)

        g_near, e_near, fm, wt, w_near = gated((g_near, e_near, fm, wt, w_near))
        f_far = across(w_near)
        gm_end, ft_end, em_end = partner(end_part(g_near), mask), partner(end_part(fm), rest), inward(end_part(wm))
        gm_own = partner(own_part(g_near), mask)

        gm_end, ft_end, em_end, wt, fm = gated((gm_end, ft_end, em_end, wt, fm))
        gt_end, et_end, ft_own = partner(gm_end, rest), inward(end_part(wt)), partner(own_part(fm), rest)
        nears = [w_near, e_near, f_near, g_near]
        ends_m = [wm, em_end, fm, gm_end]
        flat_m = edge_tiles(flags, [ends_m], nears, [], 0, quarter, scale)

        gt_end, et_end, f_far, gm_own, wm, e_near, flat_m = gated((gt_end, et_end, f_far, gm_own, wm, e_near, flat_m))
        g_far, gt_own, em_own, sent_m = across(e_near), partner(gm_own, rest), inward(own_part(wm)), outward(flat_m)
        flat_t = edge_tiles(flags, [[wt, et_end, ft_end, gt_end]], nears, [], 0, quarter, scale)

        em_own, ft_own, flat_t, sent_m, wt = gated((em_own, ft_own, flat_t, sent_m, wt))
        et_own, sent_t = inward(own_part(wt)), outward(flat_t)
        packed = [x.astype(jnp.float32) for x in (sent_m, sent_t)]
        rows = [wm, em_end, fm, gm_end], [wt, et_end, ft_end, gt_end], [em_own, gm_own], [et_own, ft_own, gt_own]
        return *rows, [e_near, f_near, g_near], [e_far, f_far, g_far], packed

    return run


def shards_line(activations, plan):
    tokens, units = activations.shape
    top = lax.axis_size("tensor") - 1
    scale = 1.0 / math.sqrt(tokens * LINE)
    place = lax.axis_index("dp")
    low = place < 2
    first = plan[0] == top
    flags = jnp.stack([low, (place == 1) | (place == 2), first]).astype(jnp.int32)
    top_half, bottom_half = jnp.split(activations.T, 2)
    halves = [jnp.where(low, top_half, bottom_half), jnp.where(low, bottom_half, top_half)]
    other = plan[0] + plan[1] - top
    branches = [line_branch(m, top, scale) for m in range(1, top)]
    quarter = units // LINE
    ends_m, ends_t, own_m, own_t, nears, fars, packed = lax.switch(other - 1, branches, flags, *halves)
    ends = [ends_m, ends_t]
    own = [[ends_m[0], own_m[0], ends_m[2], own_m[1]], [ends_t[0], *own_t]]
    nears, fars = [halves[0], *nears], [halves[1], *fars]
    inner = outward(edge_tiles(flags, ends, nears, fars, 1, quarter, scale))
    outer = outward(edge_tiles(flags, ends, [], fars, 2, quarter, scale))
    out = middle_tiles(flags, own, nears, fars, packed, quarter, scale)
    return last_tiles(flags, out, inner.astype(jnp.float32), outer.astype(jnp.float32))


def solution(mesh):
    fast = mesh.shape["dp"] == LINE
    return jax.shard_map(
        shards_line if fast else shards_any,
        mesh=mesh,
        in_specs=(P("dp", "tensor"), P()),
        out_specs=P(None, "dp", "tensor"),
        check_vma=False,
    )
```

```python
import functools
import math

import jax
import jax.numpy as jnp
from jax import lax
from jax.experimental import pallas as pl
from jax.experimental.pallas import tpu as pltpu
from jax.sharding import PartitionSpec as P

ROUNDS = 2
LINE = 4
LANES = 128
STRIP = 104
TAIL = 16
EDGE_VMEM = 16 * 2**20
MIDDLE_VMEM = 24 * 2**20


def swapped(x, axis, apart):
    return lax.ppermute(x, axis, [(i, i ^ 1 << apart) for i in range(lax.axis_size(axis))])


def partner_panel(own, mask, width):
    current = own
    for bit in range(width):
        taken = jnp.bitwise_and(jnp.right_shift(mask, bit), 1) == 1
        current = jnp.where(taken, swapped(current, "tensor", bit), current)
    return current


def shards_any(activations, plan):
    width = lax.axis_size("tensor").bit_length() - 1
    scale = jnp.float32(1.0 / math.sqrt(activations.shape[0] * lax.axis_size("dp")))
    tiles = []
    for r in range(ROUNDS):
        other = partner_panel(activations, plan[r], width)
        tiles.append(
            lax.dot_general(other, activations, (((0,), (0,)), ((), ())), preferred_element_type=jnp.float32)
        )
    return lax.psum_scatter(jnp.stack(tiles), "dp", scatter_dimension=1, tiled=True) * scale


def inward(x):
    return lax.ppermute(x, "dp", [(0, 1), (3, 2)])


def across(x):
    return lax.ppermute(x, "dp", [(1, 2), (2, 1)])


def outward(x):
    return lax.ppermute(x, "dp", [(1, 0), (2, 3)])


def partner(x, mask):
    return lax.ppermute(x, "tensor", [(i, i ^ mask) for i in range(lax.axis_size("tensor"))])


def gated(values, *others):
    return lax.optimization_barrier((*values, *others))[: len(values)]


def strip(i):
    return pl.ds(pl.multiple_of(i * STRIP, 8), STRIP)


def times(rows, columns):
    return lax.dot_general(rows, columns, (((1,), (1,)), ((), ())), preferred_element_type=jnp.float32)


def end_start(low, quarter):
    return jnp.where(low, 0, quarter)


def own_start(low, quarter):
    return jnp.where(low, quarter, 0)


def pieces_of(units):
    near = units // 2 // LANES * LANES
    last = (units - near) // 2 // LANES * LANES
    return near, units - near - last, last


def cut(ref, start, size):
    return ref[pl.ds(pl.multiple_of(start, 16), size)]


class Columns:
    def __init__(self, low, quarter):
        self.low, self.half = low, 2 * quarter
        self.near_width, middle, self.last = pieces_of(4 * quarter)
        self.spill = self.half - self.near_width
        self.inner = middle - 2 * self.spill

    def near(self, block, n, tile):
        return cut(block, jnp.where(self.low, 0, self.spill) + n * tile, tile)

    def seam(self, near, far):
        top = far.shape[0] - self.spill if far.shape[0] < self.half else self.half - self.spill
        inward = jnp.where(self.low, cut(near, self.near_width, self.spill), cut(far, top, self.spill))
        outward = jnp.where(self.low, cut(far, 0, self.spill), cut(near, 0, self.spill))
        return jnp.concatenate([inward, outward])

    def middle(self, far):
        past = self.last if far.shape[0] == self.half else 0
        return cut(far, jnp.where(self.low, self.spill, past), self.inner)

    def outer(self, far):
        past = self.half - self.last if far.shape[0] == self.half else 0
        return cut(far, jnp.where(self.low, past, 0), self.last)


def summed(rows, starts, quarter, columns):
    total = None
    for v in range(4):
        parts = [cut(r[v], start[v], quarter) for r, start in zip(rows, starts)]
        term = times(jnp.concatenate(parts) if len(parts) > 1 else parts[0], columns(v))
        total = term if total is None else total + term
    return total


def edge_kernel(masks, mask, piece, scale, flags_ref, *refs):
    rows = [refs[4 * k : 4 * k + 4] for k in range(masks)]
    nears, fars = refs[4 * masks : -2][:4], refs[4 * masks : -2][-4:]
    out_ref, most = refs[-2:]
    height = out_ref.shape[0] - TAIL
    quarter = height // masks
    low = flags_ref[0] == 1

    @pl.when(flags_ref[1] == 1)
    def _():
        cols = Columns(low, quarter)
        at = end_start(low, quarter)
        starts = [[at, 0, at, 0], [at, quarter, 0, 0]][mask : mask + masks]
        most[...] = jnp.zeros_like(most)

        def put(place, columns):
            total = summed(rows, starts, quarter, columns)
            out_ref[:height, place] = total
            high = jnp.max(jnp.abs(total).reshape(height // 8, 8, total.shape[1]), axis=0)
            for i in range(total.shape[1] // LANES):
                most[...] = jnp.maximum(most[...], high[:, i * LANES : (i + 1) * LANES])

        if piece == 0:
            tile = 3 * LANES

            @pl.loop(0, cols.near_width // tile)
            def _(n):
                put(pl.ds(pl.multiple_of(n * tile, LANES), tile), lambda v: cols.near(nears[v], n, tile))

        elif piece == 1:
            seam = 2 * cols.spill
            put(
                pl.ds(pl.multiple_of(jnp.where(low, 0, cols.inner), LANES), seam),
                lambda v: cols.seam(nears[v], fars[v]),
            )
            put(
                pl.ds(pl.multiple_of(jnp.where(low, seam, 0), LANES), cols.inner),
                lambda v: cols.middle(fars[v]),
            )
        else:
            put(slice(None), lambda v: cols.outer(fars[v]))

        biggest = jnp.max(most[...], axis=(0, 1), keepdims=True)
        power = jnp.ceil(jnp.log2(jnp.maximum(biggest * scale, 1e-30)))
        factor = scale * jnp.exp2(14.0 - power)

        @pl.loop(0, height // STRIP)
        def _(i):
            out_ref[strip(i)] = out_ref[strip(i)] * factor

        out_ref[height:] = jnp.broadcast_to(power, (TAIL, out_ref.shape[1]))


def edge_tiles(flags, rows, nears, fars, mask, piece, quarter, scale):
    masks, tokens = len(rows), rows[0][0].shape[1]
    width = pieces_of(4 * quarter)[piece]
    operands = [*sum(rows, []), *nears, *fars]
    flat = pl.pallas_call(
        functools.partial(edge_kernel, masks, mask, piece, scale),
        out_shape=jax.ShapeDtypeStruct((masks * quarter + TAIL, width), jnp.float32),
        in_specs=[pl.BlockSpec(memory_space=pltpu.SMEM)] + [pl.BlockSpec(memory_space=pltpu.VMEM)] * len(operands),
        out_specs=pl.BlockSpec(memory_space=pltpu.VMEM),
        scratch_shapes=[pltpu.VMEM((8, LANES), jnp.float32)],
        compiler_params=pltpu.CompilerParams(vmem_limit_bytes=EDGE_VMEM),
        cost_estimate=pl.CostEstimate(
            flops=8 * masks * quarter * tokens * width,
            bytes_accessed=8 * (masks * quarter + width) * tokens,
            transcendentals=0,
        ),
        name="edge_tiles",
    )(flags, *operands)
    return flat.astype(jnp.float16)


def unpack(flat, target, rounds, columns, quarter):
    rows = flat.shape[0] - TAIL
    factor = jnp.exp2(flat[rows : rows + 1, :1] - 14.0)
    for k, place in enumerate(rounds):

        @pl.loop(0, quarter // STRIP)
        def _(i):
            target[place, strip(i), columns] = flat[strip(i + k * (quarter // STRIP))] * factor


def middle_kernel(scale, flags_ref, *refs):
    rows, nears, fars = [refs[:4], refs[4:8]], refs[8:12], refs[12:17]
    out_ref = refs[-1]
    quarter, units = out_ref.shape[1:]
    near_width, middle_width, last_width = pieces_of(units)
    low = flags_ref[0] == 1
    middle = flags_ref[1] == 1
    first = flags_ref[2]

    @pl.when(middle)
    def _():
        cols = Columns(low, quarter)
        at_own = own_start(low, quarter)
        starts = [[at_own, 0, at_own, 0], [at_own, quarter, 0, quarter]]

        def put(at, size, columns):
            total = summed(rows, starts, quarter, columns) * scale
            for k in range(2):
                place = (lax.bitwise_xor(first, k), slice(None), pl.ds(pl.multiple_of(at, LANES), size))
                out_ref[place] = total[k * quarter : (k + 1) * quarter]

        tile = 3 * LANES

        @pl.loop(0, near_width // tile)
        def _(n):
            put(jnp.where(low, 0, units - near_width) + n * tile, tile, lambda v: cols.near(nears[v], n, tile))

        seam = 2 * cols.spill
        put(near_width, seam, lambda v: cols.seam(nears[v], fars[v]))
        put(jnp.where(low, near_width + seam, last_width), cols.inner, lambda v: cols.middle(fars[v]))
        put(jnp.where(low, units - last_width, 0), last_width, lambda v: cols.outer(fars[v + v // 3]))


def middle_tiles(flags, rows, nears, fars, quarter, scale):
    tokens, units = rows[0][0].shape[1], 4 * quarter
    operands = [*sum(rows, []), *nears, *fars]
    return pl.pallas_call(
        functools.partial(middle_kernel, scale),
        out_shape=jax.ShapeDtypeStruct((2, quarter, units), jnp.float32),
        in_specs=[pl.BlockSpec(memory_space=pltpu.SMEM)] + [pl.BlockSpec(memory_space=pltpu.VMEM)] * len(operands),
        out_specs=pl.BlockSpec(memory_space=pltpu.VMEM),
        compiler_params=pltpu.CompilerParams(vmem_limit_bytes=MIDDLE_VMEM),
        cost_estimate=pl.CostEstimate(
            flops=16 * quarter * tokens * units, bytes_accessed=8 * (2 * quarter + units) * tokens, transcendentals=0
        ),
        name="middle_tiles",
    )(flags, *operands)


def place_kernel(starts, pieces, flags_ref, out_in, *refs):
    flats, (out_ref, buf, sem) = refs[:-3], refs[-3:]
    quarter, width = buf.shape[1:]
    low = flags_ref[0] == 1
    first = flags_ref[2]
    rounds = [first, 1 - first]

    def side(pair):
        return pl.multiple_of(jnp.where(low, *pair), LANES)

    @pl.when(flags_ref[1] == 0)
    def _():
        for flat, (masks, at) in zip(flats, pieces):
            unpack(flat, buf, [rounds[k] for k in masks], pl.ds(side(at), flat.shape[1]), quarter)
        copy = pltpu.make_async_copy(buf, out_ref.at[:, :, pl.ds(side(starts), width)], sem)
        copy.start()
        copy.wait()


def place_tiles(flags, out, flats, starts, pieces, width):
    return pl.pallas_call(
        functools.partial(place_kernel, starts, pieces),
        out_shape=jax.ShapeDtypeStruct(out.shape, out.dtype),
        in_specs=[
            pl.BlockSpec(memory_space=pltpu.SMEM),
            pl.BlockSpec(memory_space=pl.ANY),
            *[pl.BlockSpec(memory_space=pltpu.VMEM)] * len(flats),
        ],
        out_specs=pl.BlockSpec(memory_space=pl.ANY),
        scratch_shapes=[pltpu.VMEM((2, out.shape[1], width), jnp.float32), pltpu.SemaphoreType.DMA],
        input_output_aliases={1: 0},
        compiler_params=pltpu.CompilerParams(vmem_limit_bytes=EDGE_VMEM),
        cost_estimate=pl.CostEstimate(flops=0, bytes_accessed=6 * 832 * width, transcendentals=0),
        name="place_tiles",
    )(flags, out, *flats)


def line_branch(mask, top, scale):
    rest = top ^ mask

    def run(flags, w_near, w_far):
        quarter = w_near.shape[0] // 2
        units = 4 * quarter
        low = flags[0] == 1
        near_width, middle_width, last_width = pieces_of(units)

        def rows_of(x, start, size):
            return lax.dynamic_slice_in_dim(x, start, size, 0)

        def end_part(x):
            return rows_of(x, jnp.where(low, 0, quarter), quarter)

        def own_part(x):
            return rows_of(x, jnp.where(low, quarter, 0), quarter)

        def ends(x, y):
            return jnp.concatenate([end_part(x), end_part(y)])

        def owns(x, y):
            return jnp.concatenate([own_part(x), own_part(y)])

        f_near, e_far, wm, e_near = across(w_far), inward(w_far), partner(w_near, mask), inward(w_near)

        e_far, f_near, wm, w_near = gated((e_far, f_near, wm, w_near))
        g_near, f_far, fm, wt = across(e_far), across(w_near), partner(f_near, mask), partner(wm, rest)

        g_near, e_near, fm, wt, wm = gated((g_near, e_near, fm, wt, wm))
        gm_end, ft_end, e_ends = partner(end_part(g_near), mask), partner(end_part(fm), rest), inward(ends(wm, wt))
        gm_own = partner(own_part(g_near), mask)

        gm_end, ft_end = gated((gm_end, ft_end))
        gt_end = partner(gm_end, rest)

        gt_end, e_ends, gm_own, f_far, fm, wm, wt, e_near = gated((gt_end, e_ends, gm_own, f_far, fm, wm, wt, e_near))
        inner = 2 * quarter - last_width
        g_mid = across(rows_of(e_near, jnp.where(low, last_width, 0), inner))
        t_owns, e_owns = partner(jnp.concatenate([own_part(fm), gm_own]), rest), inward(owns(wm, wt))
        nears = [w_near, e_near, f_near, g_near]
        ends_m, ends_t = [wm, e_ends, fm, gm_end], [wt, e_ends, ft_end, gt_end]
        flat_m = edge_tiles(flags, [ends_m], nears, [], 0, 0, quarter, scale)
        sent_m = outward(flat_m)
        g_last = across(rows_of(e_near, jnp.where(low, 0, inner), last_width))
        ends_t, flat_m = gated((ends_t, flat_m))
        flat_t = edge_tiles(flags, [ends_t], nears, [], 1, 0, quarter, scale)

        g_mid, flat_t, sent_m = gated((g_mid, flat_t, sent_m))
        sent_t = outward(flat_t)
        fars = [w_far, e_far, f_far, g_mid]
        flat = edge_tiles(flags, [ends_m, ends_t], nears, fars, 0, 1, quarter, scale)
        sent = outward(flat)

        g_last, t_owns, e_owns, flat, sent_t = gated((g_last, t_owns, e_owns, flat, sent_t))
        fars = [w_far, e_far, f_far, g_last]
        last = outward(edge_tiles(flags, [ends_m, ends_t], [], fars, 0, 2, quarter, scale)).astype(jnp.float32)

        packed = [x.astype(jnp.float32) for x in (sent_m, sent_t, sent)]
        before = near_width + middle_width
        own = [[wm, e_owns, fm, gm_own], [wt, e_owns, t_owns, t_owns]]
        fars = [w_far, e_far, f_far, g_mid, g_last]
        out = middle_tiles(flags, own, nears, fars, quarter, scale)
        near_at, inner_at = (0, middle_width), (near_width, 0)
        pieces = [([0], near_at), ([1], near_at), ([0, 1], inner_at)]
        out = place_tiles(flags, out, packed, (0, last_width), pieces, before)
        return place_tiles(flags, out, [last], (before, 0), [([0, 1], (0, 0))], last_width)

    return run


def chosen(branches):
    if len(branches) == 1:
        return lambda index, *operands: branches[0](*operands)
    half = len(branches) // 2

    def run(index, *operands):
        def upper(i, *x):
            return chosen(branches[half:])(i - half, *x)

        return lax.cond(index < half, chosen(branches[:half]), upper, index, *operands)

    return run


def shards_line(activations, plan):
    tokens, units = activations.shape
    top = lax.axis_size("tensor") - 1
    scale = 1.0 / math.sqrt(tokens * LINE)
    place = lax.axis_index("dp")
    low = place < 2
    first = plan[0] == top
    flags = jnp.stack([low, (place == 1) | (place == 2), first]).astype(jnp.int32)
    top_half, bottom_half = jnp.split(activations.T, 2)
    halves = [jnp.where(low, top_half, bottom_half), jnp.where(low, bottom_half, top_half)]
    other = plan[0] + plan[1] - top
    return chosen([line_branch(m, top, scale) for m in range(1, top)])(other - 1, flags, *halves)


def solution(mesh):
    fast = mesh.shape["dp"] == LINE
    return jax.shard_map(
        shards_line if fast else shards_any,
        mesh=mesh,
        in_specs=(P("dp", "tensor"), P()),
        out_specs=P(None, "dp", "tensor"),
        check_vma=False,
    )
```

```python
import functools
import math

import jax
import jax.numpy as jnp
from jax import lax
from jax.experimental import pallas as pl
from jax.experimental.pallas import tpu as pltpu
from jax.sharding import PartitionSpec as P

ROUNDS = 2
LINE = 4
LANES = 128
STRIP = 104
TAIL = 16
EDGE_VMEM = 16 * 2**20
MIDDLE_VMEM = 24 * 2**20


def swapped(x, axis, apart):
    return lax.ppermute(x, axis, [(i, i ^ 1 << apart) for i in range(lax.axis_size(axis))])


def partner_panel(own, mask, width):
    current = own
    for bit in range(width):
        taken = jnp.bitwise_and(jnp.right_shift(mask, bit), 1) == 1
        current = jnp.where(taken, swapped(current, "tensor", bit), current)
    return current


def shards_any(activations, plan):
    width = lax.axis_size("tensor").bit_length() - 1
    scale = jnp.float32(1.0 / math.sqrt(activations.shape[0] * lax.axis_size("dp")))
    tiles = []
    for r in range(ROUNDS):
        other = partner_panel(activations, plan[r], width)
        tiles.append(
            lax.dot_general(other, activations, (((0,), (0,)), ((), ())), preferred_element_type=jnp.float32)
        )
    return lax.psum_scatter(jnp.stack(tiles), "dp", scatter_dimension=1, tiled=True) * scale


def inward(x):
    return lax.ppermute(x, "dp", [(0, 1), (3, 2)])


def across(x):
    return lax.ppermute(x, "dp", [(1, 2), (2, 1)])


def outward(x):
    return lax.ppermute(x, "dp", [(1, 0), (2, 3)])


def partner(x, mask):
    return lax.ppermute(x, "tensor", [(i, i ^ mask) for i in range(lax.axis_size("tensor"))])


def gated(values, *others):
    return lax.optimization_barrier((*values, *others))[: len(values)]


def strip(i):
    return pl.ds(pl.multiple_of(i * STRIP, 8), STRIP)


def times(rows, columns):
    return lax.dot_general(rows, columns, (((1,), (1,)), ((), ())), preferred_element_type=jnp.float32)


def end_start(low, quarter):
    return jnp.where(low, 0, quarter)


def own_start(low, quarter):
    return jnp.where(low, quarter, 0)


def pieces_of(units):
    near = units // 2 // LANES * LANES
    last = (units - near) // 2 // LANES * LANES
    return near, units - near - last, last


def cut(ref, start, size):
    return ref[pl.ds(pl.multiple_of(start, 16), size)]


class Columns:
    def __init__(self, low, quarter):
        self.low, self.half = low, 2 * quarter
        self.near_width, middle, self.last = pieces_of(4 * quarter)
        self.spill = self.half - self.near_width
        self.inner = middle - 2 * self.spill

    def near(self, block, start, size):
        return cut(block, jnp.where(self.low, 0, self.spill) + start, size)

    def seam(self, near, far):
        top = far.shape[0] - self.spill if far.shape[0] < self.half else self.half - self.spill
        inward = jnp.where(self.low, cut(near, self.near_width, self.spill), cut(far, top, self.spill))
        outward = jnp.where(self.low, cut(far, 0, self.spill), cut(near, 0, self.spill))
        return jnp.concatenate([inward, outward])

    def middle(self, far, start, size):
        past = self.last if far.shape[0] == self.half else 0
        return cut(far, jnp.where(self.low, self.spill, past) + start, size)

    def outer(self, far, start, size):
        past = self.half - self.last if far.shape[0] == self.half else 0
        return cut(far, jnp.where(self.low, past, 0) + start, size)


def joined(parts):
    return jnp.concatenate(parts) if len(parts) > 1 else parts[0]


def shares(places, total):
    done = 0
    for at, size in places:
        yield pl.ds(pl.multiple_of(at, LANES), size), size, total[:, done : done + size]
        done += size


def summed(rows, starts, quarter, columns):
    total = None
    for v in range(4):
        parts = [cut(r[v], start[v], quarter) for r, start in zip(rows, starts)]
        term = times(joined(parts), joined([c(v) for c in columns]))
        total = term if total is None else total + term
    return total


def edge_kernel(masks, mask, piece, scale, flags_ref, *refs):
    rows = [refs[4 * k : 4 * k + 4] for k in range(masks)]
    nears, fars = refs[4 * masks : -2][:4], refs[4 * masks : -2][-4:]
    out_ref, most = refs[-2:]
    height = out_ref.shape[0] - TAIL
    quarter = height // masks
    low = flags_ref[0] == 1

    @pl.when(flags_ref[1] == 1)
    def _():
        cols = Columns(low, quarter)
        at = end_start(low, quarter)
        starts = [[at, 0, 0, quarter], [at, 0, 0, 0]][mask : mask + masks]
        most[...] = jnp.zeros_like(most)

        def put(places, *columns):
            total = summed(rows, starts, quarter, columns)
            for at, size, part in shares(places, total):
                out_ref[:height, at] = part
                high = jnp.max(jnp.abs(part).reshape(height // 8, 8, size), axis=0)
                for i in range(size // LANES):
                    most[...] = jnp.maximum(most[...], high[:, i * LANES : (i + 1) * LANES])

        if piece == 0:
            for start, size in ((0, 4 * LANES), (4 * LANES, cols.near_width - 4 * LANES)):
                put([(start, size)], lambda v: cols.near(nears[v], start, size))
        elif piece == 1:
            seam = 2 * cols.spill
            put(
                [(jnp.where(low, 0, cols.inner), seam), (jnp.where(low, seam, 0), cols.inner)],
                lambda v: cols.seam(nears[v], fars[v]),
                lambda v: cols.middle(fars[v], 0, cols.inner),
            )
        else:
            put([(0, cols.last)], lambda v: cols.outer(fars[v], 0, cols.last))

        biggest = jnp.max(most[...], axis=(0, 1), keepdims=True)
        power = jnp.ceil(jnp.log2(jnp.maximum(biggest * scale, 1e-30)))
        factor = scale * jnp.exp2(14.0 - power)

        @pl.loop(0, height // STRIP)
        def _(i):
            out_ref[strip(i)] = out_ref[strip(i)] * factor

        out_ref[height:] = jnp.broadcast_to(power, (TAIL, out_ref.shape[1]))


def edge_tiles(flags, rows, nears, fars, mask, piece, quarter, scale):
    masks, tokens = len(rows), rows[0][0].shape[1]
    width = pieces_of(4 * quarter)[piece]
    operands = [*sum(rows, []), *nears, *fars]
    flat = pl.pallas_call(
        functools.partial(edge_kernel, masks, mask, piece, scale),
        out_shape=jax.ShapeDtypeStruct((masks * quarter + TAIL, width), jnp.float32),
        in_specs=[pl.BlockSpec(memory_space=pltpu.SMEM)] + [pl.BlockSpec(memory_space=pltpu.VMEM)] * len(operands),
        out_specs=pl.BlockSpec(memory_space=pltpu.VMEM),
        scratch_shapes=[pltpu.VMEM((8, LANES), jnp.float32)],
        compiler_params=pltpu.CompilerParams(vmem_limit_bytes=EDGE_VMEM),
        cost_estimate=pl.CostEstimate(
            flops=8 * masks * quarter * tokens * width,
            bytes_accessed=8 * (masks * quarter + width) * tokens,
            transcendentals=0,
        ),
        name="edge_tiles",
    )(flags, *operands)
    return flat.astype(jnp.float16)


def unpack(flat, target, rounds, columns, quarter):
    rows = flat.shape[0] - TAIL
    factor = jnp.exp2(flat[rows : rows + 1, :1] - 14.0)
    for k, place in enumerate(rounds):

        @pl.loop(0, quarter // STRIP)
        def _(i):
            target[place, strip(i), columns] = flat[strip(i + k * (quarter // STRIP))] * factor


def middle_kernel(scale, flags_ref, *refs):
    rows, nears, fars = [refs[:4], refs[4:8]], refs[8:12], refs[12:17]
    out_ref = refs[-1]
    quarter, units = out_ref.shape[1:]
    near_width, middle_width, last_width = pieces_of(units)
    low = flags_ref[0] == 1
    middle = flags_ref[1] == 1
    first = flags_ref[2]

    @pl.when(middle)
    def _():
        cols = Columns(low, quarter)
        at_own = own_start(low, quarter)
        starts = [[at_own, 0, 0, quarter], [at_own, quarter, 0, quarter]]

        def put(places, *columns):
            total = summed(rows, starts, quarter, columns) * scale
            for at, size, part in shares(places, total):
                for k in range(2):
                    out_ref[lax.bitwise_xor(first, k), :, at] = part[k * quarter : (k + 1) * quarter]

        wide, seam = 4 * LANES, 2 * cols.spill
        near_at = jnp.where(low, 0, units - near_width)
        middle_at = jnp.where(low, near_width + seam, last_width)
        last_at = jnp.where(low, units - last_width, 0)
        rest = near_width - wide
        put([(near_at, wide)], lambda v: cols.near(nears[v], 0, wide))
        put(
            [(near_at + wide, rest), (middle_at, wide - rest)],
            lambda v: cols.near(nears[v], wide, rest),
            lambda v: cols.middle(fars[v], 0, wide - rest),
        )
        left, taken = cols.inner - (wide - rest), wide - seam - (cols.inner - (wide - rest))
        put(
            [(near_width, seam), (middle_at + wide - rest, left), (last_at, taken)],
            lambda v: cols.seam(nears[v], fars[v]),
            lambda v: cols.middle(fars[v], wide - rest, left),
            lambda v: cols.outer(fars[v + v // 3], 0, taken),
        )
        put([(last_at + taken, last_width - taken)], lambda v: cols.outer(fars[v + v // 3], taken, last_width - taken))


def middle_tiles(flags, rows, nears, fars, quarter, scale):
    tokens, units = rows[0][0].shape[1], 4 * quarter
    operands = [*sum(rows, []), *nears, *fars]
    return pl.pallas_call(
        functools.partial(middle_kernel, scale),
        out_shape=jax.ShapeDtypeStruct((2, quarter, units), jnp.float32),
        in_specs=[pl.BlockSpec(memory_space=pltpu.SMEM)] + [pl.BlockSpec(memory_space=pltpu.VMEM)] * len(operands),
        out_specs=pl.BlockSpec(memory_space=pltpu.VMEM),
        compiler_params=pltpu.CompilerParams(vmem_limit_bytes=MIDDLE_VMEM),
        cost_estimate=pl.CostEstimate(
            flops=16 * quarter * tokens * units, bytes_accessed=8 * (2 * quarter + units) * tokens, transcendentals=0
        ),
        name="middle_tiles",
    )(flags, *operands)


def place_kernel(starts, pieces, flags_ref, out_in, *refs):
    flats, (out_ref, buf, sem) = refs[:-3], refs[-3:]
    quarter, width = buf.shape[1:]
    low = flags_ref[0] == 1
    first = flags_ref[2]
    rounds = [first, 1 - first]

    def side(pair):
        return pl.multiple_of(jnp.where(low, *pair), LANES)

    @pl.when(flags_ref[1] == 0)
    def _():
        for flat, (masks, at) in zip(flats, pieces):
            unpack(flat, buf, [rounds[k] for k in masks], pl.ds(side(at), flat.shape[1]), quarter)
        copy = pltpu.make_async_copy(buf, out_ref.at[:, :, pl.ds(side(starts), width)], sem)
        copy.start()
        copy.wait()


def place_tiles(flags, out, flats, starts, pieces, width):
    return pl.pallas_call(
        functools.partial(place_kernel, starts, pieces),
        out_shape=jax.ShapeDtypeStruct(out.shape, out.dtype),
        in_specs=[
            pl.BlockSpec(memory_space=pltpu.SMEM),
            pl.BlockSpec(memory_space=pl.ANY),
            *[pl.BlockSpec(memory_space=pltpu.VMEM)] * len(flats),
        ],
        out_specs=pl.BlockSpec(memory_space=pl.ANY),
        scratch_shapes=[pltpu.VMEM((2, out.shape[1], width), jnp.float32), pltpu.SemaphoreType.DMA],
        input_output_aliases={1: 0},
        compiler_params=pltpu.CompilerParams(vmem_limit_bytes=EDGE_VMEM),
        cost_estimate=pl.CostEstimate(flops=0, bytes_accessed=6 * 832 * width, transcendentals=0),
        name="place_tiles",
    )(flags, out, *flats)


def line_branch(hop, top, scale):
    rest = top ^ hop

    def run(flags, picks, w_near, w_far):
        quarter = w_near.shape[0] // 2
        low = flags[0] == 1
        near_width, middle_width, last_width = pieces_of(4 * quarter)

        def rows_of(x, start, size):
            return lax.dynamic_slice_in_dim(x, start, size, 0)

        def end_part(x):
            return rows_of(x, jnp.where(low, 0, quarter), quarter)

        def own_part(x):
            return rows_of(x, jnp.where(low, quarter, 0), quarter)

        def sibling(x, u, v):
            return partner(jnp.where(picks[0] == 1, x, jnp.where(picks[1] == 1, v, u)), 1)

        def masked(u, swapped_in):
            return jnp.where(picks[2] == 1, u, swapped_in)

        f_near, e_far, wu, e_near = across(w_far), inward(w_far), partner(w_near, hop), inward(w_near)

        e_far, f_near, wu, w_near = gated((e_far, f_near, wu, w_near))
        g_near, f_far, fu, wv = across(e_far), across(w_near), partner(f_near, hop), partner(wu, rest)

        g_near, e_near, fu, wv, wu = gated((g_near, e_near, fu, wv, wu))
        gu_end, fv_end, ev_end = partner(end_part(g_near), hop), partner(end_part(fu), rest), inward(end_part(wv))
        w_swap = sibling(w_near, wu, wv)

        gu_end, fv_end, ev_end, w_swap, g_near = gated((gu_end, fv_end, ev_end, w_swap, g_near))
        wm = masked(wu, w_swap)
        gv_end, gu_own, em_end = partner(gu_end, rest), partner(own_part(g_near), hop), inward(end_part(wm))

        gv_end, gu_own, em_end, f_far, fu, e_near = gated((gv_end, gu_own, em_end, f_far, fu, e_near))
        inner = 2 * quarter - last_width
        u_ends, u_owns = [jnp.concatenate(x) for x in ([end_part(fu), gu_end], [own_part(fu), gu_own])]
        x_ends, x_owns = [jnp.concatenate([part(f_near), part(g_near)]) for part in (end_part, own_part)]
        swap_ends = sibling(x_ends, u_ends, jnp.concatenate([fv_end, gv_end]))
        g_mid = across(rows_of(e_near, jnp.where(low, last_width, 0), inner))
        v_owns, e_owns = partner(u_owns, rest), inward(jnp.concatenate([own_part(wm), own_part(wv)]))
        nears = [w_near, e_near, f_near, g_near]
        ends_v = [wv, ev_end, fv_end, gv_end]
        flat_v = edge_tiles(flags, [ends_v], nears, [], 1, 0, quarter, scale)
        sent_v = outward(flat_v)

        swap_ends, flat_v = gated((swap_ends, flat_v))
        m_ends = masked(u_ends, swap_ends)
        g_last = across(rows_of(e_near, jnp.where(low, 0, inner), last_width))
        ends_m = [wm, em_end, m_ends, m_ends]
        flat_m = edge_tiles(flags, [ends_m], nears, [], 0, 0, quarter, scale)

        g_mid, flat_m, sent_v = gated((g_mid, flat_m, sent_v))
        sent_m = outward(flat_m)
        fars = [w_far, e_far, f_far, g_mid]
        flat = edge_tiles(flags, [ends_m, ends_v], nears, fars, 0, 1, quarter, scale)
        sent = outward(flat)

        g_last, v_owns, e_owns, flat, sent_m = gated((g_last, v_owns, e_owns, flat, sent_m))
        swap_owns = sibling(x_owns, u_owns, v_owns)
        fars = [w_far, e_far, f_far, g_last]
        last = outward(edge_tiles(flags, [ends_m, ends_v], [], fars, 0, 2, quarter, scale)).astype(jnp.float32)
        m_owns = masked(u_owns, swap_owns)

        packed = [x.astype(jnp.float32) for x in (sent_m, sent_v, sent)]
        before = near_width + middle_width
        own = [[wm, e_owns, m_owns, m_owns], [wv, e_owns, v_owns, v_owns]]
        fars = [w_far, e_far, f_far, g_mid, g_last]
        out = middle_tiles(flags, own, nears, fars, quarter, scale)
        near_at, inner_at = (0, middle_width), (near_width, 0)
        pieces = [([0], near_at), ([1], near_at), ([0, 1], inner_at)]
        out = place_tiles(flags, out, packed, (0, last_width), pieces, before)
        return place_tiles(flags, out, [last], (before, 0), [([0, 1], (0, 0))], last_width)

    return run


def shards_line(activations, plan):
    tokens, units = activations.shape
    top = lax.axis_size("tensor") - 1
    scale = 1.0 / math.sqrt(tokens * LINE)
    place = lax.axis_index("dp")
    low = place < 2
    first = plan[0] == top
    flags = jnp.stack([low, (place == 1) | (place == 2), first]).astype(jnp.int32)
    top_half, bottom_half = jnp.split(activations.T, 2)
    halves = [jnp.where(low, top_half, bottom_half), jnp.where(low, bottom_half, top_half)]
    mask = plan[0] + plan[1] - top
    high = (mask >> 1) == 2
    hop = jnp.where(high, 4, 2)
    picks = jnp.stack([mask == 1, mask == (top ^ 1), mask == hop]).astype(jnp.int32)
    return lax.cond(high, line_branch(4, top, scale), line_branch(2, top, scale), flags, picks, *halves)


def solution(mesh):
    fast = mesh.shape["dp"] == LINE and mesh.shape["tensor"] == 8
    return jax.shard_map(
        shards_line if fast else shards_any,
        mesh=mesh,
        in_specs=(P("dp", "tensor"), P()),
        out_specs=P(None, "dp", "tensor"),
        check_vma=False,
    )
```

```python
import functools
import math

import jax
import jax.numpy as jnp
from jax import lax
from jax.experimental import pallas as pl
from jax.experimental.pallas import tpu as pltpu
from jax.sharding import PartitionSpec as P

ROUNDS = 2
LINE = 4
LANES = 128
STRIP = 104
TAIL = 16
EDGE_VMEM = 16 * 2**20
MIDDLE_VMEM = 24 * 2**20


def swapped(x, axis, apart):
    return lax.ppermute(x, axis, [(i, i ^ 1 << apart) for i in range(lax.axis_size(axis))])


def partner_panel(own, mask, width):
    current = own
    for bit in range(width):
        taken = jnp.bitwise_and(jnp.right_shift(mask, bit), 1) == 1
        current = jnp.where(taken, swapped(current, "tensor", bit), current)
    return current


def shards_any(activations, plan):
    width = lax.axis_size("tensor").bit_length() - 1
    scale = jnp.float32(1.0 / math.sqrt(activations.shape[0] * lax.axis_size("dp")))
    tiles = []
    for r in range(ROUNDS):
        other = partner_panel(activations, plan[r], width)
        tiles.append(
            lax.dot_general(other, activations, (((0,), (0,)), ((), ())), preferred_element_type=jnp.float32)
        )
    return lax.psum_scatter(jnp.stack(tiles), "dp", scatter_dimension=1, tiled=True) * scale


def inward(x):
    return lax.ppermute(x, "dp", [(0, 1), (3, 2)])


def across(x):
    return lax.ppermute(x, "dp", [(1, 2), (2, 1)])


def outward(x):
    return lax.ppermute(x, "dp", [(1, 0), (2, 3)])


def partner(x, mask):
    return lax.ppermute(x, "tensor", [(i, i ^ mask) for i in range(lax.axis_size("tensor"))])


def gated(values, *others):
    return lax.optimization_barrier((*values, *others))[: len(values)]


def strip(i):
    return pl.ds(pl.multiple_of(i * STRIP, 8), STRIP)


def times(rows, columns):
    return lax.dot_general(rows, columns, (((1,), (1,)), ((), ())), preferred_element_type=jnp.float32)


def end_start(low, quarter):
    return jnp.where(low, 0, quarter)


def own_start(low, quarter):
    return jnp.where(low, quarter, 0)


def pieces_of(units):
    near = units // 2 // LANES * LANES
    last = (units - near) // 2 // LANES * LANES
    return near, units - near - last, last


def cut(ref, start, size):
    return ref[pl.ds(pl.multiple_of(start, 16), size)]


class Columns:
    def __init__(self, low, quarter):
        self.low, self.half = low, 2 * quarter
        self.near_width, middle, self.last = pieces_of(4 * quarter)
        self.spill = self.half - self.near_width
        self.inner = middle - 2 * self.spill

    def near(self, block, start, size):
        return cut(block, jnp.where(self.low, 0, self.spill) + start, size)

    def seam(self, near, far):
        top = far.shape[0] - self.spill if far.shape[0] < self.half else self.half - self.spill
        inward = jnp.where(self.low, cut(near, self.near_width, self.spill), cut(far, top, self.spill))
        outward = jnp.where(self.low, cut(far, 0, self.spill), cut(near, 0, self.spill))
        return jnp.concatenate([inward, outward])

    def middle(self, far, start, size):
        past = self.last if far.shape[0] == self.half else 0
        return cut(far, jnp.where(self.low, self.spill, past) + start, size)

    def outer(self, far, start, size):
        past = self.half - self.last if far.shape[0] == self.half else 0
        return cut(far, jnp.where(self.low, past, 0) + start, size)


def joined(parts):
    return jnp.concatenate(parts) if len(parts) > 1 else parts[0]


def shares(places, total):
    done = 0
    for at, size in places:
        yield pl.ds(pl.multiple_of(at, LANES), size), size, total[:, done : done + size]
        done += size


def summed(rows, starts, quarter, columns):
    total = None
    for v in range(4):
        parts = [cut(r[v], start[v], quarter) for r, start in zip(rows, starts)]
        term = times(joined(parts), joined([c(v) for c in columns]))
        total = term if total is None else total + term
    return total


def edge_kernel(masks, mask, piece, scale, flags_ref, *refs):
    rows = [refs[4 * k : 4 * k + 4] for k in range(masks)]
    nears, fars = refs[4 * masks : -2][:4], refs[4 * masks : -2][-4:]
    out_ref, most = refs[-2:]
    height = out_ref.shape[0] - TAIL
    quarter = height // masks
    low = flags_ref[0] == 1

    @pl.when(flags_ref[1] == 1)
    def _():
        cols = Columns(low, quarter)
        at = end_start(low, quarter)
        starts = [[at, 0, 0, quarter], [at, 0, 0, 0]][mask : mask + masks]
        most[...] = jnp.zeros_like(most)

        def put(places, *columns):
            total = summed(rows, starts, quarter, columns)
            for at, size, part in shares(places, total):
                out_ref[:height, at] = part
                high = jnp.max(jnp.abs(part).reshape(height // 8, 8, size), axis=0)
                for i in range(size // LANES):
                    most[...] = jnp.maximum(most[...], high[:, i * LANES : (i + 1) * LANES])

        if piece == 0:
            for start, size in ((0, 4 * LANES), (4 * LANES, cols.near_width - 4 * LANES)):
                put([(start, size)], lambda v: cols.near(nears[v], start, size))
        elif piece == 1:
            seam = 2 * cols.spill
            put(
                [(jnp.where(low, 0, cols.inner), seam), (jnp.where(low, seam, 0), cols.inner)],
                lambda v: cols.seam(nears[v], fars[v]),
                lambda v: cols.middle(fars[v], 0, cols.inner),
            )
        else:
            put([(0, cols.last)], lambda v: cols.outer(fars[v], 0, cols.last))

        biggest = jnp.max(most[...], axis=(0, 1), keepdims=True)
        power = jnp.ceil(jnp.log2(jnp.maximum(biggest * scale, 1e-30)))
        factor = scale * jnp.exp2(14.0 - power)

        @pl.loop(0, height // STRIP)
        def _(i):
            out_ref[strip(i)] = out_ref[strip(i)] * factor

        out_ref[height:] = jnp.broadcast_to(power, (TAIL, out_ref.shape[1]))


def edge_tiles(flags, rows, nears, fars, mask, piece, quarter, scale):
    masks, tokens = len(rows), rows[0][0].shape[1]
    width = pieces_of(4 * quarter)[piece]
    operands = [*sum(rows, []), *nears, *fars]
    flat = pl.pallas_call(
        functools.partial(edge_kernel, masks, mask, piece, scale),
        out_shape=jax.ShapeDtypeStruct((masks * quarter + TAIL, width), jnp.float32),
        in_specs=[pl.BlockSpec(memory_space=pltpu.SMEM)] + [pl.BlockSpec(memory_space=pltpu.VMEM)] * len(operands),
        out_specs=pl.BlockSpec(memory_space=pltpu.VMEM),
        scratch_shapes=[pltpu.VMEM((8, LANES), jnp.float32)],
        compiler_params=pltpu.CompilerParams(vmem_limit_bytes=EDGE_VMEM),
        cost_estimate=pl.CostEstimate(
            flops=8 * masks * quarter * tokens * width,
            bytes_accessed=8 * (masks * quarter + width) * tokens,
            transcendentals=0,
        ),
        name="edge_tiles",
    )(flags, *operands)
    return flat.astype(jnp.float16)


def unpack(flat, target, rounds, columns, quarter):
    rows = flat.shape[0] - TAIL
    factor = jnp.exp2(flat[rows : rows + 1, :1] - 14.0)
    for k, place in enumerate(rounds):

        @pl.loop(0, quarter // STRIP)
        def _(i):
            target[place, strip(i), columns] = flat[strip(i + k * (quarter // STRIP))] * factor


def middle_kernel(scale, flags_ref, *refs):
    rows, nears, fars, packed = [refs[:4], refs[4:8]], refs[8:12], refs[12:17], refs[17:19]
    out_ref = refs[-1]
    quarter, units = out_ref.shape[1:]
    near_width, middle_width, last_width = pieces_of(units)
    low = flags_ref[0] == 1
    middle = flags_ref[1] == 1
    first = flags_ref[2]

    @pl.when(middle)
    def _():
        cols = Columns(low, quarter)
        at_own = own_start(low, quarter)
        starts = [[at_own, 0, 0, quarter], [at_own, quarter, 0, quarter]]

        def put(places, *columns):
            total = summed(rows, starts, quarter, columns) * scale
            for at, size, part in shares(places, total):
                for k in range(2):
                    out_ref[lax.bitwise_xor(first, k), :, at] = part[k * quarter : (k + 1) * quarter]

        wide, seam = 4 * LANES, 2 * cols.spill
        near_at = jnp.where(low, 0, units - near_width)
        middle_at = jnp.where(low, near_width + seam, last_width)
        last_at = jnp.where(low, units - last_width, 0)
        rest = near_width - wide
        put([(near_at, wide)], lambda v: cols.near(nears[v], 0, wide))
        put(
            [(near_at + wide, rest), (middle_at, wide - rest)],
            lambda v: cols.near(nears[v], wide, rest),
            lambda v: cols.middle(fars[v], 0, wide - rest),
        )
        left, taken = cols.inner - (wide - rest), wide - seam - (cols.inner - (wide - rest))
        put(
            [(near_width, seam), (middle_at + wide - rest, left), (last_at, taken)],
            lambda v: cols.seam(nears[v], fars[v]),
            lambda v: cols.middle(fars[v], wide - rest, left),
            lambda v: cols.outer(fars[v + v // 3], 0, taken),
        )
        put([(last_at + taken, last_width - taken)], lambda v: cols.outer(fars[v + v // 3], taken, last_width - taken))

    @pl.when(jnp.logical_not(middle))
    def _():
        near = pl.ds(pl.multiple_of(jnp.where(low, 0, units - near_width), LANES), near_width)
        unpack(packed[0], out_ref, [first], near, quarter)
        unpack(packed[1], out_ref, [1 - first], near, quarter)


def middle_tiles(flags, rows, nears, fars, packed, quarter, scale):
    tokens, units = rows[0][0].shape[1], 4 * quarter
    operands = [*sum(rows, []), *nears, *fars, *packed]
    return pl.pallas_call(
        functools.partial(middle_kernel, scale),
        out_shape=jax.ShapeDtypeStruct((2, quarter, units), jnp.float32),
        in_specs=[pl.BlockSpec(memory_space=pltpu.SMEM)] + [pl.BlockSpec(memory_space=pltpu.VMEM)] * len(operands),
        out_specs=pl.BlockSpec(memory_space=pltpu.VMEM),
        compiler_params=pltpu.CompilerParams(vmem_limit_bytes=MIDDLE_VMEM),
        cost_estimate=pl.CostEstimate(
            flops=16 * quarter * tokens * units, bytes_accessed=8 * (2 * quarter + units) * tokens, transcendentals=0
        ),
        name="middle_tiles",
    )(flags, *operands)


def place_kernel(starts, pieces, flags_ref, out_in, *refs):
    flats, (out_ref, buf, sem) = refs[:-3], refs[-3:]
    quarter, width = buf.shape[1:]
    low = flags_ref[0] == 1
    first = flags_ref[2]
    rounds = [first, 1 - first]

    def side(pair):
        return pl.multiple_of(jnp.where(low, *pair), LANES)

    @pl.when(flags_ref[1] == 0)
    def _():
        for flat, (masks, at) in zip(flats, pieces):
            unpack(flat, buf, [rounds[k] for k in masks], pl.ds(side(at), flat.shape[1]), quarter)
        copy = pltpu.make_async_copy(buf, out_ref.at[:, :, pl.ds(side(starts), width)], sem)
        copy.start()
        copy.wait()


def place_tiles(flags, out, flats, starts, pieces, width):
    return pl.pallas_call(
        functools.partial(place_kernel, starts, pieces),
        out_shape=jax.ShapeDtypeStruct(out.shape, out.dtype),
        in_specs=[
            pl.BlockSpec(memory_space=pltpu.SMEM),
            pl.BlockSpec(memory_space=pl.ANY),
            *[pl.BlockSpec(memory_space=pltpu.VMEM)] * len(flats),
        ],
        out_specs=pl.BlockSpec(memory_space=pl.ANY),
        scratch_shapes=[pltpu.VMEM((2, out.shape[1], width), jnp.float32), pltpu.SemaphoreType.DMA],
        input_output_aliases={1: 0},
        compiler_params=pltpu.CompilerParams(vmem_limit_bytes=EDGE_VMEM),
        cost_estimate=pl.CostEstimate(flops=0, bytes_accessed=6 * 832 * width, transcendentals=0),
        name="place_tiles",
    )(flags, out, *flats)


def line_branch(hop, top, scale):
    rest = top ^ hop

    def run(flags, picks, w_near, w_far):
        quarter = w_near.shape[0] // 2
        low = flags[0] == 1
        near_width, middle_width, last_width = pieces_of(4 * quarter)

        def rows_of(x, start, size):
            return lax.dynamic_slice_in_dim(x, start, size, 0)

        def end_part(x):
            return rows_of(x, jnp.where(low, 0, quarter), quarter)

        def own_part(x):
            return rows_of(x, jnp.where(low, quarter, 0), quarter)

        def sibling(x, u, v):
            return partner(jnp.where(picks[0] == 1, x, jnp.where(picks[1] == 1, v, u)), 1)

        def masked(u, swapped_in):
            return jnp.where(picks[2] == 1, u, swapped_in)

        f_near, e_far, wu, e_near = across(w_far), inward(w_far), partner(w_near, hop), inward(w_near)

        e_far, f_near, wu, w_near = gated((e_far, f_near, wu, w_near))
        g_near, f_far, fu, wv = across(e_far), across(w_near), partner(f_near, hop), partner(wu, rest)

        g_near, e_near, fu, wv, wu = gated((g_near, e_near, fu, wv, wu))
        gu_end, fv_end, ev_end = partner(end_part(g_near), hop), partner(end_part(fu), rest), inward(end_part(wv))
        w_swap = sibling(w_near, wu, wv)

        gu_end, fv_end, ev_end, w_swap, g_near = gated((gu_end, fv_end, ev_end, w_swap, g_near))
        wm = masked(wu, w_swap)
        gv_end, gu_own, em_end = partner(gu_end, rest), partner(own_part(g_near), hop), inward(end_part(wm))

        gv_end, gu_own, em_end, f_far, fu, e_near = gated((gv_end, gu_own, em_end, f_far, fu, e_near))
        inner = 2 * quarter - last_width
        u_ends, u_owns = [jnp.concatenate(x) for x in ([end_part(fu), gu_end], [own_part(fu), gu_own])]
        x_ends, x_owns = [jnp.concatenate([part(f_near), part(g_near)]) for part in (end_part, own_part)]
        swap_ends = sibling(x_ends, u_ends, jnp.concatenate([fv_end, gv_end]))
        g_mid = across(rows_of(e_near, jnp.where(low, last_width, 0), inner))
        v_owns, e_owns = partner(u_owns, rest), inward(jnp.concatenate([own_part(wm), own_part(wv)]))
        nears = [w_near, e_near, f_near, g_near]
        ends_v = [wv, ev_end, fv_end, gv_end]
        flat_v = edge_tiles(flags, [ends_v], nears, [], 1, 0, quarter, scale)
        sent_v = outward(flat_v)

        swap_ends, flat_v = gated((swap_ends, flat_v))
        m_ends = masked(u_ends, swap_ends)
        g_last = across(rows_of(e_near, jnp.where(low, 0, inner), last_width))
        ends_m = [wm, em_end, m_ends, m_ends]
        flat_m = edge_tiles(flags, [ends_m], nears, [], 0, 0, quarter, scale)

        g_mid, flat_m, sent_v = gated((g_mid, flat_m, sent_v))
        sent_m = outward(flat_m)
        fars = [w_far, e_far, f_far, g_mid]
        flat = edge_tiles(flags, [ends_m, ends_v], nears, fars, 0, 1, quarter, scale)
        sent = outward(flat)

        g_last, v_owns, e_owns, flat, sent_m = gated((g_last, v_owns, e_owns, flat, sent_m))
        fars = [w_far, e_far, f_far, g_last]
        last = outward(edge_tiles(flags, [ends_m, ends_v], [], fars, 0, 2, quarter, scale))
        swap_owns = sibling(x_owns, u_owns, v_owns)
        m_owns = masked(u_owns, swap_owns)

        packed = [x.astype(jnp.float32) for x in (sent_m, sent_v)]
        own = [[wm, e_owns, m_owns, m_owns], [wv, e_owns, v_owns, v_owns]]
        fars = [w_far, e_far, f_far, g_mid, g_last]
        out = middle_tiles(flags, own, nears, fars, packed, quarter, scale)
        out, sent, last = gated((out, sent, last))
        pieces = [([0, 1], (0, last_width)), ([0, 1], (middle_width, 0))]
        return place_tiles(
            flags, out, [sent.astype(jnp.float32), last.astype(jnp.float32)], (near_width, 0), pieces, middle_width + last_width
        )

    return run


def shards_line(activations, plan):
    tokens, units = activations.shape
    top = lax.axis_size("tensor") - 1
    scale = 1.0 / math.sqrt(tokens * LINE)
    place = lax.axis_index("dp")
    low = place < 2
    first = plan[0] == top
    flags = jnp.stack([low, (place == 1) | (place == 2), first]).astype(jnp.int32)
    top_half, bottom_half = jnp.split(activations.T, 2)
    halves = [jnp.where(low, top_half, bottom_half), jnp.where(low, bottom_half, top_half)]
    mask = plan[0] + plan[1] - top
    high = (mask >> 1) == 2
    hop = jnp.where(high, 4, 2)
    picks = jnp.stack([mask == 1, mask == (top ^ 1), mask == hop]).astype(jnp.int32)
    return lax.cond(high, line_branch(4, top, scale), line_branch(2, top, scale), flags, picks, *halves)


def solution(mesh):
    fast = mesh.shape["dp"] == LINE and mesh.shape["tensor"] == 8
    return jax.shard_map(
        shards_line if fast else shards_any,
        mesh=mesh,
        in_specs=(P("dp", "tensor"), P()),
        out_specs=P(None, "dp", "tensor"),
        check_vma=False,
    )
```

```python
import functools
import math

import jax
import jax.numpy as jnp
from jax import lax
from jax.experimental import pallas as pl
from jax.experimental.pallas import tpu as pltpu
from jax.sharding import PartitionSpec as P

ROUNDS = 2
LINE = 4
LANES = 128
STRIP = 104
TAIL = 16
EDGE_VMEM = 16 * 2**20
MIDDLE_VMEM = 24 * 2**20


def swapped(x, axis, apart):
    return lax.ppermute(x, axis, [(i, i ^ 1 << apart) for i in range(lax.axis_size(axis))])


def partner_panel(own, mask, width):
    current = own
    for bit in range(width):
        taken = jnp.bitwise_and(jnp.right_shift(mask, bit), 1) == 1
        current = jnp.where(taken, swapped(current, "tensor", bit), current)
    return current


def shards_any(activations, plan):
    width = lax.axis_size("tensor").bit_length() - 1
    scale = jnp.float32(1.0 / math.sqrt(activations.shape[0] * lax.axis_size("dp")))
    tiles = []
    for r in range(ROUNDS):
        other = partner_panel(activations, plan[r], width)
        tiles.append(
            lax.dot_general(other, activations, (((0,), (0,)), ((), ())), preferred_element_type=jnp.float32)
        )
    return lax.psum_scatter(jnp.stack(tiles), "dp", scatter_dimension=1, tiled=True) * scale


def inward(x):
    return lax.ppermute(x, "dp", [(0, 1), (3, 2)])


def across(x):
    return lax.ppermute(x, "dp", [(1, 2), (2, 1)])


def outward(x):
    return lax.ppermute(x, "dp", [(1, 0), (2, 3)])


def partner(x, mask):
    return lax.ppermute(x, "tensor", [(i, i ^ mask) for i in range(lax.axis_size("tensor"))])


def gated(values, *others):
    return lax.optimization_barrier((*values, *others))[: len(values)]


def strip(i):
    return pl.ds(pl.multiple_of(i * STRIP, 8), STRIP)


def times(rows, columns):
    return lax.dot_general(rows, columns, (((1,), (1,)), ((), ())), preferred_element_type=jnp.float32)


def pieces_of(units):
    near = units // 2 // LANES * LANES
    last = (units - near) // 2 // LANES * LANES
    return near, units - near - last, last


def cut(ref, start, size):
    return ref[pl.ds(pl.multiple_of(start, 16), size)]


class Columns:
    def __init__(self, low, quarter):
        self.low, self.half = low, 2 * quarter
        self.near_width, middle, self.last = pieces_of(4 * quarter)
        self.spill = self.half - self.near_width
        self.inner = middle - 2 * self.spill

    def near(self, block, start, size):
        return cut(block, jnp.where(self.low, 0, self.spill) + start, size)

    def seam(self, near, far):
        top = far.shape[0] - self.spill if far.shape[0] < self.half else self.half - self.spill
        inward = jnp.where(self.low, cut(near, self.near_width, self.spill), cut(far, top, self.spill))
        outward = jnp.where(self.low, cut(far, 0, self.spill), cut(near, 0, self.spill))
        return jnp.concatenate([inward, outward])

    def middle(self, far, start, size):
        past = self.last if far.shape[0] == self.half else 0
        return cut(far, jnp.where(self.low, self.spill, past) + start, size)

    def outer(self, far, start, size):
        past = self.half - self.last if far.shape[0] == self.half else 0
        return cut(far, jnp.where(self.low, past, 0) + start, size)


def joined(parts):
    return jnp.concatenate(parts) if len(parts) > 1 else parts[0]


def shares(places, total):
    done = 0
    for at, size in places:
        yield pl.ds(pl.multiple_of(at, LANES), size), size, total[:, done : done + size]
        done += size


def summed(rows, starts, quarter, columns):
    total = None
    for v in range(4):
        parts = [cut(r[v], start[v], quarter) for r, start in zip(rows, starts)]
        term = times(joined(parts), joined([c(v) for c in columns]))
        total = term if total is None else total + term
    return total


def edge_kernel(masks, mask, piece, scale, flags_ref, *refs):
    rows = [refs[4 * k : 4 * k + 4] for k in range(masks)]
    nears, fars = refs[4 * masks : -2][:4], refs[4 * masks : -2][-4:]
    out_ref, most = refs[-2:]
    height = out_ref.shape[0] - TAIL
    quarter = height // masks
    low = flags_ref[0] == 1

    @pl.when(flags_ref[1] == 1)
    def _():
        cols = Columns(low, quarter)
        starts = [[0, 0, 0, quarter], [0, 0, 0, 0]][mask : mask + masks]
        most[...] = jnp.zeros_like(most)

        def put(places, *columns):
            total = summed(rows, starts, quarter, columns)
            for at, size, part in shares(places, total):
                out_ref[:height, at] = part
                high = jnp.max(jnp.abs(part).reshape(height // 8, 8, size), axis=0)
                for i in range(size // LANES):
                    most[...] = jnp.maximum(most[...], high[:, i * LANES : (i + 1) * LANES])

        if piece == 0:
            for start, size in ((0, 4 * LANES), (4 * LANES, cols.near_width - 4 * LANES)):
                put([(start, size)], lambda v: cols.near(nears[v], start, size))
        elif piece == 1:
            seam = 2 * cols.spill
            put(
                [(jnp.where(low, 0, cols.inner), seam), (jnp.where(low, seam, 0), cols.inner)],
                lambda v: cols.seam(nears[v], fars[v]),
                lambda v: cols.middle(fars[v], 0, cols.inner),
            )
        else:
            put([(0, cols.last)], lambda v: cols.outer(fars[v], 0, cols.last))

        biggest = jnp.max(most[...], axis=(0, 1), keepdims=True)
        power = jnp.ceil(jnp.log2(jnp.maximum(biggest * scale, 1e-30)))
        factor = scale * jnp.exp2(14.0 - power)

        @pl.loop(0, height // STRIP)
        def _(i):
            out_ref[strip(i)] = out_ref[strip(i)] * factor

        out_ref[height:] = jnp.broadcast_to(power, (TAIL, out_ref.shape[1]))


def edge_tiles(flags, rows, nears, fars, mask, piece, quarter, scale):
    masks, tokens = len(rows), rows[0][0].shape[1]
    width = pieces_of(4 * quarter)[piece]
    operands = [*sum(rows, []), *nears, *fars]
    flat = pl.pallas_call(
        functools.partial(edge_kernel, masks, mask, piece, scale),
        out_shape=jax.ShapeDtypeStruct((masks * quarter + TAIL, width), jnp.float32),
        in_specs=[pl.BlockSpec(memory_space=pltpu.SMEM)] + [pl.BlockSpec(memory_space=pltpu.VMEM)] * len(operands),
        out_specs=pl.BlockSpec(memory_space=pltpu.VMEM),
        scratch_shapes=[pltpu.VMEM((8, LANES), jnp.float32)],
        compiler_params=pltpu.CompilerParams(vmem_limit_bytes=EDGE_VMEM),
        cost_estimate=pl.CostEstimate(
            flops=8 * masks * quarter * tokens * width,
            bytes_accessed=8 * (masks * quarter + width) * tokens,
            transcendentals=0,
        ),
        name="edge_tiles",
    )(flags, *operands)
    return flat.astype(jnp.float16)


def unpack(flat, target, rounds, columns, quarter):
    rows = flat.shape[0] - TAIL
    factor = jnp.exp2(flat[rows : rows + 1, :1] - 14.0)
    for k, place in enumerate(rounds):

        @pl.loop(0, quarter // STRIP)
        def _(i):
            target[place, strip(i), columns] = flat[strip(i + k * (quarter // STRIP))] * factor


def middle_kernel(scale, flags_ref, *refs):
    rows, nears, fars, packed = [refs[:4], refs[4:8]], refs[8:12], refs[12:17], refs[17:19]
    out_ref = refs[-1]
    quarter, units = out_ref.shape[1:]
    near_width, middle_width, last_width = pieces_of(units)
    low = flags_ref[0] == 1
    middle = flags_ref[1] == 1
    first = flags_ref[2]

    @pl.when(middle)
    def _():
        cols = Columns(low, quarter)
        starts = [[quarter, 0, 0, quarter], [0, quarter, 0, quarter]]

        def put(places, *columns):
            total = summed(rows, starts, quarter, columns) * scale
            for at, size, part in shares(places, total):
                for k in range(2):
                    out_ref[lax.bitwise_xor(first, k), :, at] = part[k * quarter : (k + 1) * quarter]

        wide, seam = 4 * LANES, 2 * cols.spill
        near_at = jnp.where(low, 0, units - near_width)
        middle_at = jnp.where(low, near_width + seam, last_width)
        last_at = jnp.where(low, units - last_width, 0)
        rest = near_width - wide
        put([(near_at, wide)], lambda v: cols.near(nears[v], 0, wide))
        put(
            [(near_at + wide, rest), (middle_at, wide - rest)],
            lambda v: cols.near(nears[v], wide, rest),
            lambda v: cols.middle(fars[v], 0, wide - rest),
        )
        left, taken = cols.inner - (wide - rest), wide - seam - (cols.inner - (wide - rest))
        put(
            [(near_width, seam), (middle_at + wide - rest, left), (last_at, taken)],
            lambda v: cols.seam(nears[v], fars[v]),
            lambda v: cols.middle(fars[v], wide - rest, left),
            lambda v: cols.outer(fars[v + v // 3], 0, taken),
        )
        put([(last_at + taken, last_width - taken)], lambda v: cols.outer(fars[v + v // 3], taken, last_width - taken))

    @pl.when(jnp.logical_not(middle))
    def _():
        near = pl.ds(pl.multiple_of(jnp.where(low, 0, units - near_width), LANES), near_width)
        unpack(packed[0], out_ref, [first], near, quarter)
        unpack(packed[1], out_ref, [1 - first], near, quarter)


def middle_tiles(flags, rows, nears, fars, packed, quarter, scale):
    tokens, units = rows[0][0].shape[1], 4 * quarter
    operands = [*sum(rows, []), *nears, *fars, *packed]
    return pl.pallas_call(
        functools.partial(middle_kernel, scale),
        out_shape=jax.ShapeDtypeStruct((2, quarter, units), jnp.float32),
        in_specs=[pl.BlockSpec(memory_space=pltpu.SMEM)] + [pl.BlockSpec(memory_space=pltpu.VMEM)] * len(operands),
        out_specs=pl.BlockSpec(memory_space=pltpu.VMEM),
        compiler_params=pltpu.CompilerParams(vmem_limit_bytes=MIDDLE_VMEM),
        cost_estimate=pl.CostEstimate(
            flops=16 * quarter * tokens * units, bytes_accessed=8 * (2 * quarter + units) * tokens, transcendentals=0
        ),
        name="middle_tiles",
    )(flags, *operands)


def place_kernel(starts, pieces, flags_ref, out_in, *refs):
    flats, (out_ref, buf, sem) = refs[:-3], refs[-3:]
    quarter, width = buf.shape[1:]
    low = flags_ref[0] == 1
    first = flags_ref[2]
    rounds = [first, 1 - first]

    def side(pair):
        return pl.multiple_of(jnp.where(low, *pair), LANES)

    @pl.when(flags_ref[1] == 0)
    def _():
        for flat, (masks, at) in zip(flats, pieces):
            unpack(flat, buf, [rounds[k] for k in masks], pl.ds(side(at), flat.shape[1]), quarter)
        copy = pltpu.make_async_copy(buf, out_ref.at[:, :, pl.ds(side(starts), width)], sem)
        copy.start()
        copy.wait()


def place_tiles(flags, out, flats, starts, pieces, width):
    return pl.pallas_call(
        functools.partial(place_kernel, starts, pieces),
        out_shape=jax.ShapeDtypeStruct(out.shape, out.dtype),
        in_specs=[
            pl.BlockSpec(memory_space=pltpu.SMEM),
            pl.BlockSpec(memory_space=pl.ANY),
            *[pl.BlockSpec(memory_space=pltpu.VMEM)] * len(flats),
        ],
        out_specs=pl.BlockSpec(memory_space=pl.ANY),
        scratch_shapes=[pltpu.VMEM((2, out.shape[1], width), jnp.float32), pltpu.SemaphoreType.DMA],
        input_output_aliases={1: 0},
        compiler_params=pltpu.CompilerParams(vmem_limit_bytes=EDGE_VMEM),
        cost_estimate=pl.CostEstimate(flops=0, bytes_accessed=6 * 832 * width, transcendentals=0),
        name="place_tiles",
    )(flags, out, *flats)


def line_branch(hop, top, scale):
    rest = top ^ hop

    def run(flags, picks, w_near, w_far):
        quarter = w_near.shape[0] // 2
        low = flags[0] == 1
        near_width, middle_width, last_width = pieces_of(4 * quarter)

        def rows_of(x, start, size):
            return lax.dynamic_slice_in_dim(x, start, size, 0)

        def end_part(x):
            return rows_of(x, jnp.where(low, 0, quarter), quarter)

        def own_part(x):
            return rows_of(x, jnp.where(low, quarter, 0), quarter)

        def sibling(x, u, v):
            return partner(jnp.where(picks[0] == 1, x, jnp.where(picks[1] == 1, v, u)), 1)

        def masked(u, swapped_in):
            return jnp.where(picks[2] == 1, u, swapped_in)

        def in_order(end, own):
            return jnp.concatenate([jnp.where(low, end, own), jnp.where(low, own, end)])

        def paired(end, own):
            return jnp.concatenate([end, own])

        w_end, w_own = end_part(w_near), own_part(w_near)
        f_near, e_first, wu_end, wu_own = across(w_far), inward(own_part(w_far)), partner(w_end, hop), partner(w_own, hop)
        e_second = inward(end_part(w_far))

        e_first, wu_end, w_near = gated((e_first, wu_end, w_near))
        wv_end, e_near = partner(wu_end, rest), inward(w_near)

        f_near, wu_own, wv_end, e_second = gated((f_near, wu_own, wv_end, e_second))
        f_end, f_own = end_part(f_near), own_part(f_near)
        g_end, fu_end, wv_own, g_own = across(e_first), partner(f_end, hop), partner(wu_own, rest), across(e_second)

        g_end, fu_end, wv_own = gated((g_end, fu_end, wv_own))
        gu_end, fv_end = partner(g_end, hop), partner(fu_end, rest)
        wu = paired(wu_end, wu_own)
        w_swap = sibling(paired(w_end, w_own), wu, paired(wv_end, wv_own))

        g_own, gu_end, fv_end, w_swap, e_near, w_near, wv_end = gated((g_own, gu_end, fv_end, w_swap, e_near, w_near, wv_end))
        wm, x_owns = masked(wu, w_swap), paired(f_own, g_own)
        f_far, ev_end, gv_end = across(w_near), inward(wv_end), partner(gu_end, rest)
        em_end, u_owns = inward(wm[:quarter]), partner(x_owns, hop)

        gv_end, ev_end = gated((gv_end, ev_end))
        nears = [w_near, e_near, f_near, in_order(g_end, g_own)]
        ends_v = [wv_end, ev_end, fv_end, gv_end]
        flat_v = edge_tiles(flags, [ends_v], nears, [], 1, 0, quarter, scale)
        sent_v = outward(flat_v)
        u_ends = paired(fu_end, gu_end)
        swap_ends = sibling(paired(f_end, g_end), u_ends, paired(fv_end, gv_end))

        f_far, u_owns, em_end, swap_ends, sent_v, wv_own = gated((f_far, u_owns, em_end, swap_ends, sent_v, wv_own))
        inner = 2 * quarter - last_width
        g_mid = across(rows_of(e_near, jnp.where(low, last_width, 0), inner))
        v_owns, e_owns = partner(u_owns, rest), inward(paired(wm[quarter:], wv_own))
        m_ends = masked(u_ends, swap_ends)
        ends_m = [wm, em_end, m_ends, m_ends]
        flat_m = edge_tiles(flags, [ends_m], nears, [], 0, 0, quarter, scale)
        sent_m = outward(flat_m)
        g_last = across(rows_of(e_near, jnp.where(low, 0, inner), last_width))

        g_mid, sent_m = gated((g_mid, sent_m))
        e_far = in_order(e_second, e_first)
        fars = [w_far, e_far, f_far, g_mid]
        flat = edge_tiles(flags, [ends_m, ends_v], nears, fars, 0, 1, quarter, scale)
        sent = outward(flat)

        g_last, v_owns, e_owns, sent = gated((g_last, v_owns, e_owns, sent))
        fars = [w_far, e_far, f_far, g_last]
        last = outward(edge_tiles(flags, [ends_m, ends_v], [], fars, 0, 2, quarter, scale))
        swap_owns = sibling(x_owns, u_owns, v_owns)
        m_owns = masked(u_owns, swap_owns)

        packed = [x.astype(jnp.float32) for x in (sent_m, sent_v)]
        own = [[wm, e_owns, m_owns, m_owns], [wv_own, e_owns, v_owns, v_owns]]
        fars = [w_far, e_far, f_far, g_mid, g_last]
        out = middle_tiles(flags, own, nears, fars, packed, quarter, scale)
        out, sent, last = gated((out, sent, last))
        pieces = [([0, 1], (0, last_width)), ([0, 1], (middle_width, 0))]
        return place_tiles(
            flags, out, [sent.astype(jnp.float32), last.astype(jnp.float32)], (near_width, 0), pieces, middle_width + last_width
        )

    return run


def shards_line(activations, plan):
    tokens, units = activations.shape
    top = lax.axis_size("tensor") - 1
    scale = 1.0 / math.sqrt(tokens * LINE)
    place = lax.axis_index("dp")
    low = place < 2
    first = plan[0] == top
    flags = jnp.stack([low, (place == 1) | (place == 2), first]).astype(jnp.int32)
    top_half, bottom_half = jnp.split(activations.T, 2)
    halves = [jnp.where(low, top_half, bottom_half), jnp.where(low, bottom_half, top_half)]
    mask = plan[0] + plan[1] - top
    high = (mask >> 1) == 2
    hop = jnp.where(high, 4, 2)
    picks = jnp.stack([mask == 1, mask == (top ^ 1), mask == hop]).astype(jnp.int32)
    return lax.cond(high, line_branch(4, top, scale), line_branch(2, top, scale), flags, picks, *halves)


def solution(mesh):
    fast = mesh.shape["dp"] == LINE and mesh.shape["tensor"] == 8
    return jax.shard_map(
        shards_line if fast else shards_any,
        mesh=mesh,
        in_specs=(P("dp", "tensor"), P()),
        out_specs=P(None, "dp", "tensor"),
        check_vma=False,
    )
```

```python
import functools
import math

import jax
import jax.numpy as jnp
from jax import lax
from jax.experimental import pallas as pl
from jax.experimental.pallas import tpu as pltpu
from jax.sharding import PartitionSpec as P

ROUNDS = 2
LINE = 4
LANES = 128
STRIP = 104
TAIL = 16
EDGE_VMEM = 16 * 2**20
MIDDLE_VMEM = 24 * 2**20


def swapped(x, axis, apart):
    return lax.ppermute(x, axis, [(i, i ^ 1 << apart) for i in range(lax.axis_size(axis))])


def partner_panel(own, mask, width):
    current = own
    for bit in range(width):
        taken = jnp.bitwise_and(jnp.right_shift(mask, bit), 1) == 1
        current = jnp.where(taken, swapped(current, "tensor", bit), current)
    return current


def shards_any(activations, plan):
    width = lax.axis_size("tensor").bit_length() - 1
    scale = jnp.float32(1.0 / math.sqrt(activations.shape[0] * lax.axis_size("dp")))
    tiles = []
    for r in range(ROUNDS):
        other = partner_panel(activations, plan[r], width)
        tiles.append(
            lax.dot_general(other, activations, (((0,), (0,)), ((), ())), preferred_element_type=jnp.float32)
        )
    return lax.psum_scatter(jnp.stack(tiles), "dp", scatter_dimension=1, tiled=True) * scale


def inward(x):
    return lax.ppermute(x, "dp", [(0, 1), (3, 2)])


def across(x):
    return lax.ppermute(x, "dp", [(1, 2), (2, 1)])


def outward(x):
    return lax.ppermute(x, "dp", [(1, 0), (2, 3)])


def partner(x, mask):
    return lax.ppermute(x, "tensor", [(i, i ^ mask) for i in range(lax.axis_size("tensor"))])


def gated(values, *others):
    return lax.optimization_barrier((*values, *others))[: len(values)]


def strip(i):
    return pl.ds(pl.multiple_of(i * STRIP, 8), STRIP)


def times(rows, columns):
    return lax.dot_general(rows, columns, (((1,), (1,)), ((), ())), preferred_element_type=jnp.float32)


def end_start(low, quarter):
    return jnp.where(low, 0, quarter)


def own_start(low, quarter):
    return jnp.where(low, quarter, 0)


def pieces_of(units):
    near = units // 2 // LANES * LANES
    middle = (units - near) // 2 // LANES * LANES
    return near, middle, units - near - middle


def cut(ref, start, size):
    return ref[pl.ds(pl.multiple_of(start, 16), size)]


class Columns:
    def __init__(self, low, quarter):
        self.low, self.half = low, 2 * quarter
        self.near_width, middle, self.last = pieces_of(4 * quarter)
        self.spill = self.half - self.near_width
        self.inner = middle - 2 * self.spill

    def near(self, block, start, size):
        return cut(block, jnp.where(self.low, 0, self.spill) + start, size)

    def seam(self, near, far):
        top = far.shape[0] - self.spill if far.shape[0] < self.half else self.half - self.spill
        inward = jnp.where(self.low, cut(near, self.near_width, self.spill), cut(far, top, self.spill))
        outward = jnp.where(self.low, cut(far, 0, self.spill), cut(near, 0, self.spill))
        return jnp.concatenate([inward, outward])

    def middle(self, far, start, size):
        past = self.last if far.shape[0] == self.half else 0
        return cut(far, jnp.where(self.low, self.spill, past) + start, size)

    def outer(self, far, start, size):
        past = self.half - self.last if far.shape[0] == self.half else 0
        return cut(far, jnp.where(self.low, past, 0) + start, size)


def joined(parts):
    return jnp.concatenate(parts) if len(parts) > 1 else parts[0]


def shares(places, total):
    done = 0
    for at, size in places:
        yield pl.ds(pl.multiple_of(at, LANES), size), size, total[:, done : done + size]
        done += size


def summed(rows, starts, quarter, columns):
    total = None
    for v in range(4):
        parts = [cut(r[v], start[v], quarter) for r, start in zip(rows, starts)]
        term = times(joined(parts), joined([c(v) for c in columns]))
        total = term if total is None else total + term
    return total


def edge_kernel(masks, mask, piece, scale, flags_ref, *refs):
    rows = [refs[4 * k : 4 * k + 4] for k in range(masks)]
    nears, fars = refs[4 * masks : -2][:4], refs[4 * masks : -2][-4:]
    out_ref, most = refs[-2:]
    height = out_ref.shape[0] - TAIL
    quarter = height // masks
    low = flags_ref[0] == 1

    @pl.when(flags_ref[1] == 1)
    def _():
        cols = Columns(low, quarter)
        at = end_start(low, quarter)
        starts = [[at, 0, 0, quarter], [at, 0, 0, 0]][mask : mask + masks]
        most[...] = jnp.zeros_like(most)

        def put(places, *columns):
            total = summed(rows, starts, quarter, columns)
            for at, size, part in shares(places, total):
                out_ref[:height, at] = part
                high = jnp.max(jnp.abs(part).reshape(height // 8, 8, size), axis=0)
                for i in range(size // LANES):
                    most[...] = jnp.maximum(most[...], high[:, i * LANES : (i + 1) * LANES])

        if piece == 0:
            for start, size in ((0, 4 * LANES), (4 * LANES, cols.near_width - 4 * LANES)):
                put([(start, size)], lambda v: cols.near(nears[v], start, size))
        elif piece == 1:
            seam = 2 * cols.spill
            put(
                [(jnp.where(low, 0, cols.inner), seam), (jnp.where(low, seam, 0), cols.inner)],
                lambda v: cols.seam(nears[v], fars[v]),
                lambda v: cols.middle(fars[v], 0, cols.inner),
            )
        else:
            put([(0, cols.last)], lambda v: cols.outer(fars[v], 0, cols.last))

        biggest = jnp.max(most[...], axis=(0, 1), keepdims=True)
        power = jnp.ceil(jnp.log2(jnp.maximum(biggest * scale, 1e-30)))
        factor = scale * jnp.exp2(14.0 - power)

        @pl.loop(0, height // STRIP)
        def _(i):
            out_ref[strip(i)] = out_ref[strip(i)] * factor

        out_ref[height:] = jnp.broadcast_to(power, (TAIL, out_ref.shape[1]))


def edge_tiles(flags, rows, nears, fars, mask, piece, quarter, scale):
    masks, tokens = len(rows), rows[0][0].shape[1]
    width = pieces_of(4 * quarter)[piece]
    operands = [*sum(rows, []), *nears, *fars]
    flat = pl.pallas_call(
        functools.partial(edge_kernel, masks, mask, piece, scale),
        out_shape=jax.ShapeDtypeStruct((masks * quarter + TAIL, width), jnp.float32),
        in_specs=[pl.BlockSpec(memory_space=pltpu.SMEM)] + [pl.BlockSpec(memory_space=pltpu.VMEM)] * len(operands),
        out_specs=pl.BlockSpec(memory_space=pltpu.VMEM),
        scratch_shapes=[pltpu.VMEM((8, LANES), jnp.float32)],
        compiler_params=pltpu.CompilerParams(vmem_limit_bytes=EDGE_VMEM),
        cost_estimate=pl.CostEstimate(
            flops=8 * masks * quarter * tokens * width,
            bytes_accessed=8 * (masks * quarter + width) * tokens,
            transcendentals=0,
        ),
        name="edge_tiles",
    )(flags, *operands)
    return flat.astype(jnp.float16)


def unpack(flat, target, rounds, columns, quarter):
    rows = flat.shape[0] - TAIL
    factor = jnp.exp2(flat[rows : rows + 1, :1] - 14.0)
    for k, place in enumerate(rounds):

        @pl.loop(0, quarter // STRIP)
        def _(i):
            target[place, strip(i), columns] = flat[strip(i + k * (quarter // STRIP))] * factor


def middle_kernel(scale, flags_ref, *refs):
    rows, nears, fars, packed = [refs[:4], refs[4:8]], refs[8:12], refs[12:17], refs[17:19]
    out_ref = refs[-1]
    quarter, units = out_ref.shape[1:]
    near_width, middle_width, last_width = pieces_of(units)
    low = flags_ref[0] == 1
    middle = flags_ref[1] == 1
    first = flags_ref[2]

    @pl.when(middle)
    def _():
        cols = Columns(low, quarter)
        at_own = own_start(low, quarter)
        starts = [[at_own, 0, 0, quarter], [at_own, quarter, 0, quarter]]

        def put(places, *columns):
            total = summed(rows, starts, quarter, columns) * scale
            for at, size, part in shares(places, total):
                for k in range(2):
                    out_ref[lax.bitwise_xor(first, k), :, at] = part[k * quarter : (k + 1) * quarter]

        wide, seam = 4 * LANES, 2 * cols.spill
        near_at = jnp.where(low, 0, units - near_width)
        middle_at = jnp.where(low, near_width + seam, last_width)
        last_at = jnp.where(low, units - last_width, 0)
        rest = near_width - wide
        put([(near_at, wide)], lambda v: cols.near(nears[v], 0, wide))
        put(
            [(near_at + wide, rest), (middle_at, cols.inner)],
            lambda v: cols.near(nears[v], wide, rest),
            lambda v: cols.middle(fars[v], 0, cols.inner),
        )
        taken = wide - seam
        put(
            [(near_width, seam), (last_at, taken)],
            lambda v: cols.seam(nears[v], fars[v]),
            lambda v: cols.outer(fars[v + v // 3], 0, taken),
        )
        put([(last_at + taken, last_width - taken)], lambda v: cols.outer(fars[v + v // 3], taken, last_width - taken))

    @pl.when(jnp.logical_not(middle))
    def _():
        near = pl.ds(pl.multiple_of(jnp.where(low, 0, units - near_width), LANES), near_width)
        unpack(packed[0], out_ref, [first], near, quarter)
        unpack(packed[1], out_ref, [1 - first], near, quarter)


def middle_tiles(flags, rows, nears, fars, packed, quarter, scale):
    tokens, units = rows[0][0].shape[1], 4 * quarter
    operands = [*sum(rows, []), *nears, *fars, *packed]
    return pl.pallas_call(
        functools.partial(middle_kernel, scale),
        out_shape=jax.ShapeDtypeStruct((2, quarter, units), jnp.float32),
        in_specs=[pl.BlockSpec(memory_space=pltpu.SMEM)] + [pl.BlockSpec(memory_space=pltpu.VMEM)] * len(operands),
        out_specs=pl.BlockSpec(memory_space=pltpu.VMEM),
        compiler_params=pltpu.CompilerParams(vmem_limit_bytes=MIDDLE_VMEM),
        cost_estimate=pl.CostEstimate(
            flops=16 * quarter * tokens * units, bytes_accessed=8 * (2 * quarter + units) * tokens, transcendentals=0
        ),
        name="middle_tiles",
    )(flags, *operands)


def place_kernel(starts, pieces, flags_ref, out_in, *refs):
    flats, (out_ref, buf, sem) = refs[:-3], refs[-3:]
    quarter, width = buf.shape[1:]
    low = flags_ref[0] == 1
    first = flags_ref[2]
    rounds = [first, 1 - first]

    def side(pair):
        return pl.multiple_of(jnp.where(low, *pair), LANES)

    @pl.when(flags_ref[1] == 0)
    def _():
        for flat, (masks, at) in zip(flats, pieces):
            unpack(flat, buf, [rounds[k] for k in masks], pl.ds(side(at), flat.shape[1]), quarter)
        copy = pltpu.make_async_copy(buf, out_ref.at[:, :, pl.ds(side(starts), width)], sem)
        copy.start()
        copy.wait()


def place_tiles(flags, out, flats, starts, pieces, width):
    return pl.pallas_call(
        functools.partial(place_kernel, starts, pieces),
        out_shape=jax.ShapeDtypeStruct(out.shape, out.dtype),
        in_specs=[
            pl.BlockSpec(memory_space=pltpu.SMEM),
            pl.BlockSpec(memory_space=pl.ANY),
            *[pl.BlockSpec(memory_space=pltpu.VMEM)] * len(flats),
        ],
        out_specs=pl.BlockSpec(memory_space=pl.ANY),
        scratch_shapes=[pltpu.VMEM((2, out.shape[1], width), jnp.float32), pltpu.SemaphoreType.DMA],
        input_output_aliases={1: 0},
        compiler_params=pltpu.CompilerParams(vmem_limit_bytes=EDGE_VMEM),
        cost_estimate=pl.CostEstimate(flops=0, bytes_accessed=6 * 832 * width, transcendentals=0),
        name="place_tiles",
    )(flags, out, *flats)


def line_branch(hop, top, scale):
    rest = top ^ hop

    def run(flags, picks, w_near, w_far):
        quarter = w_near.shape[0] // 2
        low = flags[0] == 1
        near_width, middle_width, last_width = pieces_of(4 * quarter)

        def rows_of(x, start, size):
            return lax.dynamic_slice_in_dim(x, start, size, 0)

        def end_part(x):
            return rows_of(x, jnp.where(low, 0, quarter), quarter)

        def own_part(x):
            return rows_of(x, jnp.where(low, quarter, 0), quarter)

        def sibling(x, u, v):
            return partner(jnp.where(picks[0] == 1, x, jnp.where(picks[1] == 1, v, u)), 1)

        def masked(u, swapped_in):
            return jnp.where(picks[2] == 1, u, swapped_in)

        f_near, e_far, wu, e_near = across(w_far), inward(w_far), partner(w_near, hop), inward(w_near)

        e_far, f_near, wu, w_near = gated((e_far, f_near, wu, w_near))
        g_near, f_far, fu, wv = across(e_far), across(w_near), partner(f_near, hop), partner(wu, rest)

        g_near, e_near, fu, wv, wu = gated((g_near, e_near, fu, wv, wu))
        gu_end, fv_end, ev_end = partner(end_part(g_near), hop), partner(end_part(fu), rest), inward(end_part(wv))
        w_swap = sibling(w_near, wu, wv)

        gu_end, fv_end, ev_end, w_swap, g_near = gated((gu_end, fv_end, ev_end, w_swap, g_near))
        wm = masked(wu, w_swap)
        gv_end, gu_own, em_end = partner(gu_end, rest), partner(own_part(g_near), hop), inward(end_part(wm))

        gv_end, gu_own, em_end, f_far, fu, e_near = gated((gv_end, gu_own, em_end, f_far, fu, e_near))
        nears = [w_near, e_near, f_near, g_near]
        ends_v = [wv, ev_end, fv_end, gv_end]
        flat_v = edge_tiles(flags, [ends_v], nears, [], 1, 0, quarter, scale)
        fu, gu_own, wm, flat_v = gated((fu, gu_own, wm, flat_v))
        sent_v = outward(flat_v)
        inner = 2 * quarter - last_width
        u_ends, u_owns = [jnp.concatenate(x) for x in ([end_part(fu), gu_end], [own_part(fu), gu_own])]
        x_ends, x_owns = [jnp.concatenate([part(f_near), part(g_near)]) for part in (end_part, own_part)]
        swap_ends = sibling(x_ends, u_ends, jnp.concatenate([fv_end, gv_end]))
        g_mid = across(rows_of(e_near, jnp.where(low, last_width, 0), inner))
        v_owns, e_owns = partner(u_owns, rest), inward(jnp.concatenate([own_part(wm), own_part(wv)]))

        swap_ends, flat_v = gated((swap_ends, flat_v))
        m_ends = masked(u_ends, swap_ends)
        g_last = across(rows_of(e_near, jnp.where(low, 0, inner), last_width))
        ends_m = [wm, em_end, m_ends, m_ends]
        flat_m = edge_tiles(flags, [ends_m], nears, [], 0, 0, quarter, scale)

        g_mid, flat_m, sent_v = gated((g_mid, flat_m, sent_v))
        sent_m = outward(flat_m)
        fars = [w_far, e_far, f_far, g_mid]
        flat = edge_tiles(flags, [ends_m, ends_v], nears, fars, 0, 1, quarter, scale)
        sent = outward(flat)

        g_last, flat = gated((g_last, flat))
        fars = [w_far, e_far, f_far, g_last]
        flat = edge_tiles(flags, [ends_m, ends_v], [], fars, 0, 2, quarter, scale)
        v_owns, e_owns, sent_m, sent, flat = gated((v_owns, e_owns, sent_m, sent, flat))
        last = outward(flat)
        swap_owns = sibling(x_owns, u_owns, v_owns)
        m_owns = masked(u_owns, swap_owns)

        packed = [x.astype(jnp.float32) for x in (sent_m, sent_v)]
        own = [[wm, e_owns, m_owns, m_owns], [wv, e_owns, v_owns, v_owns]]
        fars = [w_far, e_far, f_far, g_mid, g_last]
        out = middle_tiles(flags, own, nears, fars, packed, quarter, scale)
        out, sent, last = gated((out, sent, last))
        pieces = [([0, 1], (0, last_width)), ([0, 1], (middle_width, 0))]
        return place_tiles(
            flags, out, [sent.astype(jnp.float32), last.astype(jnp.float32)], (near_width, 0), pieces, middle_width + last_width
        )

    return run


def shards_line(activations, plan):
    tokens, units = activations.shape
    top = lax.axis_size("tensor") - 1
    scale = 1.0 / math.sqrt(tokens * LINE)
    place = lax.axis_index("dp")
    low = place < 2
    first = plan[0] == top
    flags = jnp.stack([low, (place == 1) | (place == 2), first]).astype(jnp.int32)
    top_half, bottom_half = jnp.split(activations.T, 2)
    halves = [jnp.where(low, top_half, bottom_half), jnp.where(low, bottom_half, top_half)]
    mask = plan[0] + plan[1] - top
    high = (mask >> 1) == 2
    hop = jnp.where(high, 4, 2)
    picks = jnp.stack([mask == 1, mask == (top ^ 1), mask == hop]).astype(jnp.int32)
    return lax.cond(high, line_branch(4, top, scale), line_branch(2, top, scale), flags, picks, *halves)


def solution(mesh):
    fast = mesh.shape["dp"] == LINE and mesh.shape["tensor"] == 8
    return jax.shard_map(
        shards_line if fast else shards_any,
        mesh=mesh,
        in_specs=(P("dp", "tensor"), P()),
        out_specs=P(None, "dp", "tensor"),
        check_vma=False,
    )
```

```python
import functools
import math

import jax
import jax.numpy as jnp
from jax import lax
from jax.experimental import pallas as pl
from jax.experimental.pallas import tpu as pltpu
from jax.sharding import PartitionSpec as P

ROUNDS = 2
LINE = 4
LANES = 128
STRIP = 104
TAIL = 16
EDGE_VMEM = 16 * 2**20
MIDDLE_VMEM = 24 * 2**20


def swapped(x, axis, apart):
    return lax.ppermute(x, axis, [(i, i ^ 1 << apart) for i in range(lax.axis_size(axis))])


def partner_panel(own, mask, width):
    current = own
    for bit in range(width):
        taken = jnp.bitwise_and(jnp.right_shift(mask, bit), 1) == 1
        current = jnp.where(taken, swapped(current, "tensor", bit), current)
    return current


def shards_any(activations, plan):
    width = lax.axis_size("tensor").bit_length() - 1
    scale = jnp.float32(1.0 / math.sqrt(activations.shape[0] * lax.axis_size("dp")))
    tiles = []
    for r in range(ROUNDS):
        other = partner_panel(activations, plan[r], width)
        tiles.append(
            lax.dot_general(other, activations, (((0,), (0,)), ((), ())), preferred_element_type=jnp.float32)
        )
    return lax.psum_scatter(jnp.stack(tiles), "dp", scatter_dimension=1, tiled=True) * scale


def inward(x):
    return lax.ppermute(x, "dp", [(0, 1), (3, 2)])


def across(x):
    return lax.ppermute(x, "dp", [(1, 2), (2, 1)])


def outward(x):
    return lax.ppermute(x, "dp", [(1, 0), (2, 3)])


def partner(x, mask):
    return lax.ppermute(x, "tensor", [(i, i ^ mask) for i in range(lax.axis_size("tensor"))])


def gated(values, *others):
    return lax.optimization_barrier((*values, *others))[: len(values)]


def strip(i):
    return pl.ds(pl.multiple_of(i * STRIP, 8), STRIP)


def times(rows, columns):
    return lax.dot_general(rows, columns, (((1,), (1,)), ((), ())), preferred_element_type=jnp.float32)


def end_start(low, quarter):
    return jnp.where(low, 0, quarter)


def own_start(low, quarter):
    return jnp.where(low, quarter, 0)


def pieces_of(units):
    near = units // 2 // LANES * LANES
    middle = (units - near) // 2 // LANES * LANES
    return near, middle, units - near - middle


def cut(ref, start, size):
    return ref[pl.ds(pl.multiple_of(start, 16), size)]


class Columns:
    def __init__(self, low, quarter):
        self.low, self.half = low, 2 * quarter
        self.near_width, middle, self.last = pieces_of(4 * quarter)
        self.spill = self.half - self.near_width
        self.inner = middle - 2 * self.spill

    def near(self, block, start, size):
        return cut(block, jnp.where(self.low, 0, self.spill) + start, size)

    def seam(self, near, far):
        top = far.shape[0] - self.spill if far.shape[0] < self.half else self.half - self.spill
        inward = jnp.where(self.low, cut(near, self.near_width, self.spill), cut(far, top, self.spill))
        outward = jnp.where(self.low, cut(far, 0, self.spill), cut(near, 0, self.spill))
        return jnp.concatenate([inward, outward])

    def middle(self, far, start, size):
        past = self.last if far.shape[0] == self.half else 0
        return cut(far, jnp.where(self.low, self.spill, past) + start, size)

    def outer(self, far, start, size):
        past = self.half - self.last if far.shape[0] == self.half else 0
        return cut(far, jnp.where(self.low, past, 0) + start, size)


def joined(parts):
    return jnp.concatenate(parts) if len(parts) > 1 else parts[0]


def shares(places, total):
    done = 0
    for at, size in places:
        yield pl.ds(pl.multiple_of(at, LANES), size), size, total[:, done : done + size]
        done += size


def summed(rows, starts, quarter, columns):
    total = None
    for v in range(4):
        parts = [cut(r[v], start[v], quarter) for r, start in zip(rows, starts)]
        term = times(joined(parts), joined([c(v) for c in columns]))
        total = term if total is None else total + term
    return total


def edge_kernel(masks, mask, piece, scale, flags_ref, *refs):
    rows = [refs[4 * k : 4 * k + 4] for k in range(masks)]
    nears, fars = refs[4 * masks : -2][:4], refs[4 * masks : -2][-4:]
    out_ref, most = refs[-2:]
    height = out_ref.shape[0] - TAIL
    quarter = height // masks
    low = flags_ref[0] == 1

    @pl.when(flags_ref[1] == 1)
    def _():
        cols = Columns(low, quarter)
        at = end_start(low, quarter)
        starts = [[at, 0, 0, quarter], [at, 0, 0, 0]][mask : mask + masks]
        most[...] = jnp.zeros_like(most)

        def put(places, *columns):
            total = summed(rows, starts, quarter, columns)
            for at, size, part in shares(places, total):
                out_ref[:height, at] = part
                high = jnp.max(jnp.abs(part).reshape(height // 8, 8, size), axis=0)
                for i in range(size // LANES):
                    most[...] = jnp.maximum(most[...], high[:, i * LANES : (i + 1) * LANES])

        if piece == 0:
            for start, size in ((0, 4 * LANES), (4 * LANES, cols.near_width - 4 * LANES)):
                put([(start, size)], lambda v: cols.near(nears[v], start, size))
        elif piece == 1:
            seam = 2 * cols.spill
            put(
                [(jnp.where(low, 0, cols.inner), seam), (jnp.where(low, seam, 0), cols.inner)],
                lambda v: cols.seam(nears[v], fars[v]),
                lambda v: cols.middle(fars[v], 0, cols.inner),
            )
        else:
            put([(0, cols.last)], lambda v: cols.outer(fars[v], 0, cols.last))

        biggest = jnp.max(most[...], axis=(0, 1), keepdims=True)
        power = jnp.ceil(jnp.log2(jnp.maximum(biggest * scale, 1e-30)))
        factor = scale * jnp.exp2(14.0 - power)

        @pl.loop(0, height // STRIP)
        def _(i):
            out_ref[strip(i)] = out_ref[strip(i)] * factor

        out_ref[height:] = jnp.broadcast_to(power, (TAIL, out_ref.shape[1]))


def edge_tiles(flags, rows, nears, fars, mask, piece, quarter, scale):
    masks, tokens = len(rows), rows[0][0].shape[1]
    width = pieces_of(4 * quarter)[piece]
    operands = [*sum(rows, []), *nears, *fars]
    flat = pl.pallas_call(
        functools.partial(edge_kernel, masks, mask, piece, scale),
        out_shape=jax.ShapeDtypeStruct((masks * quarter + TAIL, width), jnp.float32),
        in_specs=[pl.BlockSpec(memory_space=pltpu.SMEM)] + [pl.BlockSpec(memory_space=pltpu.VMEM)] * len(operands),
        out_specs=pl.BlockSpec(memory_space=pltpu.VMEM),
        scratch_shapes=[pltpu.VMEM((8, LANES), jnp.float32)],
        compiler_params=pltpu.CompilerParams(vmem_limit_bytes=EDGE_VMEM),
        cost_estimate=pl.CostEstimate(
            flops=8 * masks * quarter * tokens * width,
            bytes_accessed=8 * (masks * quarter + width) * tokens,
            transcendentals=0,
        ),
        name="edge_tiles",
    )(flags, *operands)
    return flat.astype(jnp.float16)


def unpack(flat, target, rounds, columns, quarter):
    rows = flat.shape[0] - TAIL
    factor = jnp.exp2(flat[rows : rows + 1, :1] - 14.0)
    for k, place in enumerate(rounds):

        @pl.loop(0, quarter // STRIP)
        def _(i):
            target[place, strip(i), columns] = flat[strip(i + k * (quarter // STRIP))] * factor


def middle_kernel(scale, flags_ref, *refs):
    rows, nears, fars, packed = [refs[:4], refs[4:8]], refs[8:12], refs[12:17], refs[17:19]
    out_ref = refs[-1]
    quarter, units = out_ref.shape[1:]
    near_width, middle_width, last_width = pieces_of(units)
    low = flags_ref[0] == 1
    middle = flags_ref[1] == 1
    first = flags_ref[2]

    @pl.when(middle)
    def _():
        cols = Columns(low, quarter)
        at_own = own_start(low, quarter)
        starts = [[at_own, 0, 0, quarter], [at_own, quarter, 0, quarter]]

        def put(places, *columns):
            total = summed(rows, starts, quarter, columns) * scale
            for at, size, part in shares(places, total):
                for k in range(2):
                    out_ref[lax.bitwise_xor(first, k), :, at] = part[k * quarter : (k + 1) * quarter]

        wide, seam = 4 * LANES, 2 * cols.spill
        near_at = jnp.where(low, 0, units - near_width)
        middle_at = jnp.where(low, near_width + seam, last_width)
        last_at = jnp.where(low, units - last_width, 0)
        rest = near_width - wide
        put([(near_at, wide)], lambda v: cols.near(nears[v], 0, wide))
        put(
            [(near_at + wide, rest), (middle_at, cols.inner)],
            lambda v: cols.near(nears[v], wide, rest),
            lambda v: cols.middle(fars[v], 0, cols.inner),
        )
        taken = wide - seam
        put(
            [(near_width, seam), (last_at, taken)],
            lambda v: cols.seam(nears[v], fars[v]),
            lambda v: cols.outer(fars[v + v // 3], 0, taken),
        )
        put([(last_at + taken, last_width - taken)], lambda v: cols.outer(fars[v + v // 3], taken, last_width - taken))

    @pl.when(jnp.logical_not(middle))
    def _():
        near = pl.ds(pl.multiple_of(jnp.where(low, 0, units - near_width), LANES), near_width)
        unpack(packed[0], out_ref, [first], near, quarter)
        unpack(packed[1], out_ref, [1 - first], near, quarter)


def middle_tiles(flags, rows, nears, fars, packed, quarter, scale):
    tokens, units = rows[0][0].shape[1], 4 * quarter
    operands = [*sum(rows, []), *nears, *fars, *packed]
    return pl.pallas_call(
        functools.partial(middle_kernel, scale),
        out_shape=jax.ShapeDtypeStruct((2, quarter, units), jnp.float32),
        in_specs=[pl.BlockSpec(memory_space=pltpu.SMEM)] + [pl.BlockSpec(memory_space=pltpu.VMEM)] * len(operands),
        out_specs=pl.BlockSpec(memory_space=pltpu.VMEM),
        compiler_params=pltpu.CompilerParams(vmem_limit_bytes=MIDDLE_VMEM),
        cost_estimate=pl.CostEstimate(
            flops=16 * quarter * tokens * units, bytes_accessed=8 * (2 * quarter + units) * tokens, transcendentals=0
        ),
        name="middle_tiles",
    )(flags, *operands)


def place_kernel(starts, pieces, flags_ref, out_in, *refs):
    flats, (out_ref, buf, sem) = refs[:-3], refs[-3:]
    quarter, width = buf.shape[1:]
    low = flags_ref[0] == 1
    first = flags_ref[2]
    rounds = [first, 1 - first]

    def side(pair):
        return pl.multiple_of(jnp.where(low, *pair), LANES)

    @pl.when(flags_ref[1] == 0)
    def _():
        for flat, (masks, at) in zip(flats, pieces):
            unpack(flat, buf, [rounds[k] for k in masks], pl.ds(side(at), flat.shape[1]), quarter)
        copy = pltpu.make_async_copy(buf, out_ref.at[:, :, pl.ds(side(starts), width)], sem)
        copy.start()
        copy.wait()


def place_tiles(flags, out, flats, starts, pieces, width):
    return pl.pallas_call(
        functools.partial(place_kernel, starts, pieces),
        out_shape=jax.ShapeDtypeStruct(out.shape, out.dtype),
        in_specs=[
            pl.BlockSpec(memory_space=pltpu.SMEM),
            pl.BlockSpec(memory_space=pl.ANY),
            *[pl.BlockSpec(memory_space=pltpu.VMEM)] * len(flats),
        ],
        out_specs=pl.BlockSpec(memory_space=pl.ANY),
        scratch_shapes=[pltpu.VMEM((2, out.shape[1], width), jnp.float32), pltpu.SemaphoreType.DMA],
        input_output_aliases={1: 0},
        compiler_params=pltpu.CompilerParams(vmem_limit_bytes=EDGE_VMEM),
        cost_estimate=pl.CostEstimate(flops=0, bytes_accessed=6 * 832 * width, transcendentals=0),
        name="place_tiles",
    )(flags, out, *flats)


def line_branch(hop, top, scale):
    rest = top ^ hop

    def run(flags, picks, w_near, w_far):
        quarter = w_near.shape[0] // 2
        low = flags[0] == 1
        near_width, middle_width, last_width = pieces_of(4 * quarter)

        def rows_of(x, start, size):
            return lax.dynamic_slice_in_dim(x, start, size, 0)

        def end_part(x):
            return rows_of(x, jnp.where(low, 0, quarter), quarter)

        def own_part(x):
            return rows_of(x, jnp.where(low, quarter, 0), quarter)

        def sibling(x, u, v):
            return partner(jnp.where(picks[0] == 1, x, jnp.where(picks[1] == 1, v, u)), 1)

        def masked(u, swapped_in):
            return jnp.where(picks[2] == 1, u, swapped_in)

        f_near, e_far, wu, e_near = across(w_far), inward(w_far), partner(w_near, hop), inward(w_near)

        e_far, f_near, wu, w_near = gated((e_far, f_near, wu, w_near))
        g_near, f_far, fu, wv = across(e_far), across(w_near), partner(f_near, hop), partner(wu, rest)

        g_near, e_near, fu, wv, wu = gated((g_near, e_near, fu, wv, wu))
        gu_end, fv_end, ev_end = partner(end_part(g_near), hop), partner(end_part(fu), rest), inward(end_part(wv))
        w_swap = sibling(w_near, wu, wv)

        gu_end, fv_end, ev_end, w_swap, g_near = gated((gu_end, fv_end, ev_end, w_swap, g_near))
        wm = masked(wu, w_swap)
        gv_end, gu_own, em_end = partner(gu_end, rest), partner(own_part(g_near), hop), inward(end_part(wm))

        gv_end, gu_own, em_end, f_far, fu, e_near = gated((gv_end, gu_own, em_end, f_far, fu, e_near))
        inner = 2 * quarter - last_width
        u_ends, u_owns = [jnp.concatenate(x) for x in ([end_part(fu), gu_end], [own_part(fu), gu_own])]
        x_ends, x_owns = [jnp.concatenate([part(f_near), part(g_near)]) for part in (end_part, own_part)]
        swap_ends = sibling(x_ends, u_ends, jnp.concatenate([fv_end, gv_end]))
        g_mid = across(rows_of(e_near, jnp.where(low, last_width, 0), inner))
        v_owns, e_owns = partner(u_owns, rest), inward(jnp.concatenate([own_part(wm), own_part(wv)]))
        nears = [w_near, e_near, f_near, g_near]
        swap_ends, gv_end = gated((swap_ends, gv_end))
        ends_v = [wv, ev_end, fv_end, gv_end]
        flat_v = edge_tiles(flags, [ends_v], nears, [], 1, 0, quarter, scale)
        sent_v = outward(flat_v)

        swap_ends, flat_v = gated((swap_ends, flat_v))
        m_ends = masked(u_ends, swap_ends)
        g_last = across(rows_of(e_near, jnp.where(low, 0, inner), last_width))
        ends_m = [wm, em_end, m_ends, m_ends]
        flat_m = edge_tiles(flags, [ends_m], nears, [], 0, 0, quarter, scale)

        flat_m, sent_v = gated((flat_m, sent_v))
        sent_m = outward(flat_m)
        g_mid, flat_m = gated((g_mid, flat_m))
        fars = [w_far, e_far, f_far, g_mid]
        flat = edge_tiles(flags, [ends_m, ends_v], nears, fars, 0, 1, quarter, scale)
        sent = outward(flat)

        g_last, flat = gated((g_last, flat))
        fars = [w_far, e_far, f_far, g_last]
        flat = edge_tiles(flags, [ends_m, ends_v], [], fars, 0, 2, quarter, scale)
        v_owns, e_owns, sent_m, sent, flat = gated((v_owns, e_owns, sent_m, sent, flat))
        last = outward(flat)
        swap_owns = sibling(x_owns, u_owns, v_owns)
        m_owns = masked(u_owns, swap_owns)

        packed = [x.astype(jnp.float32) for x in (sent_m, sent_v)]
        own = [[wm, e_owns, m_owns, m_owns], [wv, e_owns, v_owns, v_owns]]
        fars = [w_far, e_far, f_far, g_mid, g_last]
        out = middle_tiles(flags, own, nears, fars, packed, quarter, scale)
        out, sent, last = gated((out, sent, last))
        pieces = [([0, 1], (0, last_width)), ([0, 1], (middle_width, 0))]
        return place_tiles(
            flags, out, [sent.astype(jnp.float32), last.astype(jnp.float32)], (near_width, 0), pieces, middle_width + last_width
        )

    return run


def shards_line(activations, plan):
    tokens, units = activations.shape
    top = lax.axis_size("tensor") - 1
    scale = 1.0 / math.sqrt(tokens * LINE)
    place = lax.axis_index("dp")
    low = place < 2
    first = plan[0] == top
    flags = jnp.stack([low, (place == 1) | (place == 2), first]).astype(jnp.int32)
    top_half, bottom_half = jnp.split(activations.T, 2)
    halves = [jnp.where(low, top_half, bottom_half), jnp.where(low, bottom_half, top_half)]
    mask = plan[0] + plan[1] - top
    high = (mask >> 1) == 2
    hop = jnp.where(high, 4, 2)
    picks = jnp.stack([mask == 1, mask == (top ^ 1), mask == hop]).astype(jnp.int32)
    return lax.cond(high, line_branch(4, top, scale), line_branch(2, top, scale), flags, picks, *halves)


def solution(mesh):
    fast = mesh.shape["dp"] == LINE and mesh.shape["tensor"] == 8
    return jax.shard_map(
        shards_line if fast else shards_any,
        mesh=mesh,
        in_specs=(P("dp", "tensor"), P()),
        out_specs=P(None, "dp", "tensor"),
        check_vma=False,
    )
```

```python
import functools
import math

import jax
import jax.numpy as jnp
from jax import lax
from jax.experimental import pallas as pl
from jax.experimental.pallas import tpu as pltpu
from jax.sharding import PartitionSpec as P

ROUNDS = 2
LINE = 4
LANES = 128
STRIP = 104
TAIL = 16
EDGE_VMEM = 18 * 2**20
MIDDLE_VMEM = 32 * 2**20


def swapped(x, axis, apart):
    return lax.ppermute(x, axis, [(i, i ^ 1 << apart) for i in range(lax.axis_size(axis))])


def partner_panel(own, mask, width):
    current = own
    for bit in range(width):
        taken = jnp.bitwise_and(jnp.right_shift(mask, bit), 1) == 1
        current = jnp.where(taken, swapped(current, "tensor", bit), current)
    return current


def shards_any(activations, plan):
    width = lax.axis_size("tensor").bit_length() - 1
    scale = jnp.float32(1.0 / math.sqrt(activations.shape[0] * lax.axis_size("dp")))
    tiles = []
    for r in range(ROUNDS):
        other = partner_panel(activations, plan[r], width)
        tiles.append(
            lax.dot_general(other, activations, (((0,), (0,)), ((), ())), preferred_element_type=jnp.float32)
        )
    return lax.psum_scatter(jnp.stack(tiles), "dp", scatter_dimension=1, tiled=True) * scale


def inward(x):
    return lax.ppermute(x, "dp", [(0, 1), (3, 2)])


def across(x):
    return lax.ppermute(x, "dp", [(1, 2), (2, 1)])


def outward(x):
    return lax.ppermute(x, "dp", [(1, 0), (2, 3)])


def partner(x, mask):
    return lax.ppermute(x, "tensor", [(i, i ^ mask) for i in range(lax.axis_size("tensor"))])


def gated(values, *others):
    return lax.optimization_barrier((*values, *others))[: len(values)]


def strip(i):
    return pl.ds(pl.multiple_of(i * STRIP, 8), STRIP)


def times(rows, columns):
    return lax.dot_general(rows, columns, (((1,), (1,)), ((), ())), preferred_element_type=jnp.float32)


def end_start(low, quarter):
    return jnp.where(low, 0, quarter)


def own_start(low, quarter):
    return jnp.where(low, quarter, 0)


def pieces_of(units):
    near = units // 2 // LANES * LANES
    last = (units - near) // 2 // LANES * LANES
    return near, units - near - last, last


def wait_all(buf, sem):
    pltpu.make_async_copy(buf, buf, sem).wait()


def load(block, source, size, buf, target, sem):
    pltpu.make_async_copy(
        block.at[pl.ds(pl.multiple_of(source, 16), size)], buf.at[pl.ds(pl.multiple_of(target, 16), size)], sem
    ).start()


def load_rows(rows, starts, row_buf, sem, v, quarter):
    for k, blocks in enumerate(rows):
        load(blocks[v], starts[k][v], quarter, row_buf.at[v], k * quarter, sem.at[v])


def clear(ref, rows):
    @pl.loop(0, rows // STRIP)
    def _(i):
        ref[strip(i)] = jnp.zeros((STRIP, ref.shape[1]), jnp.float32)


def edge_kernel(masks, mask, piece, scale, flags_ref, *refs):
    rows = [refs[4 * k : 4 * k + 4] for k in range(masks)]
    out_ref, row_buf, col_buf, row_sems, col_sems = refs[-5:]
    nears, fars = refs[4 * masks : -5][:4], refs[4 * masks : -5][-4:]
    height, width = out_ref.shape[0] - TAIL, out_ref.shape[1]
    quarter = height // masks
    half = 2 * quarter
    near_width = pieces_of(4 * quarter)[0]
    low = flags_ref[0] == 1

    @pl.when(flags_ref[1] == 1)
    def _():
        at = end_start(low, quarter)
        starts = [[at, 0, at, 0], [at, quarter, 0, 0]][mask : mask + masks]
        for v in range(4):
            load_rows(rows, starts, row_buf, row_sems, v, quarter)
            buf, sem = col_buf.at[v], col_sems.at[v]
            whole = fars[v].shape[0] == half
            if piece == 0:
                load(nears[v], jnp.where(low, 0, half - width), width, buf, 0, sem)
            elif piece == 1:
                before = half - near_width
                new = width - before
                load(nears[v], jnp.where(low, near_width, 0), before, buf, jnp.where(low, 0, new), sem)
                load(fars[v], jnp.where(low, 0, half - new) if whole else 0, new, buf, jnp.where(low, before, 0), sem)
            else:
                load(fars[v], jnp.where(low, half - width, 0) if whole else 0, width, buf, 0, sem)

        clear(out_ref, height)
        tile = next(t for t in (512, 384, 256, 128) if width % t == 0)

        @pl.loop(0, 4)
        def _(v):
            wait_all(row_buf.at[v], row_sems.at[v])
            wait_all(col_buf.at[v], col_sems.at[v])

            @pl.loop(0, width // tile)
            def _(n):
                columns = pl.ds(pl.multiple_of(n * tile, LANES), tile)
                out_ref[:height, columns] += times(row_buf[v], col_buf[v, columns])

        def larger(i, most):
            return jnp.maximum(most, jnp.max(jnp.abs(out_ref[strip(i)]).reshape(STRIP // 8, 8, width), axis=0))

        most = lax.fori_loop(0, height // STRIP, larger, jnp.zeros((8, width), jnp.float32))
        biggest = jnp.max(most, axis=(0, 1), keepdims=True)
        power = jnp.ceil(jnp.log2(jnp.maximum(biggest * scale, 1e-30)))
        factor = scale * jnp.exp2(14.0 - power)

        @pl.loop(0, height // STRIP)
        def _(i):
            out_ref[strip(i)] = out_ref[strip(i)] * factor

        out_ref[height:] = jnp.broadcast_to(power, (TAIL, width))


def edge_tiles(flags, rows, nears, fars, mask, piece, quarter, scale):
    masks, tokens = len(rows), rows[0][0].shape[1]
    width = pieces_of(4 * quarter)[piece]
    operands = [*sum(rows, []), *nears, *fars]
    flat = pl.pallas_call(
        functools.partial(edge_kernel, masks, mask, piece, scale),
        out_shape=jax.ShapeDtypeStruct((masks * quarter + TAIL, width), jnp.float32),
        in_specs=[pl.BlockSpec(memory_space=pltpu.SMEM)] + [pl.BlockSpec(memory_space=pl.ANY)] * len(operands),
        out_specs=pl.BlockSpec(memory_space=pltpu.VMEM),
        scratch_shapes=[
            pltpu.VMEM((4, masks * quarter, tokens), jnp.bfloat16),
            pltpu.VMEM((4, width, tokens), jnp.bfloat16),
            pltpu.SemaphoreType.DMA((4,)),
            pltpu.SemaphoreType.DMA((4,)),
        ],
        compiler_params=pltpu.CompilerParams(vmem_limit_bytes=EDGE_VMEM),
        cost_estimate=pl.CostEstimate(
            flops=8 * masks * quarter * tokens * width,
            bytes_accessed=8 * (masks * quarter + width) * tokens,
            transcendentals=0,
        ),
        name="edge_tiles",
    )(flags, *operands)
    return flat.astype(jnp.float16)


def unpack(flat, target, rounds, columns, quarter):
    rows = flat.shape[0] - TAIL
    factor = jnp.exp2(flat[rows : rows + 1, :1] - 14.0)
    for k, place in enumerate(rounds):

        @pl.loop(0, quarter // STRIP)
        def _(i):
            target[place, strip(i), columns] = flat[strip(i + k * (quarter // STRIP))] * factor


def middle_kernel(scale, flags_ref, *refs):
    rows, nears, fars = [refs[:4], refs[4:8]], refs[8:12], refs[12:17]
    out_ref, row_buf, col_buf, row_sems, col_sems = refs[-5:]
    quarter, units = out_ref.shape[1:]
    half = 2 * quarter
    last_width = pieces_of(units)[2]
    low = flags_ref[0] == 1
    first = flags_ref[2]

    @pl.when(flags_ref[1] == 1)
    def _():
        at = own_start(low, quarter)
        starts = [[at, 0, at, 0], [at, quarter, 0, quarter]]
        for v in range(4):
            load_rows(rows, starts, row_buf, row_sems, v, quarter)
            buf, sem = col_buf.at[v], col_sems.at[v]
            load(nears[v], 0, half, buf, jnp.where(low, 0, half), sem)
            if v < 3:
                load(fars[v], 0, half, buf, jnp.where(low, half, 0), sem)
            else:
                load(fars[3], 0, half - last_width, buf, jnp.where(low, half, last_width), sem)
                load(fars[4], 0, last_width, buf, jnp.where(low, units - last_width, 0), sem)
        for k in range(2):
            clear(out_ref.at[k], quarter)

        def add(v, start, width):
            columns = pl.ds(start, width)
            total = times(row_buf[v], col_buf[v, columns]) * scale
            for k in range(2):
                out_ref[lax.bitwise_xor(first, k), :, columns] += total[k * quarter : (k + 1) * quarter]

        wide = 4 * LANES
        full = units // wide

        @pl.loop(0, 4)
        def _(v):
            wait_all(row_buf.at[v], row_sems.at[v])
            wait_all(col_buf.at[v], col_sems.at[v])

            @pl.loop(0, full)
            def _(i):
                add(v, pl.multiple_of(i * wide, wide), wide)

            if units % wide:
                add(v, full * wide, units % wide)


def middle_tiles(flags, rows, nears, fars, quarter, scale):
    tokens, units = rows[0][0].shape[1], 4 * quarter
    operands = [*sum(rows, []), *nears, *fars]
    return pl.pallas_call(
        functools.partial(middle_kernel, scale),
        out_shape=jax.ShapeDtypeStruct((2, quarter, units), jnp.float32),
        in_specs=[pl.BlockSpec(memory_space=pltpu.SMEM)] + [pl.BlockSpec(memory_space=pl.ANY)] * len(operands),
        out_specs=pl.BlockSpec(memory_space=pltpu.VMEM),
        scratch_shapes=[
            pltpu.VMEM((4, 2 * quarter, tokens), jnp.bfloat16),
            pltpu.VMEM((4, units, tokens), jnp.bfloat16),
            pltpu.SemaphoreType.DMA((4,)),
            pltpu.SemaphoreType.DMA((4,)),
        ],
        compiler_params=pltpu.CompilerParams(vmem_limit_bytes=MIDDLE_VMEM),
        cost_estimate=pl.CostEstimate(
            flops=16 * quarter * tokens * units, bytes_accessed=8 * (2 * quarter + units) * tokens, transcendentals=0
        ),
        name="middle_tiles",
    )(flags, *operands)


def place_kernel(starts, pieces, flags_ref, out_in, *refs):
    flats, (out_ref, buf, sem) = refs[:-3], refs[-3:]
    quarter, width = buf.shape[1:]
    low = flags_ref[0] == 1
    first = flags_ref[2]
    rounds = [first, 1 - first]

    def side(pair):
        return pl.multiple_of(jnp.where(low, *pair), LANES)

    @pl.when(flags_ref[1] == 0)
    def _():
        for flat, (masks, at) in zip(flats, pieces):
            unpack(flat, buf, [rounds[k] for k in masks], pl.ds(side(at), flat.shape[1]), quarter)
        copy = pltpu.make_async_copy(buf, out_ref.at[:, :, pl.ds(side(starts), width)], sem)
        copy.start()
        copy.wait()


def place_tiles(flags, out, flats, starts, pieces, width):
    return pl.pallas_call(
        functools.partial(place_kernel, starts, pieces),
        out_shape=jax.ShapeDtypeStruct(out.shape, out.dtype),
        in_specs=[
            pl.BlockSpec(memory_space=pltpu.SMEM),
            pl.BlockSpec(memory_space=pl.ANY),
            *[pl.BlockSpec(memory_space=pltpu.VMEM)] * len(flats),
        ],
        out_specs=pl.BlockSpec(memory_space=pl.ANY),
        scratch_shapes=[pltpu.VMEM((2, out.shape[1], width), jnp.float32), pltpu.SemaphoreType.DMA],
        input_output_aliases={1: 0},
        compiler_params=pltpu.CompilerParams(vmem_limit_bytes=EDGE_VMEM),
        cost_estimate=pl.CostEstimate(flops=0, bytes_accessed=6 * 832 * width, transcendentals=0),
        name="place_tiles",
    )(flags, out, *flats)


def line_branch(mask, top, scale):
    rest = top ^ mask

    def run(flags, w_near, w_far):
        quarter = w_near.shape[0] // 2
        units = 4 * quarter
        low = flags[0] == 1
        near_width, middle_width, last_width = pieces_of(units)

        def rows_of(x, start, size):
            return lax.dynamic_slice_in_dim(x, start, size, 0)

        def end_part(x):
            return rows_of(x, jnp.where(low, 0, quarter), quarter)

        def own_part(x):
            return rows_of(x, jnp.where(low, quarter, 0), quarter)

        def ends(x, y):
            return jnp.concatenate([end_part(x), end_part(y)])

        def owns(x, y):
            return jnp.concatenate([own_part(x), own_part(y)])

        f_near, e_far, wm, e_near = across(w_far), inward(w_far), partner(w_near, mask), inward(w_near)

        e_far, f_near, wm, w_near = gated((e_far, f_near, wm, w_near))
        g_near, f_far, fm, wt = across(e_far), across(w_near), partner(f_near, mask), partner(wm, rest)

        g_near, e_near, fm, wt, wm = gated((g_near, e_near, fm, wt, wm))
        gm_end, ft_end, e_ends = partner(end_part(g_near), mask), partner(end_part(fm), rest), inward(ends(wm, wt))
        gm_own = partner(own_part(g_near), mask)

        gm_end, ft_end = gated((gm_end, ft_end))
        gt_end = partner(gm_end, rest)

        gt_end, e_ends, gm_own, f_far, fm, wm, wt, e_near = gated((gt_end, e_ends, gm_own, f_far, fm, wm, wt, e_near))
        inner = 2 * quarter - last_width
        g_mid = across(rows_of(e_near, jnp.where(low, last_width, 0), inner))
        t_owns, e_owns = partner(jnp.concatenate([own_part(fm), gm_own]), rest), inward(owns(wm, wt))
        nears = [w_near, e_near, f_near, g_near]
        ends_m, ends_t = [wm, e_ends, fm, gm_end], [wt, e_ends, ft_end, gt_end]
        flat_m = edge_tiles(flags, [ends_m], nears, [], 0, 0, quarter, scale)
        sent_m = outward(flat_m)
        g_last = across(rows_of(e_near, jnp.where(low, 0, inner), last_width))
        ends_t, flat_m = gated((ends_t, flat_m))
        flat_t = edge_tiles(flags, [ends_t], nears, [], 1, 0, quarter, scale)

        g_mid, flat_t, sent_m = gated((g_mid, flat_t, sent_m))
        sent_t = outward(flat_t)
        fars = [w_far, e_far, f_far, g_mid]
        flat = edge_tiles(flags, [ends_m, ends_t], nears, fars, 0, 1, quarter, scale)
        sent = outward(flat)

        g_last, t_owns, e_owns, flat, sent_t = gated((g_last, t_owns, e_owns, flat, sent_t))
        fars = [w_far, e_far, f_far, g_last]
        last = outward(edge_tiles(flags, [ends_m, ends_t], [], fars, 0, 2, quarter, scale)).astype(jnp.float32)

        packed = [x.astype(jnp.float32) for x in (sent_m, sent_t, sent)]
        before = near_width + middle_width
        own = [[wm, e_owns, fm, gm_own], [wt, e_owns, t_owns, t_owns]]
        fars = [w_far, e_far, f_far, g_mid, g_last]
        out = middle_tiles(flags, own, nears, fars, quarter, scale)
        near_at, inner_at = (0, middle_width), (near_width, 0)
        pieces = [([0], near_at), ([1], near_at), ([0, 1], inner_at)]
        out = place_tiles(flags, out, packed, (0, last_width), pieces, before)
        return place_tiles(flags, out, [last], (before, 0), [([0, 1], (0, 0))], last_width)

    return run


def shards_line(activations, plan):
    tokens, units = activations.shape
    top = lax.axis_size("tensor") - 1
    scale = 1.0 / math.sqrt(tokens * LINE)
    place = lax.axis_index("dp")
    low = place < 2
    first = plan[0] == top
    flags = jnp.stack([low, (place == 1) | (place == 2), first]).astype(jnp.int32)
    top_half, bottom_half = jnp.split(activations.T, 2)
    halves = [jnp.where(low, top_half, bottom_half), jnp.where(low, bottom_half, top_half)]
    other = plan[0] + plan[1] - top
    return lax.switch(other - 1, [line_branch(m, top, scale) for m in range(1, top)], flags, *halves)


def solution(mesh):
    fast = mesh.shape["dp"] == LINE
    return jax.shard_map(
        shards_line if fast else shards_any,
        mesh=mesh,
        in_specs=(P("dp", "tensor"), P()),
        out_specs=P(None, "dp", "tensor"),
        check_vma=False,
    )
```

```python
import functools
import math

import jax
import jax.numpy as jnp
from jax import lax
from jax.experimental import pallas as pl
from jax.experimental.pallas import tpu as pltpu
from jax.sharding import PartitionSpec as P

ROUNDS = 2
LINE = 4
LANES = 128
STRIP = 104
TAIL = 16
EDGE_VMEM = 16 * 2**20
MIDDLE_VMEM = 24 * 2**20


def swapped(x, axis, apart):
    return lax.ppermute(x, axis, [(i, i ^ 1 << apart) for i in range(lax.axis_size(axis))])


def partner_panel(own, mask, width):
    current = own
    for bit in range(width):
        taken = jnp.bitwise_and(jnp.right_shift(mask, bit), 1) == 1
        current = jnp.where(taken, swapped(current, "tensor", bit), current)
    return current


def shards_any(activations, plan):
    width = lax.axis_size("tensor").bit_length() - 1
    scale = jnp.float32(1.0 / math.sqrt(activations.shape[0] * lax.axis_size("dp")))
    tiles = []
    for r in range(ROUNDS):
        other = partner_panel(activations, plan[r], width)
        tiles.append(
            lax.dot_general(other, activations, (((0,), (0,)), ((), ())), preferred_element_type=jnp.float32)
        )
    return lax.psum_scatter(jnp.stack(tiles), "dp", scatter_dimension=1, tiled=True) * scale


def inward(x):
    return lax.ppermute(x, "dp", [(0, 1), (3, 2)])


def across(x):
    return lax.ppermute(x, "dp", [(1, 2), (2, 1)])


def outward(x):
    return lax.ppermute(x, "dp", [(1, 0), (2, 3)])


def partner(x, mask):
    return lax.ppermute(x, "tensor", [(i, i ^ mask) for i in range(lax.axis_size("tensor"))])


def gated(values, *others):
    return lax.optimization_barrier((*values, *others))[: len(values)]


def strip(i):
    return pl.ds(pl.multiple_of(i * STRIP, 8), STRIP)


def times(rows, columns):
    return lax.dot_general(rows, columns, (((1,), (1,)), ((), ())), preferred_element_type=jnp.float32)


def end_start(low, quarter):
    return jnp.where(low, 0, quarter)


def own_start(low, quarter):
    return jnp.where(low, quarter, 0)


def pieces_of(units):
    near = units // 2 // LANES * LANES
    last = (units - near) // 2 // LANES * LANES
    return near, units - near - last, last


def cut(ref, start, size):
    return ref[pl.ds(pl.multiple_of(start, 16), size)]


class Columns:
    def __init__(self, low, quarter):
        self.low, self.half = low, 2 * quarter
        self.near_width, middle, self.last = pieces_of(4 * quarter)
        self.spill = self.half - self.near_width
        self.inner = middle - 2 * self.spill

    def near(self, block, start, size):
        return cut(block, jnp.where(self.low, 0, self.spill) + start, size)

    def seam(self, near, far):
        top = far.shape[0] - self.spill if far.shape[0] < self.half else self.half - self.spill
        inward = jnp.where(self.low, cut(near, self.near_width, self.spill), cut(far, top, self.spill))
        outward = jnp.where(self.low, cut(far, 0, self.spill), cut(near, 0, self.spill))
        return jnp.concatenate([inward, outward])

    def middle(self, far, start, size):
        past = self.last if far.shape[0] == self.half else 0
        return cut(far, jnp.where(self.low, self.spill, past) + start, size)

    def outer(self, far, start, size):
        past = self.half - self.last if far.shape[0] == self.half else 0
        return cut(far, jnp.where(self.low, past, 0) + start, size)


def joined(parts):
    return jnp.concatenate(parts) if len(parts) > 1 else parts[0]


def shares(places, total):
    done = 0
    for at, size in places:
        yield pl.ds(pl.multiple_of(at, LANES), size), size, total[:, done : done + size]
        done += size


def summed(rows, starts, quarter, columns):
    total = None
    for v in range(4):
        parts = [cut(r[v], start[v], quarter) for r, start in zip(rows, starts)]
        term = times(joined(parts), joined([c(v) for c in columns]))
        total = term if total is None else total + term
    return total


def edge_kernel(masks, mask, piece, scale, flags_ref, *refs):
    rows = [refs[4 * k : 4 * k + 4] for k in range(masks)]
    nears, fars = refs[4 * masks : -2][:4], refs[4 * masks : -2][-4:]
    out_ref, most = refs[-2:]
    height = out_ref.shape[0] - TAIL
    quarter = height // masks
    low = flags_ref[0] == 1

    @pl.when(flags_ref[1] == 1)
    def _():
        cols = Columns(low, quarter)
        at = end_start(low, quarter)
        starts = [[at, 0, 0, quarter], [at, 0, 0, 0]][mask : mask + masks]
        most[...] = jnp.zeros_like(most)

        def put(places, *columns):
            total = summed(rows, starts, quarter, columns)
            for at, size, part in shares(places, total):
                out_ref[:height, at] = part
                high = jnp.max(jnp.abs(part).reshape(height // 8, 8, size), axis=0)
                for i in range(size // LANES):
                    most[...] = jnp.maximum(most[...], high[:, i * LANES : (i + 1) * LANES])

        if piece == 0:
            for start, size in ((0, 4 * LANES), (4 * LANES, cols.near_width - 4 * LANES)):
                put([(start, size)], lambda v: cols.near(nears[v], start, size))
        elif piece == 1:
            seam = 2 * cols.spill
            put(
                [(jnp.where(low, 0, cols.inner), seam), (jnp.where(low, seam, 0), cols.inner)],
                lambda v: cols.seam(nears[v], fars[v]),
                lambda v: cols.middle(fars[v], 0, cols.inner),
            )
        else:
            put([(0, cols.last)], lambda v: cols.outer(fars[v], 0, cols.last))

        biggest = jnp.max(most[...], axis=(0, 1), keepdims=True)
        power = jnp.ceil(jnp.log2(jnp.maximum(biggest * scale, 1e-30)))
        factor = scale * jnp.exp2(14.0 - power)

        @pl.loop(0, height // STRIP)
        def _(i):
            out_ref[strip(i)] = out_ref[strip(i)] * factor

        out_ref[height:] = jnp.broadcast_to(power, (TAIL, out_ref.shape[1]))


def edge_tiles(flags, rows, nears, fars, mask, piece, quarter, scale):
    masks, tokens = len(rows), rows[0][0].shape[1]
    width = pieces_of(4 * quarter)[piece]
    operands = [*sum(rows, []), *nears, *fars]
    flat = pl.pallas_call(
        functools.partial(edge_kernel, masks, mask, piece, scale),
        out_shape=jax.ShapeDtypeStruct((masks * quarter + TAIL, width), jnp.float32),
        in_specs=[pl.BlockSpec(memory_space=pltpu.SMEM)] + [pl.BlockSpec(memory_space=pltpu.VMEM)] * len(operands),
        out_specs=pl.BlockSpec(memory_space=pltpu.VMEM),
        scratch_shapes=[pltpu.VMEM((8, LANES), jnp.float32)],
        compiler_params=pltpu.CompilerParams(vmem_limit_bytes=EDGE_VMEM),
        cost_estimate=pl.CostEstimate(
            flops=8 * masks * quarter * tokens * width,
            bytes_accessed=8 * (masks * quarter + width) * tokens,
            transcendentals=0,
        ),
        name="edge_tiles",
    )(flags, *operands)
    return flat.astype(jnp.float16)


def unpack(flat, target, rounds, columns, quarter):
    rows = flat.shape[0] - TAIL
    factor = jnp.exp2(flat[rows : rows + 1, :1] - 14.0)
    for k, place in enumerate(rounds):

        @pl.loop(0, quarter // STRIP)
        def _(i):
            target[place, strip(i), columns] = flat[strip(i + k * (quarter // STRIP))] * factor


def middle_kernel(scale, flags_ref, *refs):
    rows, nears, fars = [refs[:4], refs[4:8]], refs[8:12], refs[12:17]
    out_ref = refs[-1]
    quarter, units = out_ref.shape[1:]
    near_width, middle_width, last_width = pieces_of(units)
    low = flags_ref[0] == 1
    middle = flags_ref[1] == 1
    first = flags_ref[2]

    @pl.when(middle)
    def _():
        cols = Columns(low, quarter)
        at_own = own_start(low, quarter)
        starts = [[at_own, 0, 0, quarter], [at_own, quarter, 0, quarter]]

        def put(places, *columns):
            total = summed(rows, starts, quarter, columns) * scale
            for at, size, part in shares(places, total):
                for k in range(2):
                    out_ref[lax.bitwise_xor(first, k), :, at] = part[k * quarter : (k + 1) * quarter]

        wide, seam = 4 * LANES, 2 * cols.spill
        near_at = jnp.where(low, 0, units - near_width)
        middle_at = jnp.where(low, near_width + seam, last_width)
        last_at = jnp.where(low, units - last_width, 0)
        rest = near_width - wide
        put([(near_at, wide)], lambda v: cols.near(nears[v], 0, wide))
        put(
            [(near_at + wide, rest), (middle_at, wide - rest)],
            lambda v: cols.near(nears[v], wide, rest),
            lambda v: cols.middle(fars[v], 0, wide - rest),
        )
        left, taken = cols.inner - (wide - rest), wide - seam - (cols.inner - (wide - rest))
        put(
            [(near_width, seam), (middle_at + wide - rest, left), (last_at, taken)],
            lambda v: cols.seam(nears[v], fars[v]),
            lambda v: cols.middle(fars[v], wide - rest, left),
            lambda v: cols.outer(fars[v + v // 3], 0, taken),
        )
        put([(last_at + taken, last_width - taken)], lambda v: cols.outer(fars[v + v // 3], taken, last_width - taken))


def middle_tiles(flags, rows, nears, fars, quarter, scale):
    tokens, units = rows[0][0].shape[1], 4 * quarter
    operands = [*sum(rows, []), *nears, *fars]
    return pl.pallas_call(
        functools.partial(middle_kernel, scale),
        out_shape=jax.ShapeDtypeStruct((2, quarter, units), jnp.float32),
        in_specs=[pl.BlockSpec(memory_space=pltpu.SMEM)] + [pl.BlockSpec(memory_space=pltpu.VMEM)] * len(operands),
        out_specs=pl.BlockSpec(memory_space=pltpu.VMEM),
        compiler_params=pltpu.CompilerParams(vmem_limit_bytes=MIDDLE_VMEM),
        cost_estimate=pl.CostEstimate(
            flops=16 * quarter * tokens * units, bytes_accessed=8 * (2 * quarter + units) * tokens, transcendentals=0
        ),
        name="middle_tiles",
    )(flags, *operands)


def place_kernel(starts, pieces, flags_ref, out_in, *refs):
    flats, (out_ref, buf, sem) = refs[:-3], refs[-3:]
    quarter, width = buf.shape[1:]
    low = flags_ref[0] == 1
    first = flags_ref[2]
    rounds = [first, 1 - first]

    def side(pair):
        return pl.multiple_of(jnp.where(low, *pair), LANES)

    @pl.when(flags_ref[1] == 0)
    def _():
        for flat, (masks, at) in zip(flats, pieces):
            unpack(flat, buf, [rounds[k] for k in masks], pl.ds(side(at), flat.shape[1]), quarter)
        copy = pltpu.make_async_copy(buf, out_ref.at[:, :, pl.ds(side(starts), width)], sem)
        copy.start()
        copy.wait()


def place_tiles(flags, out, flats, starts, pieces, width):
    return pl.pallas_call(
        functools.partial(place_kernel, starts, pieces),
        out_shape=jax.ShapeDtypeStruct(out.shape, out.dtype),
        in_specs=[
            pl.BlockSpec(memory_space=pltpu.SMEM),
            pl.BlockSpec(memory_space=pl.ANY),
            *[pl.BlockSpec(memory_space=pltpu.VMEM)] * len(flats),
        ],
        out_specs=pl.BlockSpec(memory_space=pl.ANY),
        scratch_shapes=[pltpu.VMEM((2, out.shape[1], width), jnp.float32), pltpu.SemaphoreType.DMA],
        input_output_aliases={1: 0},
        compiler_params=pltpu.CompilerParams(vmem_limit_bytes=EDGE_VMEM),
        cost_estimate=pl.CostEstimate(flops=0, bytes_accessed=6 * 832 * width, transcendentals=0),
        name="place_tiles",
    )(flags, out, *flats)


def line_branch(hop, top, scale):
    rest = top ^ hop

    def run(flags, plain, w_near, w_far):
        quarter = w_near.shape[0] // 2
        low = flags[0] == 1
        near_width, middle_width, last_width = pieces_of(4 * quarter)

        def rows_of(x, start, size):
            return lax.dynamic_slice_in_dim(x, start, size, 0)

        def end_part(x):
            return rows_of(x, jnp.where(low, 0, quarter), quarter)

        def own_part(x):
            return rows_of(x, jnp.where(low, quarter, 0), quarter)

        def sibling(x, u):
            return partner(x if hop == top ^ 1 else u, 1)

        def masked(u, swapped_in):
            return jnp.where(plain == 1, u, swapped_in)

        f_near, e_far, wu, e_near = across(w_far), inward(w_far), partner(w_near, hop), inward(w_near)

        e_far, f_near, wu, w_near = gated((e_far, f_near, wu, w_near))
        g_near, f_far, fu, wv = across(e_far), across(w_near), partner(f_near, hop), partner(wu, rest)

        g_near, e_near, fu, wv, wu = gated((g_near, e_near, fu, wv, wu))
        gu_end, fv_end, ev_end = partner(end_part(g_near), hop), partner(end_part(fu), rest), inward(end_part(wv))
        w_swap = sibling(w_near, wu)

        gu_end, fv_end, ev_end, w_swap, g_near, fu = gated((gu_end, fv_end, ev_end, w_swap, g_near, fu))
        wm = masked(wu, w_swap)
        gv_end, gu_own, em_end = partner(gu_end, rest), partner(own_part(g_near), hop), inward(end_part(wm))
        u_ends = jnp.concatenate([end_part(fu), gu_end])
        swap_ends = sibling(jnp.concatenate([end_part(f_near), end_part(g_near)]), u_ends)

        gv_end, gu_own, em_end, f_far, swap_ends, e_near = gated((gv_end, gu_own, em_end, f_far, swap_ends, e_near))
        inner = 2 * quarter - last_width
        u_owns = jnp.concatenate([own_part(fu), gu_own])
        swap_owns = sibling(jnp.concatenate([own_part(f_near), own_part(g_near)]), u_owns)
        g_mid = across(rows_of(e_near, jnp.where(low, last_width, 0), inner))
        v_owns, e_owns = partner(u_owns, rest), inward(jnp.concatenate([own_part(wm), own_part(wv)]))

        swap_owns, gv_end = gated((swap_owns, gv_end))
        nears = [w_near, e_near, f_near, g_near]
        ends_v = [wv, ev_end, fv_end, gv_end]
        flat_v = edge_tiles(flags, [ends_v], nears, [], 1, 0, quarter, scale)
        sent_v = outward(flat_v)

        swap_ends, swap_owns, flat_v = gated((swap_ends, swap_owns, flat_v))
        g_last = across(rows_of(e_near, jnp.where(low, 0, inner), last_width))
        m_ends, m_owns = masked(u_ends, swap_ends), masked(u_owns, swap_owns)
        ends_m = [wm, em_end, m_ends, m_ends]
        flat_m = edge_tiles(flags, [ends_m], nears, [], 0, 0, quarter, scale)

        g_mid, flat_m, sent_v = gated((g_mid, flat_m, sent_v))
        sent_m = outward(flat_m)
        fars = [w_far, e_far, f_far, g_mid]
        flat = edge_tiles(flags, [ends_m, ends_v], nears, fars, 0, 1, quarter, scale)
        sent = outward(flat)

        g_last, v_owns, e_owns, flat, sent_m = gated((g_last, v_owns, e_owns, flat, sent_m))
        fars = [w_far, e_far, f_far, g_last]
        last = outward(edge_tiles(flags, [ends_m, ends_v], [], fars, 0, 2, quarter, scale)).astype(jnp.float32)

        packed = [x.astype(jnp.float32) for x in (sent_m, sent_v, sent)]
        before = near_width + middle_width
        own = [[wm, e_owns, m_owns, m_owns], [wv, e_owns, v_owns, v_owns]]
        fars = [w_far, e_far, f_far, g_mid, g_last]
        out = middle_tiles(flags, own, nears, fars, quarter, scale)
        near_at, inner_at = (0, middle_width), (near_width, 0)
        pieces = [([0], near_at), ([1], near_at), ([0, 1], inner_at)]
        out = place_tiles(flags, out, packed, (0, last_width), pieces, before)
        return place_tiles(flags, out, [last], (before, 0), [([0, 1], (0, 0))], last_width)

    return run


def shards_line(activations, plan):
    tokens, units = activations.shape
    top = lax.axis_size("tensor") - 1
    scale = 1.0 / math.sqrt(tokens * LINE)
    place = lax.axis_index("dp")
    low = place < 2
    first = plan[0] == top
    flags = jnp.stack([low, (place == 1) | (place == 2), first]).astype(jnp.int32)
    top_half, bottom_half = jnp.split(activations.T, 2)
    halves = [jnp.where(low, top_half, bottom_half), jnp.where(low, bottom_half, top_half)]
    mask = plan[0] + plan[1] - top
    chip = mask >> 1
    hop = jnp.where(chip == 0, top ^ 1, 2 * chip)
    plain = (mask == hop).astype(jnp.int32)
    branches = [line_branch(h, top, scale) for h in (2, 4, top ^ 1)]
    return lax.switch(hop // 2 - 1, branches, flags, plain, *halves)


def solution(mesh):
    fast = mesh.shape["dp"] == LINE and mesh.shape["tensor"] == 8
    return jax.shard_map(
        shards_line if fast else shards_any,
        mesh=mesh,
        in_specs=(P("dp", "tensor"), P()),
        out_specs=P(None, "dp", "tensor"),
        check_vma=False,
    )
```

```python
import functools
import math

import jax
import jax.numpy as jnp
from jax import lax
from jax.experimental import pallas as pl
from jax.experimental.pallas import tpu as pltpu
from jax.sharding import PartitionSpec as P

ROUNDS = 2
LINE = 4
LANES = 128
STRIP = 104
TAIL = 16
EDGE_VMEM = 16 * 2**20
MIDDLE_VMEM = 24 * 2**20


def swapped(x, axis, apart):
    return lax.ppermute(x, axis, [(i, i ^ 1 << apart) for i in range(lax.axis_size(axis))])


def partner_panel(own, mask, width):
    current = own
    for bit in range(width):
        taken = jnp.bitwise_and(jnp.right_shift(mask, bit), 1) == 1
        current = jnp.where(taken, swapped(current, "tensor", bit), current)
    return current


def shards_any(activations, plan):
    width = lax.axis_size("tensor").bit_length() - 1
    scale = jnp.float32(1.0 / math.sqrt(activations.shape[0] * lax.axis_size("dp")))
    tiles = []
    for r in range(ROUNDS):
        other = partner_panel(activations, plan[r], width)
        tiles.append(
            lax.dot_general(other, activations, (((0,), (0,)), ((), ())), preferred_element_type=jnp.float32)
        )
    return lax.psum_scatter(jnp.stack(tiles), "dp", scatter_dimension=1, tiled=True) * scale


def inward(x):
    return lax.ppermute(x, "dp", [(0, 1), (3, 2)])


def across(x):
    return lax.ppermute(x, "dp", [(1, 2), (2, 1)])


def outward(x):
    return lax.ppermute(x, "dp", [(1, 0), (2, 3)])


def partner(x, mask):
    return lax.ppermute(x, "tensor", [(i, i ^ mask) for i in range(lax.axis_size("tensor"))])


def gated(values, *others):
    return lax.optimization_barrier((*values, *others))[: len(values)]


def strip(i):
    return pl.ds(pl.multiple_of(i * STRIP, 8), STRIP)


def times(rows, columns):
    return lax.dot_general(rows, columns, (((1,), (1,)), ((), ())), preferred_element_type=jnp.float32)


def end_start(low, quarter):
    return jnp.where(low, 0, quarter)


def own_start(low, quarter):
    return jnp.where(low, quarter, 0)


def pieces_of(units):
    near = units // 2 // LANES * LANES
    middle = (units - near) // 2 // LANES * LANES
    return near, middle, units - near - middle


def cut(ref, start, size):
    return ref[pl.ds(pl.multiple_of(start, 16), size)]


class Columns:
    def __init__(self, low, quarter):
        self.low, self.half = low, 2 * quarter
        self.near_width, middle, self.last = pieces_of(4 * quarter)
        self.spill = self.half - self.near_width
        self.inner = middle - 2 * self.spill

    def near(self, block, start, size):
        return cut(block, jnp.where(self.low, 0, self.spill) + start, size)

    def seam(self, near, far):
        top = far.shape[0] - self.spill if far.shape[0] < self.half else self.half - self.spill
        inward = jnp.where(self.low, cut(near, self.near_width, self.spill), cut(far, top, self.spill))
        outward = jnp.where(self.low, cut(far, 0, self.spill), cut(near, 0, self.spill))
        return jnp.concatenate([inward, outward])

    def middle(self, far, start, size):
        past = self.last if far.shape[0] == self.half else 0
        return cut(far, jnp.where(self.low, self.spill, past) + start, size)

    def outer(self, far, start, size):
        past = self.half - self.last if far.shape[0] == self.half else 0
        return cut(far, jnp.where(self.low, past, 0) + start, size)


def joined(parts):
    return jnp.concatenate(parts) if len(parts) > 1 else parts[0]


def shares(places, total):
    done = 0
    for at, size in places:
        yield pl.ds(pl.multiple_of(at, LANES), size), size, total[:, done : done + size]
        done += size


def summed(rows, starts, quarter, columns):
    total = None
    for v in range(4):
        parts = [cut(r[v], start[v], quarter) for r, start in zip(rows, starts)]
        term = times(joined(parts), joined([c(v) for c in columns]))
        total = term if total is None else total + term
    return total


def edge_kernel(masks, mask, piece, scale, flags_ref, *refs):
    rows = [refs[4 * k : 4 * k + 4] for k in range(masks)]
    nears, fars = refs[4 * masks : -2][:4], refs[4 * masks : -2][-4:]
    out_ref, most = refs[-2:]
    height = out_ref.shape[0] - TAIL
    quarter = height // masks
    low = flags_ref[0] == 1

    @pl.when(flags_ref[1] == 1)
    def _():
        cols = Columns(low, quarter)
        at = end_start(low, quarter)
        starts = [[at, 0, 0, quarter], [at, 0, 0, 0]][mask : mask + masks]
        most[...] = jnp.zeros_like(most)

        def put(places, *columns):
            total = summed(rows, starts, quarter, columns)
            for at, size, part in shares(places, total):
                out_ref[:height, at] = part
                high = jnp.max(jnp.abs(part).reshape(height // 8, 8, size), axis=0)
                for i in range(size // LANES):
                    most[...] = jnp.maximum(most[...], high[:, i * LANES : (i + 1) * LANES])

        if piece == 0:
            for start, size in ((0, 4 * LANES), (4 * LANES, cols.near_width - 4 * LANES)):
                put([(start, size)], lambda v: cols.near(nears[v], start, size))
        elif piece == 1:
            seam = 2 * cols.spill
            put(
                [(jnp.where(low, 0, cols.inner), seam), (jnp.where(low, seam, 0), cols.inner)],
                lambda v: cols.seam(nears[v], fars[v]),
                lambda v: cols.middle(fars[v], 0, cols.inner),
            )
        else:
            put([(0, cols.last)], lambda v: cols.outer(fars[v], 0, cols.last))

        biggest = jnp.max(most[...], axis=(0, 1), keepdims=True)
        power = jnp.ceil(jnp.log2(jnp.maximum(biggest * scale, 1e-30)))
        factor = scale * jnp.exp2(14.0 - power)

        @pl.loop(0, height // STRIP)
        def _(i):
            out_ref[strip(i)] = out_ref[strip(i)] * factor

        out_ref[height:] = jnp.broadcast_to(power, (TAIL, out_ref.shape[1]))


def edge_tiles(flags, rows, nears, fars, mask, piece, quarter, scale):
    masks, tokens = len(rows), rows[0][0].shape[1]
    width = pieces_of(4 * quarter)[piece]
    operands = [*sum(rows, []), *nears, *fars]
    flat = pl.pallas_call(
        functools.partial(edge_kernel, masks, mask, piece, scale),
        out_shape=jax.ShapeDtypeStruct((masks * quarter + TAIL, width), jnp.float32),
        in_specs=[pl.BlockSpec(memory_space=pltpu.SMEM)] + [pl.BlockSpec(memory_space=pltpu.VMEM)] * len(operands),
        out_specs=pl.BlockSpec(memory_space=pltpu.VMEM),
        scratch_shapes=[pltpu.VMEM((8, LANES), jnp.float32)],
        compiler_params=pltpu.CompilerParams(vmem_limit_bytes=EDGE_VMEM),
        cost_estimate=pl.CostEstimate(
            flops=8 * masks * quarter * tokens * width,
            bytes_accessed=8 * (masks * quarter + width) * tokens,
            transcendentals=0,
        ),
        name="edge_tiles",
    )(flags, *operands)
    return flat.astype(jnp.float16)


def unpack(flat, target, rounds, columns, quarter):
    rows = flat.shape[0] - TAIL
    factor = jnp.exp2(flat[rows : rows + 1, :1] - 14.0)
    for k, place in enumerate(rounds):

        @pl.loop(0, quarter // STRIP)
        def _(i):
            target[place, strip(i), columns] = flat[strip(i + k * (quarter // STRIP))] * factor


def middle_kernel(scale, flags_ref, *refs):
    rows, nears, fars, packed = [refs[:4], refs[4:8]], refs[8:12], refs[12:17], refs[17:19]
    out_ref = refs[-1]
    quarter, units = out_ref.shape[1:]
    near_width, middle_width, last_width = pieces_of(units)
    low = flags_ref[0] == 1
    middle = flags_ref[1] == 1
    first = flags_ref[2]

    @pl.when(middle)
    def _():
        cols = Columns(low, quarter)
        at_own = own_start(low, quarter)
        starts = [[at_own, 0, 0, quarter], [at_own, quarter, 0, quarter]]

        def put(places, *columns):
            total = summed(rows, starts, quarter, columns) * scale
            for at, size, part in shares(places, total):
                for k in range(2):
                    out_ref[lax.bitwise_xor(first, k), :, at] = part[k * quarter : (k + 1) * quarter]

        wide, seam = 4 * LANES, 2 * cols.spill
        near_at = jnp.where(low, 0, units - near_width)
        middle_at = jnp.where(low, near_width + seam, last_width)
        last_at = jnp.where(low, units - last_width, 0)
        rest = near_width - wide
        put([(near_at, wide)], lambda v: cols.near(nears[v], 0, wide))
        put(
            [(near_at + wide, rest), (middle_at, cols.inner)],
            lambda v: cols.near(nears[v], wide, rest),
            lambda v: cols.middle(fars[v], 0, cols.inner),
        )
        taken = wide - seam
        put(
            [(near_width, seam), (last_at, taken)],
            lambda v: cols.seam(nears[v], fars[v]),
            lambda v: cols.outer(fars[v + v // 3], 0, taken),
        )
        put([(last_at + taken, last_width - taken)], lambda v: cols.outer(fars[v + v // 3], taken, last_width - taken))

    @pl.when(jnp.logical_not(middle))
    def _():
        near = pl.ds(pl.multiple_of(jnp.where(low, 0, units - near_width), LANES), near_width)
        unpack(packed[0], out_ref, [first], near, quarter)
        unpack(packed[1], out_ref, [1 - first], near, quarter)


def middle_tiles(flags, rows, nears, fars, packed, quarter, scale):
    tokens, units = rows[0][0].shape[1], 4 * quarter
    operands = [*sum(rows, []), *nears, *fars, *packed]
    return pl.pallas_call(
        functools.partial(middle_kernel, scale),
        out_shape=jax.ShapeDtypeStruct((2, quarter, units), jnp.float32),
        in_specs=[pl.BlockSpec(memory_space=pltpu.SMEM)] + [pl.BlockSpec(memory_space=pltpu.VMEM)] * len(operands),
        out_specs=pl.BlockSpec(memory_space=pltpu.VMEM),
        compiler_params=pltpu.CompilerParams(vmem_limit_bytes=MIDDLE_VMEM),
        cost_estimate=pl.CostEstimate(
            flops=16 * quarter * tokens * units, bytes_accessed=8 * (2 * quarter + units) * tokens, transcendentals=0
        ),
        name="middle_tiles",
    )(flags, *operands)


def place_kernel(starts, pieces, flags_ref, out_in, *refs):
    flats, (out_ref, buf, sem) = refs[:-3], refs[-3:]
    quarter, width = buf.shape[1:]
    low = flags_ref[0] == 1
    first = flags_ref[2]
    rounds = [first, 1 - first]

    def side(pair):
        return pl.multiple_of(jnp.where(low, *pair), LANES)

    @pl.when(flags_ref[1] == 0)
    def _():
        for flat, (masks, at) in zip(flats, pieces):
            unpack(flat, buf, [rounds[k] for k in masks], pl.ds(side(at), flat.shape[1]), quarter)
        copy = pltpu.make_async_copy(buf, out_ref.at[:, :, pl.ds(side(starts), width)], sem)
        copy.start()
        copy.wait()


def place_tiles(flags, out, flats, starts, pieces, width):
    return pl.pallas_call(
        functools.partial(place_kernel, starts, pieces),
        out_shape=jax.ShapeDtypeStruct(out.shape, out.dtype),
        in_specs=[
            pl.BlockSpec(memory_space=pltpu.SMEM),
            pl.BlockSpec(memory_space=pl.ANY),
            *[pl.BlockSpec(memory_space=pltpu.VMEM)] * len(flats),
        ],
        out_specs=pl.BlockSpec(memory_space=pl.ANY),
        scratch_shapes=[pltpu.VMEM((2, out.shape[1], width), jnp.float32), pltpu.SemaphoreType.DMA],
        input_output_aliases={1: 0},
        compiler_params=pltpu.CompilerParams(vmem_limit_bytes=EDGE_VMEM),
        cost_estimate=pl.CostEstimate(flops=0, bytes_accessed=6 * 832 * width, transcendentals=0),
        name="place_tiles",
    )(flags, out, *flats)


def line_branch(hop, top, scale):
    rest = top ^ hop

    def run(flags, core_only, all_but_core, hop_only, w_near, w_far):
        quarter = w_near.shape[0] // 2
        low = flags[0] == 1
        near_width, middle_width, last_width = pieces_of(4 * quarter)

        def rows_of(x, start, size):
            return lax.dynamic_slice_in_dim(x, start, size, 0)

        def end_part(x):
            return rows_of(x, jnp.where(low, 0, quarter), quarter)

        def own_part(x):
            return rows_of(x, jnp.where(low, quarter, 0), quarter)

        def sibling(x, u, v):
            return partner(jnp.where(core_only, x, jnp.where(all_but_core, v, u)), 1)

        def masked(u, swapped_in):
            return jnp.where(hop_only, u, swapped_in)

        f_near, e_far, wu, e_near = across(w_far), inward(w_far), partner(w_near, hop), inward(w_near)

        e_far, f_near, wu, w_near = gated((e_far, f_near, wu, w_near))
        g_near, f_far, fu, wv = across(e_far), across(w_near), partner(f_near, hop), partner(wu, rest)

        g_near, e_near, fu, wv, wu = gated((g_near, e_near, fu, wv, wu))
        gu_end, fv_end, ev_end = partner(end_part(g_near), hop), partner(end_part(fu), rest), inward(end_part(wv))
        w_swap = sibling(w_near, wu, wv)

        gu_end, fv_end, ev_end, w_swap, g_near = gated((gu_end, fv_end, ev_end, w_swap, g_near))
        wm = masked(wu, w_swap)
        gv_end, gu_own, em_end = partner(gu_end, rest), partner(own_part(g_near), hop), inward(end_part(wm))

        gv_end, gu_own, em_end, f_far, fu, e_near = gated((gv_end, gu_own, em_end, f_far, fu, e_near))
        nears = [w_near, e_near, f_near, g_near]
        ends_v = [wv, ev_end, fv_end, gv_end]
        flat_v = edge_tiles(flags, [ends_v], nears, [], 1, 0, quarter, scale)
        fu, gu_own, wm, flat_v = gated((fu, gu_own, wm, flat_v))
        sent_v = outward(flat_v)
        inner = 2 * quarter - last_width
        u_ends, u_owns = [jnp.concatenate(x) for x in ([end_part(fu), gu_end], [own_part(fu), gu_own])]
        x_ends, x_owns = [jnp.concatenate([part(f_near), part(g_near)]) for part in (end_part, own_part)]
        swap_ends = sibling(x_ends, u_ends, jnp.concatenate([fv_end, gv_end]))
        g_mid = across(rows_of(e_near, jnp.where(low, last_width, 0), inner))
        v_owns, e_owns = partner(u_owns, rest), inward(jnp.concatenate([own_part(wm), own_part(wv)]))

        swap_ends, flat_v = gated((swap_ends, flat_v))
        m_ends = masked(u_ends, swap_ends)
        g_last = across(rows_of(e_near, jnp.where(low, 0, inner), last_width))
        ends_m = [wm, em_end, m_ends, m_ends]
        flat_m = edge_tiles(flags, [ends_m], nears, [], 0, 0, quarter, scale)

        g_mid, flat_m, sent_v = gated((g_mid, flat_m, sent_v))
        sent_m = outward(flat_m)
        fars = [w_far, e_far, f_far, g_mid]
        flat = edge_tiles(flags, [ends_m, ends_v], nears, fars, 0, 1, quarter, scale)
        sent = outward(flat)

        g_last, flat = gated((g_last, flat))
        fars = [w_far, e_far, f_far, g_last]
        flat = edge_tiles(flags, [ends_m, ends_v], [], fars, 0, 2, quarter, scale)
        v_owns, e_owns, sent_m, sent, flat = gated((v_owns, e_owns, sent_m, sent, flat))
        last = outward(flat)
        swap_owns = sibling(x_owns, u_owns, v_owns)
        swap_owns, sent_m, sent_v, sent = gated((swap_owns, sent_m, sent_v, sent))
        m_owns = masked(u_owns, swap_owns)

        packed = [x.astype(jnp.float32) for x in (sent_m, sent_v)]
        own = [[wm, e_owns, m_owns, m_owns], [wv, e_owns, v_owns, v_owns]]
        fars = [w_far, e_far, f_far, g_mid, g_last]
        out = middle_tiles(flags, own, nears, fars, packed, quarter, scale)
        out = place_tiles(flags, out, [sent.astype(jnp.float32)], (near_width, last_width), [([0, 1], (0, 0))], middle_width)
        out, last = gated((out, last))
        before = near_width + middle_width
        return place_tiles(flags, out, [last.astype(jnp.float32)], (before, 0), [([0, 1], (0, 0))], last_width)

    return run


def shards_line(activations, plan):
    tokens, units = activations.shape
    top = lax.axis_size("tensor") - 1
    scale = 1.0 / math.sqrt(tokens * LINE)
    place = lax.axis_index("dp")
    low = place < 2
    first = plan[0] == top
    flags = jnp.stack([low, (place == 1) | (place == 2), first]).astype(jnp.int32)
    top_half, bottom_half = jnp.split(activations.T, 2)
    halves = [jnp.where(low, top_half, bottom_half), jnp.where(low, bottom_half, top_half)]
    mask = plan[0] + plan[1] - top
    high = (mask >> 1) == 2
    hop = jnp.where(high, 4, 2)
    picks = [mask == 1, mask == (top ^ 1), mask == hop]
    return lax.cond(high, line_branch(4, top, scale), line_branch(2, top, scale), flags, *picks, *halves)


def solution(mesh):
    fast = mesh.shape["dp"] == LINE and mesh.shape["tensor"] == 8
    return jax.shard_map(
        shards_line if fast else shards_any,
        mesh=mesh,
        in_specs=(P("dp", "tensor"), P()),
        out_specs=P(None, "dp", "tensor"),
        check_vma=False,
    )
```

```python
import functools
import math

import jax
import jax.numpy as jnp
from jax import lax
from jax.experimental import pallas as pl
from jax.experimental.pallas import tpu as pltpu
from jax.sharding import PartitionSpec as P

ROUNDS = 2
LINE = 4
LANES = 128
STRIP = 104
TAIL = 16
EDGE_VMEM = 16 * 2**20
MIDDLE_VMEM = 24 * 2**20


def swapped(x, axis, apart):
    return lax.ppermute(x, axis, [(i, i ^ 1 << apart) for i in range(lax.axis_size(axis))])


def partner_panel(own, mask, width):
    current = own
    for bit in range(width):
        taken = jnp.bitwise_and(jnp.right_shift(mask, bit), 1) == 1
        current = jnp.where(taken, swapped(current, "tensor", bit), current)
    return current


def shards_any(activations, plan):
    width = lax.axis_size("tensor").bit_length() - 1
    scale = jnp.float32(1.0 / math.sqrt(activations.shape[0] * lax.axis_size("dp")))
    tiles = []
    for r in range(ROUNDS):
        other = partner_panel(activations, plan[r], width)
        tiles.append(
            lax.dot_general(other, activations, (((0,), (0,)), ((), ())), preferred_element_type=jnp.float32)
        )
    return lax.psum_scatter(jnp.stack(tiles), "dp", scatter_dimension=1, tiled=True) * scale


def inward(x):
    return lax.ppermute(x, "dp", [(0, 1), (3, 2)])


def across(x):
    return lax.ppermute(x, "dp", [(1, 2), (2, 1)])


def outward(x):
    return lax.ppermute(x, "dp", [(1, 0), (2, 3)])


def partner(x, mask):
    return lax.ppermute(x, "tensor", [(i, i ^ mask) for i in range(lax.axis_size("tensor"))])


def gated(values, *others):
    return lax.optimization_barrier((*values, *others))[: len(values)]


def strip(i):
    return pl.ds(pl.multiple_of(i * STRIP, 8), STRIP)


def times(rows, columns):
    return lax.dot_general(rows, columns, (((1,), (1,)), ((), ())), preferred_element_type=jnp.float32)


def end_start(low, quarter):
    return jnp.where(low, 0, quarter)


def own_start(low, quarter):
    return jnp.where(low, quarter, 0)


def pieces_of(units):
    near = units // 2 // LANES * LANES
    middle = (units - near) // 2 // LANES * LANES
    return near, middle, units - near - middle


def cut(ref, start, size):
    return ref[pl.ds(pl.multiple_of(start, 16), size)]


class Columns:
    def __init__(self, low, quarter):
        self.low, self.half = low, 2 * quarter
        self.near_width, middle, self.last = pieces_of(4 * quarter)
        self.spill = self.half - self.near_width
        self.inner = middle - 2 * self.spill

    def near(self, block, start, size):
        return cut(block, jnp.where(self.low, 0, self.spill) + start, size)

    def seam(self, near, far):
        top = far.shape[0] - self.spill if far.shape[0] < self.half else self.half - self.spill
        inward = jnp.where(self.low, cut(near, self.near_width, self.spill), cut(far, top, self.spill))
        outward = jnp.where(self.low, cut(far, 0, self.spill), cut(near, 0, self.spill))
        return jnp.concatenate([inward, outward])

    def middle(self, far, start, size):
        past = self.last if far.shape[0] == self.half else 0
        return cut(far, jnp.where(self.low, self.spill, past) + start, size)

    def outer(self, far, start, size):
        past = self.half - self.last if far.shape[0] == self.half else 0
        return cut(far, jnp.where(self.low, past, 0) + start, size)


def joined(parts):
    return jnp.concatenate(parts) if len(parts) > 1 else parts[0]


def shares(places, total):
    done = 0
    for at, size in places:
        yield pl.ds(pl.multiple_of(at, LANES), size), size, total[:, done : done + size]
        done += size


def summed(rows, starts, quarter, columns):
    total = None
    for v in range(4):
        parts = [cut(r[v], start[v], quarter) for r, start in zip(rows, starts)]
        term = times(joined(parts), joined([c(v) for c in columns]))
        total = term if total is None else total + term
    return total


def edge_kernel(masks, mask, piece, scale, flags_ref, *refs):
    rows = [refs[4 * k : 4 * k + 4] for k in range(masks)]
    nears, fars = refs[4 * masks : -2][:4], refs[4 * masks : -2][-4:]
    out_ref, most = refs[-2:]
    height = out_ref.shape[0] - TAIL
    quarter = height // masks
    low = flags_ref[0] == 1

    @pl.when(flags_ref[1] == 1)
    def _():
        cols = Columns(low, quarter)
        at = end_start(low, quarter)
        starts = [[at, 0, 0, quarter], [at, 0, 0, 0]][mask : mask + masks]
        most[...] = jnp.zeros_like(most)

        def put(places, *columns):
            total = summed(rows, starts, quarter, columns)
            for at, size, part in shares(places, total):
                out_ref[:height, at] = part
                high = jnp.max(jnp.abs(part).reshape(height // 8, 8, size), axis=0)
                for i in range(size // LANES):
                    most[...] = jnp.maximum(most[...], high[:, i * LANES : (i + 1) * LANES])

        if piece == 0:
            for start, size in ((0, 4 * LANES), (4 * LANES, cols.near_width - 4 * LANES)):
                put([(start, size)], lambda v: cols.near(nears[v], start, size))
        elif piece == 1:
            seam = 2 * cols.spill
            put(
                [(jnp.where(low, 0, cols.inner), seam), (jnp.where(low, seam, 0), cols.inner)],
                lambda v: cols.seam(nears[v], fars[v]),
                lambda v: cols.middle(fars[v], 0, cols.inner),
            )
        else:
            put([(0, cols.last)], lambda v: cols.outer(fars[v], 0, cols.last))

        biggest = jnp.max(most[...], axis=(0, 1), keepdims=True)
        power = jnp.ceil(jnp.log2(jnp.maximum(biggest * scale, 1e-30)))
        factor = scale * jnp.exp2(14.0 - power)

        @pl.loop(0, height // STRIP)
        def _(i):
            out_ref[strip(i)] = out_ref[strip(i)] * factor

        out_ref[height:] = jnp.broadcast_to(power, (TAIL, out_ref.shape[1]))


def edge_tiles(flags, rows, nears, fars, mask, piece, quarter, scale):
    masks, tokens = len(rows), rows[0][0].shape[1]
    width = pieces_of(4 * quarter)[piece]
    operands = [*sum(rows, []), *nears, *fars]
    flat = pl.pallas_call(
        functools.partial(edge_kernel, masks, mask, piece, scale),
        out_shape=jax.ShapeDtypeStruct((masks * quarter + TAIL, width), jnp.float32),
        in_specs=[pl.BlockSpec(memory_space=pltpu.SMEM)] + [pl.BlockSpec(memory_space=pltpu.VMEM)] * len(operands),
        out_specs=pl.BlockSpec(memory_space=pltpu.VMEM),
        scratch_shapes=[pltpu.VMEM((8, LANES), jnp.float32)],
        compiler_params=pltpu.CompilerParams(vmem_limit_bytes=EDGE_VMEM),
        cost_estimate=pl.CostEstimate(
            flops=8 * masks * quarter * tokens * width,
            bytes_accessed=8 * (masks * quarter + width) * tokens,
            transcendentals=0,
        ),
        name="edge_tiles",
    )(flags, *operands)
    return flat.astype(jnp.float16)


def unpack(flat, target, rounds, columns, quarter):
    rows = flat.shape[0] - TAIL
    factor = jnp.exp2(flat[rows : rows + 1, :1] - 14.0)
    for k, place in enumerate(rounds):

        @pl.loop(0, quarter // STRIP)
        def _(i):
            target[place, strip(i), columns] = flat[strip(i + k * (quarter // STRIP))] * factor


def middle_kernel(scale, flags_ref, *refs):
    rows, nears, fars, packed = [refs[:4], refs[4:8]], refs[8:12], refs[12:17], refs[17:19]
    out_ref = refs[-1]
    quarter, units = out_ref.shape[1:]
    near_width, middle_width, last_width = pieces_of(units)
    low = flags_ref[0] == 1
    middle = flags_ref[1] == 1
    first = flags_ref[2]

    @pl.when(middle)
    def _():
        cols = Columns(low, quarter)
        at_own = own_start(low, quarter)
        starts = [[at_own, 0, 0, quarter], [at_own, quarter, 0, quarter]]

        def put(places, *columns):
            total = summed(rows, starts, quarter, columns) * scale
            for at, size, part in shares(places, total):
                for k in range(2):
                    out_ref[lax.bitwise_xor(first, k), :, at] = part[k * quarter : (k + 1) * quarter]

        wide, seam = 4 * LANES, 2 * cols.spill
        near_at = jnp.where(low, 0, units - near_width)
        middle_at = jnp.where(low, near_width + seam, last_width)
        last_at = jnp.where(low, units - last_width, 0)
        rest = near_width - wide
        put([(near_at, wide)], lambda v: cols.near(nears[v], 0, wide))
        put(
            [(near_at + wide, rest), (middle_at, cols.inner)],
            lambda v: cols.near(nears[v], wide, rest),
            lambda v: cols.middle(fars[v], 0, cols.inner),
        )
        taken = wide - seam
        put(
            [(near_width, seam), (last_at, taken)],
            lambda v: cols.seam(nears[v], fars[v]),
            lambda v: cols.outer(fars[v + v // 3], 0, taken),
        )
        put([(last_at + taken, last_width - taken)], lambda v: cols.outer(fars[v + v // 3], taken, last_width - taken))

    @pl.when(jnp.logical_not(middle))
    def _():
        near = pl.ds(pl.multiple_of(jnp.where(low, 0, units - near_width), LANES), near_width)
        unpack(packed[0], out_ref, [first], near, quarter)
        unpack(packed[1], out_ref, [1 - first], near, quarter)


def middle_tiles(flags, rows, nears, fars, packed, quarter, scale):
    tokens, units = rows[0][0].shape[1], 4 * quarter
    operands = [*sum(rows, []), *nears, *fars, *packed]
    return pl.pallas_call(
        functools.partial(middle_kernel, scale),
        out_shape=jax.ShapeDtypeStruct((2, quarter, units), jnp.float32),
        in_specs=[pl.BlockSpec(memory_space=pltpu.SMEM)] + [pl.BlockSpec(memory_space=pltpu.VMEM)] * len(operands),
        out_specs=pl.BlockSpec(memory_space=pltpu.VMEM),
        compiler_params=pltpu.CompilerParams(vmem_limit_bytes=MIDDLE_VMEM),
        cost_estimate=pl.CostEstimate(
            flops=16 * quarter * tokens * units, bytes_accessed=8 * (2 * quarter + units) * tokens, transcendentals=0
        ),
        name="middle_tiles",
    )(flags, *operands)


def place_kernel(starts, pieces, flags_ref, out_in, *refs):
    flats, (out_ref, buf, sem) = refs[:-3], refs[-3:]
    quarter, width = buf.shape[1:]
    low = flags_ref[0] == 1
    first = flags_ref[2]
    rounds = [first, 1 - first]

    def side(pair):
        return pl.multiple_of(jnp.where(low, *pair), LANES)

    @pl.when(flags_ref[1] == 0)
    def _():
        for flat, (masks, at) in zip(flats, pieces):
            unpack(flat, buf, [rounds[k] for k in masks], pl.ds(side(at), flat.shape[1]), quarter)
        copy = pltpu.make_async_copy(buf, out_ref.at[:, :, pl.ds(side(starts), width)], sem)
        copy.start()
        copy.wait()


def place_tiles(flags, out, flats, starts, pieces, width):
    return pl.pallas_call(
        functools.partial(place_kernel, starts, pieces),
        out_shape=jax.ShapeDtypeStruct(out.shape, out.dtype),
        in_specs=[
            pl.BlockSpec(memory_space=pltpu.SMEM),
            pl.BlockSpec(memory_space=pl.ANY),
            *[pl.BlockSpec(memory_space=pltpu.VMEM)] * len(flats),
        ],
        out_specs=pl.BlockSpec(memory_space=pl.ANY),
        scratch_shapes=[pltpu.VMEM((2, out.shape[1], width), jnp.float32), pltpu.SemaphoreType.DMA],
        input_output_aliases={1: 0},
        compiler_params=pltpu.CompilerParams(vmem_limit_bytes=EDGE_VMEM),
        cost_estimate=pl.CostEstimate(flops=0, bytes_accessed=6 * 832 * width, transcendentals=0),
        name="place_tiles",
    )(flags, out, *flats)


def line_branch(hop, top, scale):
    rest = top ^ hop

    def run(flags, core_only, all_but_core, hop_only, w_near, w_far):
        quarter = w_near.shape[0] // 2
        low = flags[0] == 1
        near_width, middle_width, last_width = pieces_of(4 * quarter)

        def rows_of(x, start, size):
            return lax.dynamic_slice_in_dim(x, start, size, 0)

        def end_part(x):
            return rows_of(x, jnp.where(low, 0, quarter), quarter)

        def own_part(x):
            return rows_of(x, jnp.where(low, quarter, 0), quarter)

        def sibling(x, u, v):
            return partner(jnp.where(core_only, x, jnp.where(all_but_core, v, u)), 1)

        def masked(u, swapped_in):
            return jnp.where(hop_only, u, swapped_in)

        f_near, e_far, wu, e_near = across(w_far), inward(w_far), partner(w_near, hop), inward(w_near)

        e_far, f_near, wu, w_near = gated((e_far, f_near, wu, w_near))
        g_near, f_far, fu, wv = across(e_far), across(w_near), partner(f_near, hop), partner(wu, rest)

        g_near, e_near, fu, wv, wu = gated((g_near, e_near, fu, wv, wu))
        gu_end, fv_end, ev_end = partner(end_part(g_near), hop), partner(end_part(fu), rest), inward(end_part(wv))
        w_swap = sibling(w_near, wu, wv)

        gu_end, fv_end, ev_end, w_swap, g_near = gated((gu_end, fv_end, ev_end, w_swap, g_near))
        wm = masked(wu, w_swap)
        gv_end, gu_own, em_end = partner(gu_end, rest), partner(own_part(g_near), hop), inward(end_part(wm))

        gv_end, gu_own, em_end, f_far, fu, e_near = gated((gv_end, gu_own, em_end, f_far, fu, e_near))
        nears = [w_near, e_near, f_near, g_near]
        ends_v = [wv, ev_end, fv_end, gv_end]
        flat_v = edge_tiles(flags, [ends_v], nears, [], 1, 0, quarter, scale)
        fu, gu_own, wm, flat_v = gated((fu, gu_own, wm, flat_v))
        sent_v = outward(flat_v)
        inner = 2 * quarter - last_width
        u_ends, u_owns = [jnp.concatenate(x) for x in ([end_part(fu), gu_end], [own_part(fu), gu_own])]
        x_ends, x_owns = [jnp.concatenate([part(f_near), part(g_near)]) for part in (end_part, own_part)]
        swap_ends = sibling(x_ends, u_ends, jnp.concatenate([fv_end, gv_end]))
        g_mid = across(rows_of(e_near, jnp.where(low, last_width, 0), inner))
        v_owns, e_owns = partner(u_owns, rest), inward(jnp.concatenate([own_part(wm), own_part(wv)]))

        swap_ends, flat_v = gated((swap_ends, flat_v))
        m_ends = masked(u_ends, swap_ends)
        g_last = across(rows_of(e_near, jnp.where(low, 0, inner), last_width))
        ends_m = [wm, em_end, m_ends, m_ends]
        flat_m = edge_tiles(flags, [ends_m], nears, [], 0, 0, quarter, scale)

        g_mid, flat_m, sent_v = gated((g_mid, flat_m, sent_v))
        sent_m = outward(flat_m)
        fars = [w_far, e_far, f_far, g_mid]
        flat = edge_tiles(flags, [ends_m, ends_v], nears, fars, 0, 1, quarter, scale)
        sent = outward(flat)

        g_last, flat = gated((g_last, flat))
        fars = [w_far, e_far, f_far, g_last]
        flat = edge_tiles(flags, [ends_m, ends_v], [], fars, 0, 2, quarter, scale)
        v_owns, e_owns, sent_m, sent, flat = gated((v_owns, e_owns, sent_m, sent, flat))
        last = outward(flat)
        swap_owns = sibling(x_owns, u_owns, v_owns)
        m_owns = masked(u_owns, swap_owns)

        packed = [x.astype(jnp.float32) for x in (sent_m, sent_v)]
        own = [[wm, e_owns, m_owns, m_owns], [wv, e_owns, v_owns, v_owns]]
        fars = [w_far, e_far, f_far, g_mid, g_last]
        out = middle_tiles(flags, own, nears, fars, packed, quarter, scale)
        out, sent, last = gated((out, sent, last))
        pieces = [([0, 1], (0, last_width)), ([0, 1], (middle_width, 0))]
        return place_tiles(
            flags, out, [sent.astype(jnp.float32), last.astype(jnp.float32)], (near_width, 0), pieces, middle_width + last_width
        )

    return run


def shards_line(activations, plan):
    tokens, units = activations.shape
    top = lax.axis_size("tensor") - 1
    scale = 1.0 / math.sqrt(tokens * LINE)
    place = lax.axis_index("dp")
    low = place < 2
    first = plan[0] == top
    flags = jnp.stack([low, (place == 1) | (place == 2), first]).astype(jnp.int32)
    top_half, bottom_half = jnp.split(activations.T, 2)
    halves = [jnp.where(low, top_half, bottom_half), jnp.where(low, bottom_half, top_half)]
    mask = plan[0] + plan[1] - top
    high = (mask >> 1) == 2
    hop = jnp.where(high, 4, 2)
    picks = [mask == 1, mask == (top ^ 1), mask == hop]
    return lax.cond(high, line_branch(4, top, scale), line_branch(2, top, scale), flags, *picks, *halves)


def solution(mesh):
    fast = mesh.shape["dp"] == LINE and mesh.shape["tensor"] == 8
    return jax.shard_map(
        shards_line if fast else shards_any,
        mesh=mesh,
        in_specs=(P("dp", "tensor"), P()),
        out_specs=P(None, "dp", "tensor"),
        check_vma=False,
    )
```

```python
import functools
import math

import jax
import jax.numpy as jnp
from jax import lax
from jax.experimental import pallas as pl
from jax.experimental.pallas import tpu as pltpu
from jax.sharding import PartitionSpec as P

ROUNDS = 2
LINE = 4
LANES = 128
STRIP = 104
TAIL = 16
EDGE_VMEM = 16 * 2**20
MIDDLE_VMEM = 24 * 2**20


def swapped(x, axis, apart):
    return lax.ppermute(x, axis, [(i, i ^ 1 << apart) for i in range(lax.axis_size(axis))])


def partner_panel(own, mask, width):
    current = own
    for bit in range(width):
        taken = jnp.bitwise_and(jnp.right_shift(mask, bit), 1) == 1
        current = jnp.where(taken, swapped(current, "tensor", bit), current)
    return current


def shards_any(activations, plan):
    width = lax.axis_size("tensor").bit_length() - 1
    scale = jnp.float32(1.0 / math.sqrt(activations.shape[0] * lax.axis_size("dp")))
    tiles = []
    for r in range(ROUNDS):
        other = partner_panel(activations, plan[r], width)
        tiles.append(
            lax.dot_general(other, activations, (((0,), (0,)), ((), ())), preferred_element_type=jnp.float32)
        )
    return lax.psum_scatter(jnp.stack(tiles), "dp", scatter_dimension=1, tiled=True) * scale


def inward(x):
    return lax.ppermute(x, "dp", [(0, 1), (3, 2)])


def across(x):
    return lax.ppermute(x, "dp", [(1, 2), (2, 1)])


def outward(x):
    return lax.ppermute(x, "dp", [(1, 0), (2, 3)])


def partner(x, mask):
    return lax.ppermute(x, "tensor", [(i, i ^ mask) for i in range(lax.axis_size("tensor"))])


def gated(values, *others):
    return lax.optimization_barrier((*values, *others))[: len(values)]


def strip(i):
    return pl.ds(pl.multiple_of(i * STRIP, 8), STRIP)


def times(rows, columns):
    return lax.dot_general(rows, columns, (((1,), (1,)), ((), ())), preferred_element_type=jnp.float32)


def end_start(low, quarter):
    return jnp.where(low, 0, quarter)


def own_start(low, quarter):
    return jnp.where(low, quarter, 0)


def pieces_of(units):
    near = units // 2 // LANES * LANES
    middle = (units - near) // 2 // LANES * LANES
    return near, middle, units - near - middle


def cut(ref, start, size):
    return ref[pl.ds(pl.multiple_of(start, 16), size)]


class Columns:
    def __init__(self, low, quarter):
        self.low, self.half = low, 2 * quarter
        self.near_width, middle, self.last = pieces_of(4 * quarter)
        self.spill = self.half - self.near_width
        self.inner = middle - 2 * self.spill

    def near(self, block, start, size):
        return cut(block, jnp.where(self.low, 0, self.spill) + start, size)

    def seam(self, near, far):
        top = far.shape[0] - self.spill if far.shape[0] < self.half else self.half - self.spill
        inward = jnp.where(self.low, cut(near, self.near_width, self.spill), cut(far, top, self.spill))
        outward = jnp.where(self.low, cut(far, 0, self.spill), cut(near, 0, self.spill))
        return jnp.concatenate([inward, outward])

    def middle(self, far, start, size):
        past = self.last if far.shape[0] == self.half else 0
        return cut(far, jnp.where(self.low, self.spill, past) + start, size)

    def outer(self, far, start, size):
        past = self.half - self.last if far.shape[0] == self.half else 0
        return cut(far, jnp.where(self.low, past, 0) + start, size)


def joined(parts):
    return jnp.concatenate(parts) if len(parts) > 1 else parts[0]


def shares(places, total):
    done = 0
    for at, size in places:
        yield pl.ds(pl.multiple_of(at, LANES), size), size, total[:, done : done + size]
        done += size


def summed(rows, starts, quarter, columns):
    total = None
    for v in range(4):
        parts = [cut(r[v], start[v], quarter) for r, start in zip(rows, starts)]
        term = times(joined(parts), joined([c(v) for c in columns]))
        total = term if total is None else total + term
    return total


def edge_kernel(masks, mask, piece, scale, flags_ref, *refs):
    rows = [refs[4 * k : 4 * k + 4] for k in range(masks)]
    nears, fars = refs[4 * masks : -2][:4], refs[4 * masks : -2][-4:]
    out_ref, most = refs[-2:]
    height = out_ref.shape[0] - TAIL
    quarter = height // masks
    low = flags_ref[0] == 1

    @pl.when(flags_ref[1] == 1)
    def _():
        cols = Columns(low, quarter)
        at = end_start(low, quarter)
        starts = [[at, 0, 0, quarter], [at, 0, 0, 0]][mask : mask + masks]
        most[...] = jnp.zeros_like(most)

        def put(places, *columns):
            total = summed(rows, starts, quarter, columns)
            for at, size, part in shares(places, total):
                out_ref[:height, at] = part
                high = jnp.max(jnp.abs(part).reshape(height // 8, 8, size), axis=0)
                for i in range(size // LANES):
                    most[...] = jnp.maximum(most[...], high[:, i * LANES : (i + 1) * LANES])

        if piece == 0:
            for start, size in ((0, 4 * LANES), (4 * LANES, cols.near_width - 4 * LANES)):
                put([(start, size)], lambda v: cols.near(nears[v], start, size))
        elif piece == 1:
            seam = 2 * cols.spill
            put(
                [(jnp.where(low, 0, cols.inner), seam), (jnp.where(low, seam, 0), cols.inner)],
                lambda v: cols.seam(nears[v], fars[v]),
                lambda v: cols.middle(fars[v], 0, cols.inner),
            )
        else:
            put([(0, cols.last)], lambda v: cols.outer(fars[v], 0, cols.last))

        biggest = jnp.max(most[...], axis=(0, 1), keepdims=True)
        power = jnp.ceil(jnp.log2(jnp.maximum(biggest * scale, 1e-30)))
        factor = scale * jnp.exp2(14.0 - power)

        @pl.loop(0, height // STRIP)
        def _(i):
            out_ref[strip(i)] = out_ref[strip(i)] * factor

        out_ref[height:] = jnp.broadcast_to(power, (TAIL, out_ref.shape[1]))


def edge_tiles(flags, rows, nears, fars, mask, piece, quarter, scale):
    masks, tokens = len(rows), rows[0][0].shape[1]
    width = pieces_of(4 * quarter)[piece]
    operands = [*sum(rows, []), *nears, *fars]
    flat = pl.pallas_call(
        functools.partial(edge_kernel, masks, mask, piece, scale),
        out_shape=jax.ShapeDtypeStruct((masks * quarter + TAIL, width), jnp.float32),
        in_specs=[pl.BlockSpec(memory_space=pltpu.SMEM)] + [pl.BlockSpec(memory_space=pltpu.VMEM)] * len(operands),
        out_specs=pl.BlockSpec(memory_space=pltpu.VMEM),
        scratch_shapes=[pltpu.VMEM((8, LANES), jnp.float32)],
        compiler_params=pltpu.CompilerParams(vmem_limit_bytes=EDGE_VMEM),
        cost_estimate=pl.CostEstimate(
            flops=8 * masks * quarter * tokens * width,
            bytes_accessed=8 * (masks * quarter + width) * tokens,
            transcendentals=0,
        ),
        name="edge_tiles",
    )(flags, *operands)
    return flat.astype(jnp.float16)


def unpack(flat, target, rounds, columns, quarter):
    rows = flat.shape[0] - TAIL
    factor = jnp.exp2(flat[rows : rows + 1, :1] - 14.0)
    for k, place in enumerate(rounds):

        @pl.loop(0, quarter // STRIP)
        def _(i):
            target[place, strip(i), columns] = flat[strip(i + k * (quarter // STRIP))] * factor


def middle_kernel(scale, flags_ref, *refs):
    rows, nears, fars, packed = [refs[:4], refs[4:8]], refs[8:12], refs[12:17], refs[17:19]
    out_ref = refs[-1]
    quarter, units = out_ref.shape[1:]
    near_width, middle_width, last_width = pieces_of(units)
    low = flags_ref[0] == 1
    middle = flags_ref[1] == 1
    first = flags_ref[2]

    @pl.when(middle)
    def _():
        cols = Columns(low, quarter)
        at_own = own_start(low, quarter)
        starts = [[at_own, 0, 0, quarter], [at_own, quarter, 0, quarter]]

        def put(places, *columns):
            total = summed(rows, starts, quarter, columns) * scale
            for at, size, part in shares(places, total):
                for k in range(2):
                    out_ref[lax.bitwise_xor(first, k), :, at] = part[k * quarter : (k + 1) * quarter]

        wide, seam = 4 * LANES, 2 * cols.spill
        near_at = jnp.where(low, 0, units - near_width)
        middle_at = jnp.where(low, near_width + seam, last_width)
        last_at = jnp.where(low, units - last_width, 0)
        rest = near_width - wide
        put([(near_at, wide)], lambda v: cols.near(nears[v], 0, wide))
        put(
            [(near_at + wide, rest), (middle_at, cols.inner)],
            lambda v: cols.near(nears[v], wide, rest),
            lambda v: cols.middle(fars[v], 0, cols.inner),
        )
        taken = wide - seam
        put(
            [(near_width, seam), (last_at, taken)],
            lambda v: cols.seam(nears[v], fars[v]),
            lambda v: cols.outer(fars[v + v // 3], 0, taken),
        )
        put([(last_at + taken, last_width - taken)], lambda v: cols.outer(fars[v + v // 3], taken, last_width - taken))

    @pl.when(jnp.logical_not(middle))
    def _():
        near = pl.ds(pl.multiple_of(jnp.where(low, 0, units - near_width), LANES), near_width)
        unpack(packed[0], out_ref, [first], near, quarter)
        unpack(packed[1], out_ref, [1 - first], near, quarter)


def middle_tiles(flags, rows, nears, fars, packed, quarter, scale):
    tokens, units = rows[0][0].shape[1], 4 * quarter
    operands = [*sum(rows, []), *nears, *fars, *packed]
    return pl.pallas_call(
        functools.partial(middle_kernel, scale),
        out_shape=jax.ShapeDtypeStruct((2, quarter, units), jnp.float32),
        in_specs=[pl.BlockSpec(memory_space=pltpu.SMEM)] + [pl.BlockSpec(memory_space=pltpu.VMEM)] * len(operands),
        out_specs=pl.BlockSpec(memory_space=pltpu.VMEM),
        compiler_params=pltpu.CompilerParams(vmem_limit_bytes=MIDDLE_VMEM),
        cost_estimate=pl.CostEstimate(
            flops=16 * quarter * tokens * units, bytes_accessed=8 * (2 * quarter + units) * tokens, transcendentals=0
        ),
        name="middle_tiles",
    )(flags, *operands)


def place_kernel(starts, pieces, flags_ref, out_in, *refs):
    flats, (out_ref, buf, sem) = refs[:-3], refs[-3:]
    quarter, width = buf.shape[1:]
    low = flags_ref[0] == 1
    first = flags_ref[2]
    rounds = [first, 1 - first]

    def side(pair):
        return pl.multiple_of(jnp.where(low, *pair), LANES)

    @pl.when(flags_ref[1] == 0)
    def _():
        for flat, (masks, at) in zip(flats, pieces):
            unpack(flat, buf, [rounds[k] for k in masks], pl.ds(side(at), flat.shape[1]), quarter)
        copy = pltpu.make_async_copy(buf, out_ref.at[:, :, pl.ds(side(starts), width)], sem)
        copy.start()
        copy.wait()


def place_tiles(flags, out, flats, starts, pieces, width):
    return pl.pallas_call(
        functools.partial(place_kernel, starts, pieces),
        out_shape=jax.ShapeDtypeStruct(out.shape, out.dtype),
        in_specs=[
            pl.BlockSpec(memory_space=pltpu.SMEM),
            pl.BlockSpec(memory_space=pl.ANY),
            *[pl.BlockSpec(memory_space=pltpu.VMEM)] * len(flats),
        ],
        out_specs=pl.BlockSpec(memory_space=pl.ANY),
        scratch_shapes=[pltpu.VMEM((2, out.shape[1], width), jnp.float32), pltpu.SemaphoreType.DMA],
        input_output_aliases={1: 0},
        compiler_params=pltpu.CompilerParams(vmem_limit_bytes=EDGE_VMEM),
        cost_estimate=pl.CostEstimate(flops=0, bytes_accessed=6 * 832 * width, transcendentals=0),
        name="place_tiles",
    )(flags, out, *flats)


def line_branch(hop, top, scale):
    rest = top ^ hop

    def run(flags, picks, w_near, w_far):
        quarter = w_near.shape[0] // 2
        low = flags[0] == 1
        near_width, middle_width, last_width = pieces_of(4 * quarter)

        def rows_of(x, start, size):
            return lax.dynamic_slice_in_dim(x, start, size, 0)

        def end_part(x):
            return rows_of(x, jnp.where(low, 0, quarter), quarter)

        def own_part(x):
            return rows_of(x, jnp.where(low, quarter, 0), quarter)

        def sibling(x, u, v):
            return partner(jnp.where(picks[0] == 1, x, jnp.where(picks[1] == 1, v, u)), 1)

        def masked(u, swapped_in):
            return jnp.where(picks[2] == 1, u, swapped_in)

        f_near, e_far, wu, e_near = across(w_far), inward(w_far), partner(w_near, hop), inward(w_near)

        e_far, f_near, wu, w_near = gated((e_far, f_near, wu, w_near))
        g_near, f_far, fu, wv = across(e_far), across(w_near), partner(f_near, hop), partner(wu, rest)

        g_near, e_near, fu, wv, wu = gated((g_near, e_near, fu, wv, wu))
        gu_end, fv_end, ev_end = partner(end_part(g_near), hop), partner(end_part(fu), rest), inward(end_part(wv))
        w_swap = sibling(w_near, wu, wv)

        gu_end, fv_end, ev_end, w_swap, g_near = gated((gu_end, fv_end, ev_end, w_swap, g_near))
        wm = masked(wu, w_swap)
        gv_end, gu_own, em_end = partner(gu_end, rest), partner(own_part(g_near), hop), inward(end_part(wm))

        gv_end, gu_own, em_end, f_far, fu, e_near = gated((gv_end, gu_own, em_end, f_far, fu, e_near))
        nears = [w_near, e_near, f_near, g_near]
        ends_v = [wv, ev_end, fv_end, gv_end]
        flat_v = edge_tiles(flags, [ends_v], nears, [], 1, 0, quarter, scale)
        fu, gu_own, wm, flat_v = gated((fu, gu_own, wm, flat_v))
        sent_v = outward(flat_v)
        inner = 2 * quarter - last_width
        u_ends, u_owns = [jnp.concatenate(x) for x in ([end_part(fu), gu_end], [own_part(fu), gu_own])]
        x_ends, x_owns = [jnp.concatenate([part(f_near), part(g_near)]) for part in (end_part, own_part)]
        swap_ends = sibling(x_ends, u_ends, jnp.concatenate([fv_end, gv_end]))
        g_mid = across(rows_of(e_near, jnp.where(low, last_width, 0), inner))
        v_owns, e_owns = partner(u_owns, rest), inward(jnp.concatenate([own_part(wm), own_part(wv)]))

        swap_ends, flat_v = gated((swap_ends, flat_v))
        m_ends = masked(u_ends, swap_ends)
        g_last = across(rows_of(e_near, jnp.where(low, 0, inner), last_width))
        ends_m = [wm, em_end, m_ends, m_ends]
        flat_m = edge_tiles(flags, [ends_m], nears, [], 0, 0, quarter, scale)

        g_mid, flat_m, sent_v = gated((g_mid, flat_m, sent_v))
        sent_m = outward(flat_m)
        fars = [w_far, e_far, f_far, g_mid]
        flat = edge_tiles(flags, [ends_m, ends_v], nears, fars, 0, 1, quarter, scale)
        sent = outward(flat)

        g_last, flat = gated((g_last, flat))
        fars = [w_far, e_far, f_far, g_last]
        flat = edge_tiles(flags, [ends_m, ends_v], [], fars, 0, 2, quarter, scale)
        v_owns, e_owns, sent_m, sent, flat = gated((v_owns, e_owns, sent_m, sent, flat))
        last = outward(flat)
        swap_owns = sibling(x_owns, u_owns, v_owns)
        swap_owns, sent_m, sent_v, sent = gated((swap_owns, sent_m, sent_v, sent))
        m_owns = masked(u_owns, swap_owns)

        packed = [x.astype(jnp.float32) for x in (sent_m, sent_v)]
        own = [[wm, e_owns, m_owns, m_owns], [wv, e_owns, v_owns, v_owns]]
        fars = [w_far, e_far, f_far, g_mid, g_last]
        out = middle_tiles(flags, own, nears, fars, packed, quarter, scale)
        out = place_tiles(flags, out, [sent.astype(jnp.float32)], (near_width, last_width), [([0, 1], (0, 0))], middle_width)
        out, last = gated((out, last))
        before = near_width + middle_width
        return place_tiles(flags, out, [last.astype(jnp.float32)], (before, 0), [([0, 1], (0, 0))], last_width)

    return run


def shards_line(activations, plan):
    tokens, units = activations.shape
    top = lax.axis_size("tensor") - 1
    scale = 1.0 / math.sqrt(tokens * LINE)
    place = lax.axis_index("dp")
    low = place < 2
    first = plan[0] == top
    flags = jnp.stack([low, (place == 1) | (place == 2), first]).astype(jnp.int32)
    top_half, bottom_half = jnp.split(activations.T, 2)
    halves = [jnp.where(low, top_half, bottom_half), jnp.where(low, bottom_half, top_half)]
    mask = plan[0] + plan[1] - top
    high = (mask >> 1) == 2
    hop = jnp.where(high, 4, 2)
    picks = jnp.stack([mask == 1, mask == (top ^ 1), mask == hop]).astype(jnp.int32)
    return lax.cond(high, line_branch(4, top, scale), line_branch(2, top, scale), flags, picks, *halves)


def solution(mesh):
    fast = mesh.shape["dp"] == LINE and mesh.shape["tensor"] == 8
    return jax.shard_map(
        shards_line if fast else shards_any,
        mesh=mesh,
        in_specs=(P("dp", "tensor"), P()),
        out_specs=P(None, "dp", "tensor"),
        check_vma=False,
    )
```

```python
import functools
import math

import jax
import jax.numpy as jnp
from jax import lax
from jax.experimental import pallas as pl
from jax.experimental.pallas import tpu as pltpu
from jax.sharding import PartitionSpec as P

ROUNDS = 2
LINE = 4
LANES = 128
STRIP = 104
TAIL = 16
EDGE_VMEM = 16 * 2**20
MIDDLE_VMEM = 24 * 2**20


def swapped(x, axis, apart):
    return lax.ppermute(x, axis, [(i, i ^ 1 << apart) for i in range(lax.axis_size(axis))])


def partner_panel(own, mask, width):
    current = own
    for bit in range(width):
        taken = jnp.bitwise_and(jnp.right_shift(mask, bit), 1) == 1
        current = jnp.where(taken, swapped(current, "tensor", bit), current)
    return current


def shards_any(activations, plan):
    width = lax.axis_size("tensor").bit_length() - 1
    scale = jnp.float32(1.0 / math.sqrt(activations.shape[0] * lax.axis_size("dp")))
    tiles = []
    for r in range(ROUNDS):
        other = partner_panel(activations, plan[r], width)
        tiles.append(
            lax.dot_general(other, activations, (((0,), (0,)), ((), ())), preferred_element_type=jnp.float32)
        )
    return lax.psum_scatter(jnp.stack(tiles), "dp", scatter_dimension=1, tiled=True) * scale


def inward(x):
    return lax.ppermute(x, "dp", [(0, 1), (3, 2)])


def across(x):
    return lax.ppermute(x, "dp", [(1, 2), (2, 1)])


def outward(x):
    return lax.ppermute(x, "dp", [(1, 0), (2, 3)])


def partner(x, mask):
    return lax.ppermute(x, "tensor", [(i, i ^ mask) for i in range(lax.axis_size("tensor"))])


def gated(values, *others):
    return lax.optimization_barrier((*values, *others))[: len(values)]


def strip(i):
    return pl.ds(pl.multiple_of(i * STRIP, 8), STRIP)


def times(rows, columns):
    return lax.dot_general(rows, columns, (((1,), (1,)), ((), ())), preferred_element_type=jnp.float32)


def end_start(low, quarter):
    return jnp.where(low, 0, quarter)


def own_start(low, quarter):
    return jnp.where(low, quarter, 0)


def pieces_of(units):
    near = units // 2 // LANES * LANES
    middle = (units - near) // 2 // LANES * LANES
    return near, middle, units - near - middle


def cut(ref, start, size):
    return ref[pl.ds(pl.multiple_of(start, 16), size)]


class Columns:
    def __init__(self, low, quarter):
        self.low, self.half = low, 2 * quarter
        self.near_width, middle, self.last = pieces_of(4 * quarter)
        self.spill = self.half - self.near_width
        self.inner = middle - 2 * self.spill

    def near(self, block, start, size):
        return cut(block, jnp.where(self.low, 0, self.spill) + start, size)

    def seam(self, near, far):
        top = far.shape[0] - self.spill if far.shape[0] < self.half else self.half - self.spill
        inward = jnp.where(self.low, cut(near, self.near_width, self.spill), cut(far, top, self.spill))
        outward = jnp.where(self.low, cut(far, 0, self.spill), cut(near, 0, self.spill))
        return jnp.concatenate([inward, outward])

    def middle(self, far, start, size):
        past = self.last if far.shape[0] == self.half else 0
        return cut(far, jnp.where(self.low, self.spill, past) + start, size)

    def outer(self, far, start, size):
        past = self.half - self.last if far.shape[0] == self.half else 0
        return cut(far, jnp.where(self.low, past, 0) + start, size)


def joined(parts):
    return jnp.concatenate(parts) if len(parts) > 1 else parts[0]


def shares(places, total):
    done = 0
    for at, size in places:
        yield pl.ds(pl.multiple_of(at, LANES), size), size, total[:, done : done + size]
        done += size


def summed(rows, starts, quarter, columns):
    total = None
    for v in range(4):
        parts = [cut(r[v], start[v], quarter) for r, start in zip(rows, starts)]
        term = times(joined(parts), joined([c(v) for c in columns]))
        total = term if total is None else total + term
    return total


def edge_kernel(masks, mask, piece, scale, flags_ref, *refs):
    rows = [refs[4 * k : 4 * k + 4] for k in range(masks)]
    nears, fars = refs[4 * masks : -2][:4], refs[4 * masks : -2][-4:]
    out_ref, most = refs[-2:]
    height = out_ref.shape[0] - TAIL
    quarter = height // masks
    low = flags_ref[0] == 1

    @pl.when(flags_ref[1] == 1)
    def _():
        cols = Columns(low, quarter)
        at = end_start(low, quarter)
        starts = [[at, 0, 0, quarter], [at, 0, 0, 0]][mask : mask + masks]
        most[...] = jnp.zeros_like(most)

        def put(places, *columns):
            total = summed(rows, starts, quarter, columns)
            for at, size, part in shares(places, total):
                out_ref[:height, at] = part
                high = jnp.max(jnp.abs(part).reshape(height // 8, 8, size), axis=0)
                for i in range(size // LANES):
                    most[...] = jnp.maximum(most[...], high[:, i * LANES : (i + 1) * LANES])

        if piece == 0:
            for start, size in ((0, 4 * LANES), (4 * LANES, cols.near_width - 4 * LANES)):
                put([(start, size)], lambda v: cols.near(nears[v], start, size))
        elif piece == 1:
            seam = 2 * cols.spill
            put(
                [(jnp.where(low, 0, cols.inner), seam), (jnp.where(low, seam, 0), cols.inner)],
                lambda v: cols.seam(nears[v], fars[v]),
                lambda v: cols.middle(fars[v], 0, cols.inner),
            )
        else:
            put([(0, cols.last)], lambda v: cols.outer(fars[v], 0, cols.last))

        biggest = jnp.max(most[...], axis=(0, 1), keepdims=True)
        power = jnp.ceil(jnp.log2(jnp.maximum(biggest * scale, 1e-30)))
        factor = scale * jnp.exp2(14.0 - power)

        @pl.loop(0, height // STRIP)
        def _(i):
            out_ref[strip(i)] = out_ref[strip(i)] * factor

        out_ref[height:] = jnp.broadcast_to(power, (TAIL, out_ref.shape[1]))


def edge_tiles(flags, rows, nears, fars, mask, piece, quarter, scale):
    masks, tokens = len(rows), rows[0][0].shape[1]
    width = pieces_of(4 * quarter)[piece]
    operands = [*sum(rows, []), *nears, *fars]
    flat = pl.pallas_call(
        functools.partial(edge_kernel, masks, mask, piece, scale),
        out_shape=jax.ShapeDtypeStruct((masks * quarter + TAIL, width), jnp.float32),
        in_specs=[pl.BlockSpec(memory_space=pltpu.SMEM)] + [pl.BlockSpec(memory_space=pltpu.VMEM)] * len(operands),
        out_specs=pl.BlockSpec(memory_space=pltpu.VMEM),
        scratch_shapes=[pltpu.VMEM((8, LANES), jnp.float32)],
        compiler_params=pltpu.CompilerParams(vmem_limit_bytes=EDGE_VMEM),
        cost_estimate=pl.CostEstimate(
            flops=8 * masks * quarter * tokens * width,
            bytes_accessed=8 * (masks * quarter + width) * tokens,
            transcendentals=0,
        ),
        name="edge_tiles",
    )(flags, *operands)
    return flat.astype(jnp.float16)


def unpack(flat, target, rounds, columns, quarter):
    rows = flat.shape[0] - TAIL
    factor = jnp.exp2(flat[rows : rows + 1, :1] - 14.0)
    for k, place in enumerate(rounds):

        @pl.loop(0, quarter // STRIP)
        def _(i):
            target[place, strip(i), columns] = flat[strip(i + k * (quarter // STRIP))] * factor


def middle_kernel(scale, flags_ref, *refs):
    rows, nears, fars, packed = [refs[:4], refs[4:8]], refs[8:12], refs[12:17], refs[17:19]
    out_ref = refs[-1]
    quarter, units = out_ref.shape[1:]
    near_width, middle_width, last_width = pieces_of(units)
    low = flags_ref[0] == 1
    middle = flags_ref[1] == 1
    first = flags_ref[2]

    @pl.when(middle)
    def _():
        cols = Columns(low, quarter)
        at_own = own_start(low, quarter)
        starts = [[at_own, 0, 0, quarter], [at_own, quarter, 0, quarter]]

        def put(places, *columns):
            total = summed(rows, starts, quarter, columns) * scale
            for at, size, part in shares(places, total):
                for k in range(2):
                    out_ref[lax.bitwise_xor(first, k), :, at] = part[k * quarter : (k + 1) * quarter]

        wide, seam = 4 * LANES, 2 * cols.spill
        near_at = jnp.where(low, 0, units - near_width)
        middle_at = jnp.where(low, near_width + seam, last_width)
        last_at = jnp.where(low, units - last_width, 0)
        rest = near_width - wide
        put([(near_at, wide)], lambda v: cols.near(nears[v], 0, wide))
        put(
            [(near_at + wide, rest), (middle_at, cols.inner)],
            lambda v: cols.near(nears[v], wide, rest),
            lambda v: cols.middle(fars[v], 0, cols.inner),
        )
        taken = wide - seam
        put(
            [(near_width, seam), (last_at, taken)],
            lambda v: cols.seam(nears[v], fars[v]),
            lambda v: cols.outer(fars[v + v // 3], 0, taken),
        )
        put([(last_at + taken, last_width - taken)], lambda v: cols.outer(fars[v + v // 3], taken, last_width - taken))

    @pl.when(jnp.logical_not(middle))
    def _():
        near = pl.ds(pl.multiple_of(jnp.where(low, 0, units - near_width), LANES), near_width)
        unpack(packed[0], out_ref, [first], near, quarter)
        unpack(packed[1], out_ref, [1 - first], near, quarter)


def middle_tiles(flags, rows, nears, fars, packed, quarter, scale):
    tokens, units = rows[0][0].shape[1], 4 * quarter
    operands = [*sum(rows, []), *nears, *fars, *packed]
    return pl.pallas_call(
        functools.partial(middle_kernel, scale),
        out_shape=jax.ShapeDtypeStruct((2, quarter, units), jnp.float32),
        in_specs=[pl.BlockSpec(memory_space=pltpu.SMEM)] + [pl.BlockSpec(memory_space=pltpu.VMEM)] * len(operands),
        out_specs=pl.BlockSpec(memory_space=pltpu.VMEM),
        compiler_params=pltpu.CompilerParams(vmem_limit_bytes=MIDDLE_VMEM),
        cost_estimate=pl.CostEstimate(
            flops=16 * quarter * tokens * units, bytes_accessed=8 * (2 * quarter + units) * tokens, transcendentals=0
        ),
        name="middle_tiles",
    )(flags, *operands)


def place_kernel(starts, pieces, flags_ref, out_in, *refs):
    flats, (out_ref, buf, sem) = refs[:-3], refs[-3:]
    quarter, width = buf.shape[1:]
    low = flags_ref[0] == 1
    first = flags_ref[2]
    rounds = [first, 1 - first]

    def side(pair):
        return pl.multiple_of(jnp.where(low, *pair), LANES)

    @pl.when(flags_ref[1] == 0)
    def _():
        for flat, (masks, at) in zip(flats, pieces):
            unpack(flat, buf, [rounds[k] for k in masks], pl.ds(side(at), flat.shape[1]), quarter)
        copy = pltpu.make_async_copy(buf, out_ref.at[:, :, pl.ds(side(starts), width)], sem)
        copy.start()
        copy.wait()


def place_tiles(flags, out, flats, starts, pieces, width):
    return pl.pallas_call(
        functools.partial(place_kernel, starts, pieces),
        out_shape=jax.ShapeDtypeStruct(out.shape, out.dtype),
        in_specs=[
            pl.BlockSpec(memory_space=pltpu.SMEM),
            pl.BlockSpec(memory_space=pl.ANY),
            *[pl.BlockSpec(memory_space=pltpu.VMEM)] * len(flats),
        ],
        out_specs=pl.BlockSpec(memory_space=pl.ANY),
        scratch_shapes=[pltpu.VMEM((2, out.shape[1], width), jnp.float32), pltpu.SemaphoreType.DMA],
        input_output_aliases={1: 0},
        compiler_params=pltpu.CompilerParams(vmem_limit_bytes=EDGE_VMEM),
        cost_estimate=pl.CostEstimate(flops=0, bytes_accessed=6 * 832 * width, transcendentals=0),
        name="place_tiles",
    )(flags, out, *flats)


def line_branch(hop, top, scale):
    rest = top ^ hop

    def run(flags, picks, w_near, w_far):
        quarter = w_near.shape[0] // 2
        low = flags[0] == 1
        near_width, middle_width, last_width = pieces_of(4 * quarter)

        def rows_of(x, start, size):
            return lax.dynamic_slice_in_dim(x, start, size, 0)

        def end_part(x):
            return rows_of(x, jnp.where(low, 0, quarter), quarter)

        def own_part(x):
            return rows_of(x, jnp.where(low, quarter, 0), quarter)

        def sibling(x, u, v):
            return partner(jnp.where(picks[0] == 1, x, jnp.where(picks[1] == 1, v, u)), 1)

        def masked(u, swapped_in):
            return jnp.where(picks[2] == 1, u, swapped_in)

        f_near, e_far, wu, e_near = across(w_far), inward(w_far), partner(w_near, hop), inward(w_near)

        e_far, f_near, wu, w_near = gated((e_far, f_near, wu, w_near))
        g_near, f_far, fu, wv = across(e_far), across(w_near), partner(f_near, hop), partner(wu, rest)

        g_near, e_near, fu, wv, wu = gated((g_near, e_near, fu, wv, wu))
        gu_end, fv_end, ev_end = partner(end_part(g_near), hop), partner(end_part(fu), rest), inward(end_part(wv))
        w_swap = sibling(w_near, wu, wv)

        gu_end, fv_end, ev_end, w_swap, g_near = gated((gu_end, fv_end, ev_end, w_swap, g_near))
        wm = masked(wu, w_swap)
        gv_end, gu_own, em_end = partner(gu_end, rest), partner(own_part(g_near), hop), inward(end_part(wm))

        gv_end, gu_own, em_end, f_far, fu, e_near = gated((gv_end, gu_own, em_end, f_far, fu, e_near))
        nears = [w_near, e_near, f_near, g_near]
        ends_v = [wv, ev_end, fv_end, gv_end]
        flat_v = edge_tiles(flags, [ends_v], nears, [], 1, 0, quarter, scale)
        fu, gu_own, wm, flat_v = gated((fu, gu_own, wm, flat_v))
        sent_v = outward(flat_v)
        inner = 2 * quarter - last_width
        u_ends, u_owns = [jnp.concatenate(x) for x in ([end_part(fu), gu_end], [own_part(fu), gu_own])]
        x_ends, x_owns = [jnp.concatenate([part(f_near), part(g_near)]) for part in (end_part, own_part)]
        swap_ends = sibling(x_ends, u_ends, jnp.concatenate([fv_end, gv_end]))
        g_mid = across(rows_of(e_near, jnp.where(low, last_width, 0), inner))
        v_owns, e_owns = partner(u_owns, rest), inward(jnp.concatenate([own_part(wm), own_part(wv)]))

        swap_ends, flat_v = gated((swap_ends, flat_v))
        m_ends = masked(u_ends, swap_ends)
        g_last = across(rows_of(e_near, jnp.where(low, 0, inner), last_width))
        ends_m = [wm, em_end, m_ends, m_ends]
        flat_m = edge_tiles(flags, [ends_m], nears, [], 0, 0, quarter, scale)

        flat_m, sent_v = gated((flat_m, sent_v))
        sent_m = outward(flat_m)
        g_mid, flat_m = gated((g_mid, flat_m))
        fars = [w_far, e_far, f_far, g_mid]
        flat = edge_tiles(flags, [ends_m, ends_v], nears, fars, 0, 1, quarter, scale)
        sent = outward(flat)

        g_last, flat = gated((g_last, flat))
        fars = [w_far, e_far, f_far, g_last]
        flat = edge_tiles(flags, [ends_m, ends_v], [], fars, 0, 2, quarter, scale)
        v_owns, e_owns, sent_m, sent, flat = gated((v_owns, e_owns, sent_m, sent, flat))
        last = outward(flat)
        swap_owns = sibling(x_owns, u_owns, v_owns)
        swap_owns, sent_m, sent_v, sent = gated((swap_owns, sent_m, sent_v, sent))
        m_owns = masked(u_owns, swap_owns)

        packed = [x.astype(jnp.float32) for x in (sent_m, sent_v)]
        own = [[wm, e_owns, m_owns, m_owns], [wv, e_owns, v_owns, v_owns]]
        fars = [w_far, e_far, f_far, g_mid, g_last]
        out = middle_tiles(flags, own, nears, fars, packed, quarter, scale)
        out = place_tiles(flags, out, [sent.astype(jnp.float32)], (near_width, last_width), [([0, 1], (0, 0))], middle_width)
        out, last = gated((out, last))
        before = near_width + middle_width
        return place_tiles(flags, out, [last.astype(jnp.float32)], (before, 0), [([0, 1], (0, 0))], last_width)

    return run


def shards_line(activations, plan):
    tokens, units = activations.shape
    top = lax.axis_size("tensor") - 1
    scale = 1.0 / math.sqrt(tokens * LINE)
    place = lax.axis_index("dp")
    low = place < 2
    first = plan[0] == top
    flags = jnp.stack([low, (place == 1) | (place == 2), first]).astype(jnp.int32)
    top_half, bottom_half = jnp.split(activations.T, 2)
    halves = [jnp.where(low, top_half, bottom_half), jnp.where(low, bottom_half, top_half)]
    mask = plan[0] + plan[1] - top
    high = (mask >> 1) == 2
    hop = jnp.where(high, 4, 2)
    picks = jnp.stack([mask == 1, mask == (top ^ 1), mask == hop]).astype(jnp.int32)
    return lax.cond(high, line_branch(4, top, scale), line_branch(2, top, scale), flags, picks, *halves)


def solution(mesh):
    fast = mesh.shape["dp"] == LINE and mesh.shape["tensor"] == 8
    return jax.shard_map(
        shards_line if fast else shards_any,
        mesh=mesh,
        in_specs=(P("dp", "tensor"), P()),
        out_specs=P(None, "dp", "tensor"),
        check_vma=False,
    )
```
